32 devices in a mesh: section: 2 (over core), seq: 4 (over z), head: 4 (over y, x).
Axes of the slice: x: 2, y: 2, z: 4, core: 2. Of those that a mesh axis runs over, the one named last changes fastest.
Arguments:
- inputs: bfloat16 [4, 1024, 1536], P(None, 'seq'), may hold values from -6 to 6
- cotangent: bfloat16 [4, 1024, 1536], P(None, 'seq'), may hold values from -6 to 6
- norm_gain: float32 [2, 1536], P('section'), may hold values from 0.5 to 1.5
- w_z: bfloat16 [2, 1536, 3072], P('section', None, 'head'), may hold values from -0.15625 to 0.15625
- w_x: bfloat16 [2, 1536, 3072], P('section', None, 'head'), may hold values from -0.15625 to 0.15625
- w_bc: bfloat16 [2, 1536, 256], P('section'), may hold values from -0.15625 to 0.15625
- w_dt: bfloat16 [2, 1536, 48], P('section', None, 'head'), may hold values from -0.15625 to 0.15625
- conv_x: float32 [2, 4, 3072], P('section', None, 'head'), may hold values from -3 to 3
- conv_x_bias: float32 [2, 3072], P('section', 'head'), may hold values from -3 to 3
- conv_bc: float32 [2, 4, 256], P('section'), may hold values from -3 to 3
- conv_bc_bias: float32 [2, 256], P('section'), may hold values from -3 to 3
- dt_bias: float32 [2, 48], P('section', 'head'), may hold values from -4 to -1
- a_log: float32 [2, 48], P('section', 'head'), may hold values from -12 to 1
- d_skip: float32 [2, 48], P('section', 'head'), may hold values from 0.5 to 1.5
- gate_gain: float32 [2, 3072], P('section', 'head'), may hold values from 0.5 to 1.5
- w_out: bfloat16 [2, 3072, 1536], P('section', 'head'), may hold values from -0.109375 to 0.109375
Outputs:
- layer_outputs: bfloat16 [2, 4, 1024, 1536], P('section', None, 'seq')
- input_grads: bfloat16 [2, 4, 1024, 1536], P('section', None, 'seq')
- grad_norm_gain: float32 [2, 1536], P('section')
- grad_w_z: float32 [2, 1536, 3072], P('section', None, 'head')
- grad_w_x: float32 [2, 1536, 3072], P('section', None, 'head')
- grad_w_bc: float32 [2, 1536, 256], P('section')
- grad_w_dt: float32 [2, 1536, 48], P('section', None, 'head')
- grad_conv_x: float32 [2, 4, 3072], P('section', None, 'head')
- grad_conv_x_bias: float32 [2, 3072], P('section', 'head')
- grad_conv_bc: float32 [2, 4, 256], P('section')
- grad_conv_bc_bias: float32 [2, 256], P('section')
- grad_dt_bias: float32 [2, 48], P('section', 'head')
- grad_a_log: float32 [2, 48], P('section', 'head')
- grad_d_skip: float32 [2, 48], P('section', 'head')
- grad_gate_gain: float32 [2, 3072], P('section', 'head')
- grad_w_out: float32 [2, 3072, 1536], P('section', 'head')
The draws below stay inside these ranges and needn't reach their ends.
All inputs are finite; a program needn't handle non-finite values.
Results may differ from the reference program's by a relative error of at most 0.035.
Values may be sent and summed in bfloat16 or wider, within the bound.
A program may use at most 320 MiB of HBM per device.

```python
import math
import jax
import jax.numpy as jnp
from jax import lax

D = 1536
H = 48
P_SIZE = 64
N = 128
KW = 4
M = 4
DI = 3072
SEQ_LEN = 1024


def draw_a_log(key, part):
    key = jax.random.fold_in(key, 7)
    low_end = jnp.log(0.5 / SEQ_LEN)
    high_end = jnp.log(2.0)
    return jax.random.uniform(key, (2, H), jnp.float32, low_end, high_end)


def block_levels(key, shape, pieces, low, high):
    def one(axis_at, blocks):
        heights = jax.random.uniform(jax.random.fold_in(jax.random.fold_in(key, 6), axis_at), (blocks,), jnp.float32, low / len(pieces), high / len(pieces))
        return jnp.repeat(jnp.exp(heights), shape[axis_at] // blocks).reshape((-1,) + (1,) * (len(shape) - axis_at - 1))

    loudness = one(*pieces[0])
    for cut in pieces[1:]:
        loudness = loudness * one(*cut)
    return loudness


def bell_draw(key, shape, spread, limit, cuts=(), dtype=jnp.bfloat16):
    array = spread * jax.random.normal(key, shape, jnp.float32)
    if cuts:
        array = array * block_levels(key, shape, cuts, -0.22, 0.18)
    return jnp.clip(array, -limit, limit).astype(dtype)


def setup_inputs(seed: int = 0) -> dict:
    streams_of = jax.random.split(jax.random.key(seed), 17)
    return {
        "inputs": bell_draw(streams_of[0], (M, SEQ_LEN, D), 1.0, 6.0, ((1, 4),)),
        "cotangent": bell_draw(streams_of[1], (M, SEQ_LEN, D), 1.0, 6.0, ((1, 4),)),
        "norm_gain": jnp.clip(1.0 + 0.1 * jax.random.normal(streams_of[2], (2, D), jnp.float32), 0.5, 1.5),
        "w_z": bell_draw(streams_of[3], (2, D, DI), D ** -0.5, 0.15625, ((0, 2), (2, 4))),
        "w_x": bell_draw(streams_of[4], (2, D, DI), D ** -0.5, 0.15625, ((0, 2), (2, 4))),
        "w_bc": bell_draw(streams_of[5], (2, D, 2 * N), D ** -0.5, 0.15625, ((0, 2),)),
        "w_dt": bell_draw(streams_of[6], (2, D, H), D ** -0.5, 0.15625, ((0, 2), (2, 4))),
        "conv_x": bell_draw(streams_of[7], (2, KW, DI), KW ** -0.5, 3.0, ((0, 2), (2, 4)), jnp.float32),
        "conv_x_bias": bell_draw(streams_of[8], (2, DI), 0.5, 3.0, ((0, 2), (1, 4)), jnp.float32),
        "conv_bc": bell_draw(streams_of[9], (2, KW, 2 * N), KW ** -0.5, 3.0, ((0, 2),), jnp.float32),
        "conv_bc_bias": bell_draw(streams_of[10], (2, 2 * N), 0.5, 3.0, ((0, 2),), jnp.float32),
        "dt_bias": jnp.clip(-4.0 + 3.0 * jax.random.uniform(streams_of[11], (2, H), jnp.float32) ** block_levels(streams_of[11], (2, H), ((0, 2), (1, 4)), -0.2, 0.2), -4.0, -1.0),
        "a_log": draw_a_log(jax.random.fold_in(streams_of[16], 71), 0),
        "d_skip": jnp.clip(0.5 + 1.0 * jax.random.uniform(streams_of[13], (2, H), jnp.float32) ** block_levels(streams_of[13], (2, H), ((0, 2), (1, 4)), -0.2, 0.2), 0.5, 1.5),
        "gate_gain": jnp.clip(1.0 + 0.1 * jax.random.normal(streams_of[14], (2, DI), jnp.float32), 0.5, 1.5),
        "w_out": bell_draw(streams_of[15], (2, DI, D), DI ** -0.5, 0.109375, ((0, 2), (1, 4))),
    }


@jax.custom_vjp
def low(v):
    return lax.optimization_barrier(v.astype(jnp.bfloat16)).astype(jnp.float32)

@jax.custom_vjp
def low_back(v):
    return v

def low_keep(v):
    return (low(v), None)

def low_pass(kept, grad):
    return (grad,)

def back_keep(v):
    return (v, None)

def back_low(kept, grad):
    return (low(grad),)
low.defvjp(low_keep, low_pass)
low_back.defvjp(back_keep, back_low)
EPSILON = 1e-05
PRECISION = lax.Precision.HIGHEST

def matmul(first_op, second_op):
    return jnp.dot(first_op, second_op, precision=PRECISION, preferred_element_type=jnp.float32)

def silu(values):
    return values * jax.nn.sigmoid(values)

def causal_conv(values, kernel, offset):
    length = values.shape[0]
    padded = jnp.pad(values, ((KW - 1, 0), (0, 0)))
    summed = jnp.broadcast_to(offset[None, :], values.shape)
    for lagged in range(KW):
        summed = summed + kernel[lagged][None, :] * padded[lagged:lagged + length]
    return silu(summed)

def ssd_block(state, block):
    x_heads, step_size, b_rows, c_rows, a_neg = block
    cumulative = jnp.cumsum(step_size * a_neg[None, :], axis=0)
    scores = matmul(c_rows, b_rows.T)
    block_len = cumulative.shape[0]
    causal_mask = (jnp.arange(block_len)[:, None] >= jnp.arange(block_len)[None, :])[:, :, None]
    decays = jnp.exp(jnp.where(causal_mask, cumulative[:, None, :] - cumulative[None, :, :], -1e+30))
    weights = scores[:, :, None] * decays * step_size[None, :, :]
    within = jnp.einsum('tsh,shp->thp', weights, x_heads, precision=PRECISION)
    carried = jnp.exp(cumulative)[:, :, None] * jnp.einsum('tn,hpn->thp', c_rows, state, precision=PRECISION)
    weighted_tail = jnp.exp(cumulative[-1][None, :] - cumulative) * step_size
    new_state = jnp.exp(cumulative[-1])[:, None, None] * state + jnp.einsum('sh,shp,sn->hpn', weighted_tail, x_heads, b_rows, precision=PRECISION)
    return (new_state, within + carried)

def layer(u_val, params):
    gain, w_z, w_x, w_bc, w_dt, kernel_x, offset_x, kernel_bc, offset_bc, dt_bias, a_log, d_skip, gate_gain, w_out = params
    length_here = u_val.shape[0]
    rms_scale = lax.rsqrt(lax.optimization_barrier(jnp.mean(u_val * u_val, axis=-1, keepdims=True)) + EPSILON)
    normed = low(u_val * rms_scale * gain[None, :])
    z_val = low_back(matmul(normed, w_z))
    x_val = low_back(low(matmul(normed, w_x)))
    bc_val = low_back(low(matmul(normed, w_bc)))
    dt_raw = low_back(matmul(normed, w_dt))
    x_conv = causal_conv(x_val, kernel_x, offset_x)
    bc_conv = causal_conv(bc_val, kernel_bc, offset_bc)
    step_size = jax.nn.softplus(dt_raw + dt_bias[None, :])
    a_neg = -jnp.exp(a_log)
    block_len = math.gcd(256, length_here)
    block_count = length_here // block_len
    blocks = (x_conv.reshape(block_count, block_len, H, P_SIZE), step_size.reshape(block_count, block_len, H), bc_conv[:, :N].reshape(block_count, block_len, N), bc_conv[:, N:].reshape(block_count, block_len, N), jnp.broadcast_to(a_neg[None, :], (block_count, H)))
    _, outputs = lax.scan(jax.checkpoint(ssd_block), jnp.zeros((H, P_SIZE, N), jnp.float32), blocks)
    mixed = outputs.reshape(length_here, H, P_SIZE) + d_skip[None, :, None] * x_conv.reshape(length_here, H, P_SIZE)
    gated = mixed.reshape(length_here, H * P_SIZE) * silu(z_val)
    gate_scale = lax.rsqrt(lax.optimization_barrier(jnp.mean(gated * gated, axis=-1, keepdims=True)) + EPSILON)
    normed_gate = low(gated * gate_scale * gate_gain[None, :])
    branch = low_back(matmul(normed_gate, w_out))
    return u_val + branch

def section_layer(stacked, params):
    return jax.vmap(layer, in_axes=(0, None))(stacked, params)

def reference(inputs, cotangent, norm_gain, w_z, w_x, w_bc, w_dt, conv_x, conv_x_bias, conv_bc, conv_bc_bias, dt_bias, a_log, d_skip, gate_gain, w_out):
    weights = (norm_gain, w_z, w_x, w_bc, w_dt, conv_x, conv_x_bias, conv_bc, conv_bc_bias, dt_bias, a_log, d_skip, gate_gain, w_out)
    weights = tuple((weight.astype(jnp.float32) for weight in weights))
    layer_zero = tuple((weight[0] for weight in weights))
    layer_one = tuple((weight[1] for weight in weights))
    middle, pull_zero = jax.vjp(section_layer, inputs.astype(jnp.float32), layer_zero)
    passed = low(middle)
    result, pull_one = jax.vjp(section_layer, passed, layer_one)
    d_passed, grads_one = pull_one(cotangent.astype(jnp.float32))
    d_inputs, grads_zero = pull_zero(d_passed)
    grads = [jnp.stack([first_grad, second_grad]) for first_grad, second_grad in zip(grads_zero, grads_one)]
    layer_outputs = jnp.stack([middle, result]).astype(jnp.bfloat16)
    input_grads = jnp.stack([d_inputs, d_passed]).astype(jnp.bfloat16)
    return (layer_outputs, input_grads, grads[0], grads[1], grads[2], grads[3], grads[4], grads[5], grads[6], grads[7], grads[8], grads[9], grads[10], grads[11], grads[12], grads[13])
```

```python
import functools

import jax
import jax.numpy as jnp
from jax import lax
from jax.experimental import pallas as pl
from jax.experimental.pallas import tpu as pltpu
from jax.sharding import PartitionSpec as P

EPSILON = 1e-05
MESH = pl.DeviceIdType.MESH
HIGH = lax.Precision.HIGHEST
BF = jnp.bfloat16
F32 = jnp.float32
LANES = 128
VMEM_LIMIT = 56 * 2**20


def shape(dims, kind):
    return jax.ShapeDtypeStruct(dims, kind)


def dot(a, b, dims=((1,), (0,)), precision=None):
    return lax.dot_general(a, b, (dims, ((), ())), precision=precision, preferred_element_type=F32)


NT = ((1,), (1,))
TN = ((0,), (0,))


def head_mask(width, heads):
    size = width // heads
    return (
        lax.broadcasted_iota(jnp.int32, (LANES, width), 0)
        == lax.broadcasted_iota(jnp.int32, (LANES, width), 1) // size
    ).astype(F32)


def order_mask(n, lower):
    rows = lax.broadcasted_iota(jnp.int32, (n, n), 0)
    columns = lax.broadcasted_iota(jnp.int32, (n, n), 1)
    return (rows >= columns) if lower else (rows <= columns)


def sigmoid(v):
    return 1.0 / (1.0 + jnp.exp(-v))


def softplus(v):
    return jnp.maximum(v, 0.0) + jnp.log1p(jnp.exp(-jnp.abs(v)))


def column(row_block):
    n = row_block.shape[1]
    return [
        jnp.transpose(jnp.broadcast_to(row_block[i : i + 1, :], (LANES, n))) for i in range(2)
    ]


def rows_of(columns):
    n = columns[0].shape[0]
    rows = [jnp.transpose(jnp.broadcast_to(c, (n, LANES)))[0:1] for c in columns]
    return jnp.concatenate(rows + [jnp.zeros((8 - len(rows), n), F32)], axis=0)


def conv_pre(ext, proj_xbc, halo, taps, bias):
    n = proj_xbc.shape[0]
    ext[0:8, :] = halo
    ext[8 : 8 + n, :] = proj_xbc
    pre = bias + taps[3:4, :] * proj_xbc
    for k in range(3):
        pre = pre + taps[k : k + 1, :] * ext[5 + k : 5 + k + n, :]
    return pre


def ssd_fwd1_kernel(dims, proj, halo, taps, bias, dt_bias, a_neg, cx, dt_o, cum_o, state, decay, ext):
    heads, inner, states = dims
    n = proj.shape[1]
    wide = inner + 2 * states
    xbc = proj[0, :, inner : inner + wide].astype(BF).astype(F32)
    pre = conv_pre(ext, xbc, halo[0].astype(F32), taps[...], bias[...])
    act = pre * sigmoid(pre)
    cx[0] = act
    dt = softplus(proj[0, :, inner + wide :] + dt_bias[...])
    cum = dot(order_mask(n, True).astype(F32), dt * a_neg[...], precision=HIGH)
    dt_o[0] = dt
    cum_o[0] = cum
    last = cum[n - 1 : n, :]
    expand = head_mask(inner, heads)
    weight = dot(jnp.exp(last - cum) * dt, expand, precision=HIGH)
    state[0] = dot(act[:, inner : inner + states].astype(BF), (act[:, :inner] * weight).astype(BF), TN)
    decay[0] = dot(jnp.broadcast_to(jnp.exp(last), (8, LANES)), expand, precision=HIGH)


def ssd_fwd1(proj, halo, taps, bias, dt_bias, a_neg, dims):
    heads, inner, states = dims
    batch, n, _ = proj.shape
    wide = inner + 2 * states
    block = lambda *s: pl.BlockSpec((1,) + s, lambda i: (i, 0, 0))
    whole = lambda a: pl.BlockSpec(a.shape, lambda i: (0, 0))
    return pl.pallas_call(
        functools.partial(ssd_fwd1_kernel, dims),
        grid=(batch,),
        out_shape=(
            shape((batch, n, wide), F32),
            shape((batch, n, LANES), F32),
            shape((batch, n, LANES), F32),
            shape((batch, states, inner), F32),
            shape((batch, 8, inner), F32),
        ),
        in_specs=[
            block(n, proj.shape[2]),
            block(8, wide),
            whole(taps),
            whole(bias),
            whole(dt_bias),
            whole(a_neg),
        ],
        out_specs=(
            block(n, wide),
            block(n, LANES),
            block(n, LANES),
            block(states, inner),
            block(8, inner),
        ),
        scratch_shapes=[pltpu.VMEM((n + 8, wide), F32)],
        compiler_params=pltpu.CompilerParams(vmem_limit_bytes=VMEM_LIMIT),
        name="ssd_fwd1",
    )(proj, halo, taps, bias, dt_bias, a_neg)


def ssd_fwd2_kernel(dims, cx, dt, cum, state, proj, skip, gain, dyn, y_o, gg_o, ssq_o):
    heads, inner, states = dims
    n = cx.shape[1]
    size = inner // heads
    expand = head_mask(inner, heads)
    x = cx[0, :, :inner]
    b = cx[0, :, inner : inner + states].astype(BF)
    c = cx[0, :, inner + states :].astype(BF)
    scores = dot(c, b, NT)
    cums = cum[0]
    cums_t = jnp.transpose(cums)
    dtx = (x * dot(dt[0], expand, precision=HIGH)).astype(BF)
    carried = dot(jnp.exp(cums), expand, precision=HIGH) * dot(c, state[0].astype(BF))
    base = carried + skip[...] * x
    keep = order_mask(n, True)
    first = lax.broadcasted_iota(jnp.int32, (n, LANES), 1) < size
    total = jnp.zeros((n, LANES), F32)
    across = jnp.zeros((n, LANES), F32)
    for p in range(heads // 2):
        lanes = slice(p * LANES, (p + 1) * LANES)
        both = []
        for h in (2 * p, 2 * p + 1):
            lag = jnp.where(keep, cums[:, h : h + 1] - cums_t[h : h + 1, :], -1e30)
            both.append(dot((scores * jnp.exp(lag)).astype(BF), dtx[:, lanes]))
        y = base[:, lanes] + jnp.where(first, both[0], both[1])
        y_o[0, :, lanes] = y
        z = proj[0, :, lanes]
        gated = y * z * sigmoid(z)
        scaled = gated * gain[:, lanes]
        gg_o[0, :, lanes] = scaled.astype(BF)
        total = total + gated * gated
        if dyn is not None:
            across = across + scaled * dyn[0, :, lanes]
    ssq_o[0] = rows_of([jnp.sum(total, axis=1, keepdims=True), jnp.sum(across, axis=1, keepdims=True)])


def ssd_fwd2(cx, dt, cum, state, proj, skip, gain, dyn, dims):
    heads, inner, states = dims
    batch, n, wide = cx.shape
    block = lambda *s: pl.BlockSpec((1,) + s, lambda i: (i, 0, 0))
    whole = lambda a: pl.BlockSpec(a.shape, lambda i: (0, 0))
    return pl.pallas_call(
        functools.partial(ssd_fwd2_kernel, dims)
        if dyn is not None
        else lambda *refs: ssd_fwd2_kernel(dims, *refs[:7], None, *refs[7:]),
        grid=(batch,),
        out_shape=(
            shape((batch, n, inner), F32),
            shape((batch, n, inner), BF),
            shape((batch, 8, n), F32),
        ),
        in_specs=[
            block(n, wide),
            block(n, LANES),
            block(n, LANES),
            block(states, inner),
            block(n, inner),
            whole(skip),
            whole(gain),
        ]
        + ([block(n, inner)] if dyn is not None else []),
        out_specs=(block(n, inner), block(n, inner), block(8, n)),
        compiler_params=pltpu.CompilerParams(vmem_limit_bytes=VMEM_LIMIT),
        name="ssd_fwd2",
    )(cx, dt, cum, state, proj, skip, gain, *([dyn] if dyn is not None else []))


def ssd_bwd1_kernel(dims, full, dyn, y, proj, cx, cum, gs, across, gain, dy_o, dz_o, yn_o, ggg_o, state_o):
    heads, inner, states = dims
    n = dyn.shape[1]
    expand = head_mask(inner, heads)
    gs_c = jnp.concatenate([column(gs[i])[0] for i in range(gs.shape[0])], axis=0)[:, 0:1]
    ac_c = jnp.concatenate([column(across[i])[1] for i in range(gs.shape[0])], axis=0)[:, 0:1]
    z = proj[0]
    sig = sigmoid(z)
    yv = y[0]
    gated = yv * z * sig
    dynv = dyn[0]
    scaled = gated * gs_c
    ggg_o[0] = jnp.broadcast_to(jnp.sum(dynv * scaled, axis=0, keepdims=True), (8, inner))
    yn_o[0] = (scaled * gain[...]).astype(BF)
    dgated = gs_c * gain[...] * dynv - gated * (gs_c * gs_c * gs_c * ac_c / full)
    dy = dgated * z * sig
    dy_o[0] = dy
    dz_o[0] = (dgated * yv * sig * (1.0 + z * (1.0 - sig))).astype(BF)
    moved = dot(jnp.exp(cum[0]), expand, precision=HIGH) * dy
    state_o[0] = dot(cx[0, :, inner + states :].astype(BF), moved.astype(BF), TN)


def ssd_bwd1(dyn, y, proj, cx, cum, stats_gs, stats_across, gain, dims, full):
    heads, inner, states = dims
    batch, n, wide = cx.shape
    per = stats_gs.shape[0] // batch
    block = lambda *s: pl.BlockSpec((1,) + s, lambda i: (i, 0, 0))
    whole = lambda a: pl.BlockSpec(a.shape, lambda i: (0, 0))
    chunk = pl.BlockSpec((per,) + stats_gs.shape[1:], lambda i: (i, 0, 0))
    return pl.pallas_call(
        functools.partial(ssd_bwd1_kernel, dims, full),
        grid=(batch,),
        out_shape=(
            shape((batch, n, inner), F32),
            shape((batch, n, inner), BF),
            shape((batch, n, inner), BF),
            shape((batch, 8, inner), F32),
            shape((batch, states, inner), F32),
        ),
        in_specs=[
            block(n, inner),
            block(n, inner),
            block(n, inner),
            block(n, wide),
            block(n, LANES),
            chunk,
            chunk,
            whole(gain),
        ],
        out_specs=(block(n, inner), block(n, inner), block(n, inner), block(8, inner), block(states, inner)),
        compiler_params=pltpu.CompilerParams(vmem_limit_bytes=VMEM_LIMIT),
        name="ssd_bwd1",
    )(dyn, y, proj, cx, cum, stats_gs, stats_across, gain)


def ssd_bwd2_kernel(
    dims, dy, proj, halo, cx, dt, cum, state, later, taps, bias, dt_bias, a_neg, skip,
    dpre_o, gdt_o, conv_o, small_o, ext, rowq,
):
    heads, inner, states = dims
    n = dy.shape[1]
    size = inner // heads
    wide = inner + 2 * states
    expand = head_mask(inner, heads)
    x = cx[0, :, :inner]
    b = cx[0, :, inner : inner + states].astype(BF)
    c = cx[0, :, inner + states :].astype(BF)
    dyv = dy[0]
    dyb = dyv.astype(BF)
    dtv = dt[0]
    cums = cum[0]
    cums_t = jnp.transpose(cums)
    last = cums[n - 1 : n, :]
    dt_wide = dot(dtv, expand, precision=HIGH)
    dtx = (x * dt_wide).astype(BF)
    scores_t = dot(b, c, NT)
    keep = order_mask(n, False)
    lane = lax.broadcasted_iota(jnp.int32, (n, LANES), 1)
    first = lane < size
    rowq[...] = jnp.zeros_like(rowq)
    colq = jnp.zeros((n, LANES), F32)
    d_scores = jnp.zeros((n, n), F32)
    pieces = []
    for p in range(heads // 2):
        lanes = slice(p * LANES, (p + 1) * LANES)
        both = []
        for j, h in enumerate((2 * p, 2 * p + 1)):
            lag = jnp.where(keep, cums_t[h : h + 1, :] - cums[:, h : h + 1], -1e30)
            decays = jnp.exp(lag)
            weights = scores_t * decays
            mine = jnp.where(first if j == 0 else jnp.logical_not(first), dtx[:, lanes], jnp.zeros((), BF))
            d_weights = dot(mine, dyb[:, lanes], NT)
            q = d_weights * weights
            d_scores = d_scores + d_weights * decays
            rowq[h : h + 1, :] = jnp.sum(q, axis=0, keepdims=True)
            colq = colq + jnp.where(lane == h, jnp.sum(q, axis=1, keepdims=True), 0.0)
            both.append(dot(weights.astype(BF), dyb[:, lanes]))
        pieces.append(jnp.where(first, both[0], both[1]))
    dxw = jnp.concatenate(pieces, axis=1)
    state_b = state[0].astype(BF)
    later_b = later[0].astype(BF)
    ecum = dot(jnp.exp(cums), expand, precision=HIGH)
    moved = ecum * dyv
    carried = dot(c, state_b)
    tail = jnp.exp(last - cums)
    weight = tail * dtv
    weight_wide = dot(weight, expand, precision=HIGH)
    pulled = dot(b, later_b)
    dx = dt_wide * dxw + weight_wide * pulled + skip[...] * dyv
    fold = lambda v: dot(v, expand, NT, precision=HIGH)
    ddt = fold(x * dxw)
    dw = fold(x * pulled)
    wdw = weight * dw
    change = jnp.transpose(rowq[...]) + fold(carried * moved) - colq - wdw
    ends = jnp.sum(wdw, axis=0, keepdims=True) + jnp.exp(last) * fold(
        jnp.broadcast_to(
            jnp.sum(state_b.astype(F32) * later_b.astype(F32), axis=0, keepdims=True), (8, inner)
        )
    )[0:1]
    log_grad = dot(order_mask(n, False).astype(F32), change, precision=HIGH) + ends
    ddt = ddt + tail * dw + a_neg[...] * log_grad
    ddt_raw = ddt * sigmoid(proj[0, :, inner + wide :] + dt_bias[...])
    gdt_o[0] = ddt_raw.astype(BF)
    small_o[0] = jnp.concatenate(
        [
            jnp.sum(ddt_raw, axis=0, keepdims=True),
            jnp.sum(dtv * log_grad, axis=0, keepdims=True) * a_neg[...],
            jnp.sum(fold(x * dyv), axis=0, keepdims=True),
            jnp.zeros((5, LANES), F32),
        ],
        axis=0,
    )
    d_scores_b = d_scores.astype(BF)
    dc = dot(d_scores_b, b, TN) + dot(moved.astype(BF), state_b, NT)
    db = dot(d_scores_b, c) + dot((x * weight_wide).astype(BF), later_b, NT)
    xbc = proj[0, :, inner : inner + wide].astype(BF).astype(F32)
    pre = conv_pre(ext, xbc, halo[0].astype(F32), taps[...], bias[...])
    sig = sigmoid(pre)
    dpre = jnp.concatenate([dx, db, dc], axis=1) * sig * (1.0 + pre * (1.0 - sig))
    dpre_o[0] = dpre
    rows = [jnp.sum(dpre * ext[5 + k : 5 + k + n, :], axis=0, keepdims=True) for k in range(4)]
    rows.append(jnp.sum(dpre, axis=0, keepdims=True))
    conv_o[0] = jnp.concatenate(rows + [jnp.zeros((3, wide), F32)], axis=0)


def ssd_bwd2(dy, proj, halo, cx, dt, cum, state, later, taps, bias, dt_bias, a_neg, skip, dims):
    heads, inner, states = dims
    batch, n, wide = cx.shape
    block = lambda *s: pl.BlockSpec((1,) + s, lambda i: (i, 0, 0))
    whole = lambda a: pl.BlockSpec(a.shape, lambda i: (0, 0))
    return pl.pallas_call(
        functools.partial(ssd_bwd2_kernel, dims),
        grid=(batch,),
        out_shape=(
            shape((batch, n, wide), F32),
            shape((batch, n, LANES), BF),
            shape((batch, 8, wide), F32),
            shape((batch, 8, LANES), F32),
        ),
        in_specs=[
            block(n, inner),
            block(n, proj.shape[2]),
            block(8, wide),
            block(n, wide),
            block(n, LANES),
            block(n, LANES),
            block(states, inner),
            block(states, inner),
            whole(taps),
            whole(bias),
            whole(dt_bias),
            whole(a_neg),
            whole(skip),
        ],
        out_specs=(block(n, wide), block(n, LANES), block(8, wide), block(8, LANES)),
        scratch_shapes=[pltpu.VMEM((n + 8, wide), F32), pltpu.VMEM((LANES, n), F32)],
        compiler_params=pltpu.CompilerParams(vmem_limit_bytes=VMEM_LIMIT),
        name="ssd_bwd2",
    )(dy, proj, halo, cx, dt, cum, state, later, taps, bias, dt_bias, a_neg, skip)


def conv_bwd_kernel(dims, dpre, halo, dz, gdt, taps, out, ext):
    heads, inner, states = dims
    n = dpre.shape[1]
    wide = inner + 2 * states
    ext[0:n, :] = dpre[0]
    ext[n : n + 8, :] = halo[0]
    total = taps[3:4, :] * dpre[0]
    for k in range(3):
        total = total + taps[k : k + 1, :] * ext[3 - k : 3 - k + n, :]
    out[0, :, :inner] = dz[0]
    out[0, :, inner : inner + wide] = total.astype(BF)
    out[0, :, inner + wide :] = gdt[0]


def conv_bwd(dpre, halo, dz, gdt, taps, dims):
    heads, inner, states = dims
    batch, n, wide = dpre.shape
    block = lambda *s: pl.BlockSpec((1,) + s, lambda i: (i, 0, 0))
    return pl.pallas_call(
        functools.partial(conv_bwd_kernel, dims),
        grid=(batch,),
        out_shape=shape((batch, n, inner + wide + LANES), BF),
        in_specs=[
            block(n, wide),
            block(8, wide),
            block(n, inner),
            block(n, LANES),
            pl.BlockSpec(taps.shape, lambda i: (0, 0)),
        ],
        out_specs=block(n, inner + wide + LANES),
        scratch_shapes=[pltpu.VMEM((n + 8, wide), F32)],
        compiler_params=pltpu.CompilerParams(vmem_limit_bytes=VMEM_LIMIT),
        name="conv_bwd",
    )(dpre, halo, dz, gdt, taps)


def push(src, dst, send, recv, device):
    copy = pltpu.make_async_remote_copy(
        src_ref=src, dst_ref=dst, send_sem=send, recv_sem=recv, device_id=device, device_id_type=MESH
    )
    copy.start()
    return copy


def both_layers_kernel(places, *refs):
    count = len(places)
    ins, outs = refs[:count], refs[count:-3]
    send, recv, local = refs[-3:]
    me = lax.axis_index("section")
    other = {"section": 1 - me}
    barrier = pltpu.get_barrier_semaphore()
    pl.semaphore_signal(barrier, inc=1, device_id=other, device_id_type=MESH)
    pl.semaphore_wait(barrier, 1)
    copies = []
    for i, (which, start) in enumerate(places):
        target = outs[which].at[me, :, pl.ds(start, ins[i].shape[1])]
        copies.append(push(ins[i], target, send.at[i], recv.at[i], other))
        own = pltpu.make_async_copy(ins[i], target, local.at[i])
        own.start()
        copies.append(own)
    for copy in copies:
        copy.wait()


def both_layers(groups):
    places, flat, outs = [], [], []
    for i, group in enumerate(groups):
        start = 0
        for a in group:
            places.append((i, start))
            flat.append(a)
            start += a.shape[1]
        outs.append(shape((2, group[0].shape[0], start), group[0].dtype))
    count = len(flat)
    vm = pl.BlockSpec(memory_space=pltpu.VMEM)
    anywhere = pl.BlockSpec(memory_space=pl.ANY)
    return pl.pallas_call(
        functools.partial(both_layers_kernel, places),
        out_shape=tuple(outs),
        in_specs=[vm] * count,
        out_specs=(anywhere,) * len(outs),
        scratch_shapes=[pltpu.SemaphoreType.DMA((count,)) for _ in range(3)],
        compiler_params=pltpu.CompilerParams(
            collective_id=0, has_side_effects=True, vmem_limit_bytes=VMEM_LIMIT
        ),
        name="both_layers",
    )(*flat)


def chain_kernel(forward, size, parts, own, decay, out, outgoing, incoming, send, recv):
    me = lax.axis_index("seq")
    batch = own.shape[0]
    step = 1 if forward else -1
    width = own.shape[2] // parts
    has_from = (me > 0) if forward else (me < size - 1)
    has_to = (me < size - 1) if forward else (me > 0)
    target = {"seq": me + step}
    barrier = pltpu.get_barrier_semaphore()

    @pl.when(has_from)
    def _():
        pl.semaphore_signal(barrier, inc=1, device_id={"seq": me - step}, device_id_type=MESH)

    @pl.when(has_to)
    def _():
        pl.semaphore_wait(barrier, 1)

    def copy(m, p):
        at = pl.ds(p * width, width)
        return pltpu.make_async_remote_copy(
            src_ref=outgoing.at[m, :, at],
            dst_ref=incoming.at[m, :, at],
            send_sem=send.at[m * parts + p],
            recv_sem=recv.at[m * parts + p],
            device_id=target,
            device_id_type=MESH,
        )

    for m in range(batch):
        for p in range(parts):
            at = slice(p * width, (p + 1) * width)

            @pl.when(has_from)
            def _():
                copy(m, p).wait_recv()
                out[m, :, at] = incoming[m, :, at].astype(F32)

            @pl.when(jnp.logical_not(has_from))
            def _():
                out[m, :, at] = jnp.zeros_like(out[m, :, at])

            @pl.when(has_to)
            def _():
                outgoing[m, :, at] = (decay[m, 0:1, at] * out[m, :, at] + own[m, :, at]).astype(BF)
                copy(m, p).start()

    @pl.when(has_to)
    def _():
        for m in range(batch):
            for p in range(parts):
                copy(m, p).wait_send()


def chain(own, decay, forward, size, parts=3):
    batch = own.shape[0]
    vm = pl.BlockSpec(memory_space=pltpu.VMEM)
    return pl.pallas_call(
        functools.partial(chain_kernel, forward, size, parts),
        out_shape=shape(own.shape, F32),
        in_specs=[vm, vm],
        out_specs=vm,
        scratch_shapes=[
            pltpu.VMEM(own.shape, BF),
            pltpu.VMEM(own.shape, BF),
            pltpu.SemaphoreType.DMA((batch * parts,)),
            pltpu.SemaphoreType.DMA((batch * parts,)),
        ],
        compiler_params=pltpu.CompilerParams(
            collective_id=1 if forward else 2, has_side_effects=True, vmem_limit_bytes=VMEM_LIMIT
        ),
        name="chain_fwd" if forward else "chain_bwd",
    )(own, decay)


def greet(size):
    me = lax.axis_index("head")
    barrier = pltpu.get_barrier_semaphore()
    peers = [{"head": lax.rem(me + d, size)} for d in range(1, size)]
    for peer in peers:
        pl.semaphore_signal(barrier, inc=1, device_id=peer, device_id_type=MESH)
    pl.semaphore_wait(barrier, size - 1)
    return me, peers


def head_fwd_kernel(size, full, partial, ssq, u, h_o, stats_o, got, got_ssq, send, recv):
    rows = partial.shape[0] // size
    me, peers = greet(size)
    copies = []
    for d, peer in enumerate(peers):
        to = lax.rem(me + d + 1, size)
        at = pl.ds(pl.multiple_of(to * rows, rows), rows)
        copies.append(push(partial.at[at], got.at[d], send.at[0, d], recv.at[0, d], peer))
        copies.append(push(ssq.at[to], got_ssq.at[d], send.at[1, d], recv.at[1, d], peer))
    mine = pl.ds(pl.multiple_of(me * rows, rows), rows)
    for copy in copies:
        copy.wait()
    squares = ssq[me]
    for d in range(size - 1):
        squares = squares + got_ssq[d]
    gs = lax.rsqrt(column(squares)[0] / full + EPSILON)[:, 0:1]
    total = partial[mine, :].astype(F32)
    for d in range(size - 1):
        total = total + got[d].astype(F32)
    h_o[mine, :] = (u[mine, :].astype(F32) + gs * total).astype(BF)
    stats_o[me] = jnp.concatenate([rows_of([gs])[0:1], squares[1:]], axis=0)
    copies = []
    for d, peer in enumerate(peers):
        copies.append(push(h_o.at[mine], h_o.at[mine], send.at[2, d], recv.at[2, d], peer))
        copies.append(push(stats_o.at[me], stats_o.at[me], send.at[3, d], recv.at[3, d], peer))
    for copy in copies:
        copy.wait()


def head_fwd(partial, ssq, u, size, full):
    n, d_model = partial.shape
    rows = n // size
    vm = pl.BlockSpec(memory_space=pltpu.VMEM)
    return pl.pallas_call(
        functools.partial(head_fwd_kernel, size, full),
        out_shape=(shape((n, d_model), BF), shape((size, 8, rows), F32)),
        in_specs=[vm] * 3,
        out_specs=(vm,) * 2,
        scratch_shapes=[
            pltpu.VMEM((size - 1, rows, d_model), BF),
            pltpu.VMEM((size - 1, 8, rows), F32),
            pltpu.SemaphoreType.DMA((4, size - 1)),
            pltpu.SemaphoreType.DMA((4, size - 1)),
        ],
        compiler_params=pltpu.CompilerParams(
            collective_id=3, has_side_effects=True, vmem_limit_bytes=VMEM_LIMIT
        ),
        name="head_fwd",
    )(partial, ssq, u)


def head_bwd_kernel(size, last, partial, upper, u, gain, du_o, mine_o, grad_o, got, send, recv):
    rows = partial.shape[0] // size
    me, peers = greet(size)
    copies = []
    for d, peer in enumerate(peers):
        to = lax.rem(me + d + 1, size)
        at = pl.ds(pl.multiple_of(to * rows, rows), rows)
        copies.append(push(partial.at[at], got.at[d], send.at[0, d], recv.at[0, d], peer))
    mine = pl.ds(pl.multiple_of(me * rows, rows), rows)
    for copy in copies:
        copy.wait()
    dn = partial[mine, :].astype(F32)
    for d in range(size - 1):
        dn = dn + got[d].astype(F32)
    uv = u[mine, :].astype(F32)
    width = uv.shape[1]
    s = lax.rsqrt(jnp.sum(uv * uv, axis=1, keepdims=True) / width + EPSILON)
    grad_o[...] = jnp.broadcast_to(jnp.sum(dn * uv * s, axis=0, keepdims=True), grad_o.shape)
    scaled = dn * gain[...]
    inner = jnp.sum(scaled * uv, axis=1, keepdims=True)
    above = upper[mine, :].astype(F32) if last else upper[...]
    du = above + s * scaled - uv * (s * s * s * inner / width)
    mine_o[...] = du
    du_o[mine, :] = du.astype(BF)
    copies = []
    for d, peer in enumerate(peers):
        copies.append(push(du_o.at[mine], du_o.at[mine], send.at[1, d], recv.at[1, d], peer))
    for copy in copies:
        copy.wait()


def head_bwd(partial, upper, u, gain, size, last):
    n, d_model = partial.shape
    rows = n // size
    vm = pl.BlockSpec(memory_space=pltpu.VMEM)
    return pl.pallas_call(
        functools.partial(head_bwd_kernel, size, last),
        out_shape=(
            shape((n, d_model), BF),
            shape((rows, d_model), F32),
            shape((8, d_model), F32),
        ),
        in_specs=[vm] * 4,
        out_specs=(vm,) * 3,
        scratch_shapes=[
            pltpu.VMEM((size - 1, rows, d_model), BF),
            pltpu.SemaphoreType.DMA((2, size - 1)),
            pltpu.SemaphoreType.DMA((2, size - 1)),
        ],
        compiler_params=pltpu.CompilerParams(
            collective_id=6 if last else 5, has_side_effects=True, vmem_limit_bytes=VMEM_LIMIT
        ),
        name="head_bwd",
    )(partial, upper, u, gain)


def swap_kernel(mine, got, send, recv):
    me = lax.axis_index("section")
    other = {"section": 1 - me}
    barrier = pltpu.get_barrier_semaphore()
    pl.semaphore_signal(barrier, inc=1, device_id=other, device_id_type=MESH)
    pl.semaphore_wait(barrier, 1)
    push(mine.at[1 - me], got, send, recv, other).wait()


def swap(pair, which):
    anywhere = pl.BlockSpec(memory_space=pl.ANY)
    return pl.pallas_call(
        swap_kernel,
        out_shape=shape(pair.shape[1:], pair.dtype),
        in_specs=[anywhere],
        out_specs=anywhere,
        scratch_shapes=[pltpu.SemaphoreType.DMA, pltpu.SemaphoreType.DMA],
        compiler_params=pltpu.CompilerParams(collective_id=which, has_side_effects=True),
        name="swap",
    )(pair)


OWN = 16
SHARED = 80
PIECE = 48
TAIL = (OWN + SHARED) // PIECE


def grad_pack_kernel(dims, heads_axis, normed, g_in, yn, go, conv, scalars, gate, gain, out, few, few_shared):
    heads, inner, states = dims
    width = normed.shape[1]
    tile = 256

    def in_rows(i, _):
        at = pl.ds(pl.multiple_of(i * tile, tile), tile)
        out[at, :] = dot(normed[:, at], g_in[:, : 2 * inner], TN).astype(BF)
        return 0

    lax.fori_loop(0, width // tile, in_rows, 0)

    def out_rows(i, _):
        at = pl.ds(pl.multiple_of(i * tile, tile), tile)
        to = pl.ds(pl.multiple_of(width + i * tile, tile), tile)
        out[to, :] = dot(yn[:, at], go[...], TN).astype(BF)
        return 0

    lax.fori_loop(0, inner // tile, out_rows, 0)
    plain = width + inner + OWN
    split = 2 * inner + 2 * states
    out[plain : plain + 2 * states, :] = dot(g_in[:, 2 * inner : split], normed[...], TN).astype(BF)
    conv_sum = conv[0]
    scalar_sum = scalars[0]
    gate_sum = gate[0]
    for i in range(1, conv.shape[0]):
        conv_sum, scalar_sum, gate_sum = conv_sum + conv[i], scalar_sum + scalars[i], gate_sum + gate[i]
    few[...] = jnp.zeros_like(few)
    few[0:heads, :] = dot(g_in[:, split:], normed[...], TN)[0:heads]
    few[heads : heads + 4, 0:inner] = conv_sum[0:4, :inner]
    few[heads : heads + 1, inner : 2 * inner] = conv_sum[4:5, :inner]
    few[heads + 1 : heads + 2, inner : 2 * inner] = gate_sum[0:1]
    for i in range(3):
        few[heads + 2 : heads + 3, inner + i * LANES : inner + (i + 1) * LANES] = scalar_sum[i : i + 1]
    out[plain - OWN : plain, :] = few[...].astype(BF)
    few_shared[...] = jnp.zeros_like(few_shared)
    few_shared[0:1, :] = gain[0:1, :]
    few_shared[1:6, 0 : 2 * states] = conv_sum[0:5, inner:]
    out[plain + 2 * states :, :] = few_shared[...].astype(BF)


def grad_pack(normed, g_in, yn, go, conv, scalars, gate, gain, dims, heads_axis):
    heads, inner, states = dims
    width = normed.shape[1]
    rows = width + inner + OWN + heads_axis * SHARED
    vm = pl.BlockSpec(memory_space=pltpu.VMEM)
    return pl.pallas_call(
        functools.partial(grad_pack_kernel, dims, heads_axis),
        out_shape=shape((rows, width), BF),
        in_specs=[vm] * 8,
        out_specs=vm,
        scratch_shapes=[
            pltpu.VMEM((OWN, width), F32),
            pltpu.VMEM((heads_axis * SHARED - 2 * states, width), F32),
        ],
        compiler_params=pltpu.CompilerParams(vmem_limit_bytes=VMEM_LIMIT),
        name="grad_pack",
    )(normed, g_in, yn, go, conv, scalars, gate, gain)


def grad_sum_kernel(size, heads, skew, pack0, pack1, out, shared_o, own, core, got, shared, shared_core, shared_got,
                    ls, cs, cr, rs, rr, bs, br, hs, hr, xs):
    me, layer, head = lax.axis_index("seq"), lax.axis_index("section"), lax.axis_index("head")
    rows = pack0.shape[0] - heads * SHARED + SHARED
    plain = rows - SHARED
    half = rows // 2
    parts = half // PIECE
    up, down, other = {"seq": me + 1}, {"seq": me - 1}, {"section": 1 - layer}
    peers = [{"head": lax.rem(head + d, heads)} for d in range(1, heads)]
    low_end, high_end = me == 0, me == size - 1
    barrier = pltpu.get_barrier_semaphore()
    pl.semaphore_signal(barrier, inc=1, device_id=other, device_id_type=MESH)
    for peer in peers:
        pl.semaphore_signal(barrier, inc=1, device_id=peer, device_id_type=MESH)

    @pl.when(jnp.logical_not(low_end))
    def _():
        pl.semaphore_signal(barrier, inc=1, device_id=down, device_id_type=MESH)

    @pl.when(jnp.logical_not(high_end))
    def _():
        pl.semaphore_signal(barrier, inc=1, device_id=up, device_id_type=MESH)

    @pl.when(jnp.logical_not(jnp.logical_or(low_end, high_end)))
    def _():
        pl.semaphore_wait(barrier, heads + 2)

    @pl.when(jnp.logical_or(low_end, high_end))
    def _():
        pl.semaphore_wait(barrier, heads + 1)

    part = pl.ds(plain - OWN, OWN + heads * SHARED)
    def fetch_shared(ours, others):
        return (
            pltpu.make_async_copy(ours.at[part], shared, xs.at[0]),
            pltpu.make_async_remote_copy(
                src_ref=others.at[part], dst_ref=shared_core, send_sem=xs.at[1], recv_sem=xs.at[2],
                device_id=other, device_id_type=MESH,
            ),
        )

    def by_layer(act):
        pl.when(layer == 0)(lambda: act(pack0, pack1))
        pl.when(layer == 1)(lambda: act(pack1, pack0))

    def start_all(copies):
        for copy in copies:
            copy.start()

    by_layer(lambda a, b: start_all(fetch_shared(a, b)))

    shift = parts * 3 // 5

    def order(side, p):
        return lax.rem(p + (shift if side else 0), parts)

    def place(side, p):
        return pl.ds(pl.multiple_of(side * half + order(side, p) * PIECE, PIECE), PIECE)

    def unless_tail(side, p, act):
        if side:
            pl.when(order(side, p) < parts - TAIL)(act)
        else:
            act()

    def fetch(side, p, ours, others):
        at = place(side, p)
        return (
            pltpu.make_async_copy(ours.at[at], own.at[at], ls.at[side, p]),
            pltpu.make_async_remote_copy(
                src_ref=others.at[at], dst_ref=core.at[at], send_sem=cs.at[side, p],
                recv_sem=cr.at[side, p], device_id=other, device_id_type=MESH,
            ),
        )

    def start_fetch(p, _):
        for side in range(2):

            unless_tail(side, p, lambda: by_layer(lambda a, b: start_all(fetch(side, p, a, b))))
        return 0

    lax.fori_loop(0, parts, start_fetch, 0)
    for copy in fetch_shared(pack0, pack1):
        copy.wait()
    shared[...] = (shared[...].astype(F32) + shared_core[...].astype(F32)).astype(BF)
    block = lambda i: pl.ds(pl.multiple_of(OWN + i * SHARED, 16), SHARED)
    scatter = lambda d: pltpu.make_async_remote_copy(
        src_ref=shared.at[block(lax.rem(head + d + 1, heads))], dst_ref=shared_got.at[d],
        send_sem=hs.at[0, d], recv_sem=hr.at[0, d], device_id=peers[d], device_id_type=MESH,
    )
    gather = lambda d: pltpu.make_async_remote_copy(
        src_ref=shared_o.at[head], dst_ref=shared_o.at[head],
        send_sem=hs.at[1, d], recv_sem=hr.at[1, d], device_id=peers[d], device_id_type=MESH,
    )
    for d in range(heads - 1):
        scatter(d).start()

    def sending(side, p, back, source):
        at = place(side, p)
        towards = down if (side == 0) != back else up
        target, send, recv = (out, bs, br) if back else (got, rs, rr)
        return pltpu.make_async_remote_copy(
            src_ref=source.at[at], dst_ref=target.at[at], send_sem=send.at[side, p],
            recv_sem=recv.at[side, p], device_id=towards, device_id_type=MESH,
        )

    def reduce(side, p):
        start, end = (high_end, low_end) if side == 0 else (low_end, high_end)
        at = place(side, p)

        def collect():
            local, remote = fetch(side, p, pack0, pack1)
            local.wait()
            remote.wait()
            own[at, :] = (own[at, :].astype(F32) + core[at, :].astype(F32)).astype(BF)

        unless_tail(side, p, collect)

        @pl.when(start)
        def _():
            sending(side, p, False, own).start()

        @pl.when(jnp.logical_not(start))
        def _():
            sending(side, p, False, got).wait_recv()
            summed = (own[at, :].astype(F32) + got[at, :].astype(F32)).astype(BF)

            @pl.when(end)
            def _():
                out[at, :] = summed
                sending(side, p, True, out).start()

            @pl.when(jnp.logical_not(end))
            def _():
                got[at, :] = summed
                sending(side, p, False, got).start()

    def back(side, p):
        start, end = (high_end, low_end) if side == 0 else (low_end, high_end)

        @pl.when(jnp.logical_not(end))
        def _():
            sending(side, p, True, out).wait_recv()

            @pl.when(jnp.logical_not(start))
            def _():
                sending(side, p, True, out).start()

    def guarded(act, side, p):
        @pl.when(jnp.logical_and(p >= 0, p < parts))
        def _():
            act(side, p)

    far = size - 1
    ready = parts - shift - TAIL - 1
    finished = parts - shift + skew * (2 * far - me)

    def step(t, _):
        @pl.when(t == ready)
        def _():
            total = shared[block(head), :].astype(F32)
            for d in range(heads - 1):
                scatter(d).wait()
                total = total + shared_got[d].astype(F32)
            own[plain : plain + SHARED, :] = total.astype(BF)
            own[plain - OWN : plain, :] = shared[0:OWN, :]

        guarded(reduce, 0, t - skew * (far - me))
        guarded(reduce, 1, t - skew * me)
        guarded(back, 0, t - skew * (far + me))
        guarded(back, 1, t - skew * (2 * far - me))

        @pl.when(t == finished)
        def _():
            shared_o[head] = out[plain:rows, :]
            for d in range(heads - 1):
                gather(d).start()

        return 0

    lax.fori_loop(0, parts + 2 * skew * far, step, 0)

    def drain(p, _):
        for side in range(2):
            start, end = (high_end, low_end) if side == 0 else (low_end, high_end)

            @pl.when(jnp.logical_not(end))
            def _():
                sending(side, p, False, got).wait_send()

            @pl.when(jnp.logical_not(start))
            def _():
                sending(side, p, True, out).wait_send()

        return 0

    lax.fori_loop(0, parts, drain, 0)
    for d in range(heads - 1):
        gather(d).wait()


def grad_sum(pack0, pack1, size, heads, skew=2):
    rows = pack0.shape[0] - (heads - 1) * SHARED
    width = pack0.shape[1]
    parts = rows // 2 // PIECE
    vm = pl.BlockSpec(memory_space=pltpu.VMEM)
    pair = pltpu.SemaphoreType.DMA((2, parts))
    return pl.pallas_call(
        functools.partial(grad_sum_kernel, size, heads, skew),
        out_shape=(shape((rows, width), BF), shape((heads, SHARED, width), BF)),
        in_specs=[pl.BlockSpec(memory_space=pl.ANY)] * 2,
        out_specs=(vm, vm),
        scratch_shapes=[pltpu.VMEM((rows, width), BF) for _ in range(3)]
        + [pltpu.VMEM((OWN + heads * SHARED, width), BF) for _ in range(2)]
        + [pltpu.VMEM((heads - 1, SHARED, width), BF)]
        + [pair] * 7
        + [pltpu.SemaphoreType.DMA((2, heads - 1)) for _ in range(2)]
        + [pltpu.SemaphoreType.DMA((3,))],
        compiler_params=pltpu.CompilerParams(
            collective_id=8, has_side_effects=True, vmem_limit_bytes=VMEM_LIMIT
        ),
        name="grad_sum",
    )(pack0, pack1)


def over_seq(block, distance):
    size = lax.axis_size("seq")
    route = [(i - distance, i) for i in range(size) if 0 <= i - distance < size]
    return lax.ppermute(block, "seq", route)


def normalise(u, gain):
    uv = u.astype(F32)
    s = lax.rsqrt(jnp.mean(uv * uv, axis=-1, keepdims=True) + EPSILON)
    return (uv * s * gain).astype(BF)


def on_device(
    inputs, cotangent, norm_gain, w_z, w_x, w_bc, w_dt, conv_x, conv_x_bias, conv_bc, conv_bc_bias,
    dt_bias, a_log, d_skip, gate_gain, w_out,
):
    me = lax.axis_index("section")
    seq_size, head_size = lax.axis_size("seq"), lax.axis_size("head")
    micro, n, d_model = inputs.shape
    batch = micro // 2
    tokens = batch * n
    inner, heads, states = w_z.shape[2], w_dt.shape[2], w_bc.shape[2] // 2
    wide = inner + 2 * states
    full = inner * head_size
    dims = (heads, inner, states)
    pad_heads = lambda a: jnp.pad(a, ((0, 0),) * (a.ndim - 1) + ((0, LANES - heads),))

    taps_x = jnp.concatenate([conv_x[0], conv_x_bias, jnp.zeros((3, inner), F32)], axis=0)
    taps_bc = jnp.concatenate([conv_bc[0], conv_bc_bias, jnp.zeros((3, 2 * states), F32)], axis=0)
    taps = jnp.concatenate([taps_x, taps_bc], axis=1)
    scalars = pad_heads(jnp.concatenate([dt_bias, -jnp.exp(a_log)], axis=0)).reshape(1, -1)
    vectors = jnp.concatenate(
        [
            jnp.repeat(d_skip[0], inner // heads)[None],
            gate_gain,
            jnp.pad(scalars, ((0, 0), (0, inner - 2 * LANES))),
            jnp.zeros((5, inner), F32),
        ],
        axis=0,
    )
    gains = jnp.broadcast_to(norm_gain, (8, d_model))
    w_in2, w_out2, vectors2 = both_layers(
        [[w_z[0], w_x[0], w_bc[0], pad_heads(w_dt[0])], [w_out[0]], [taps, vectors, gains]]
    )
    gains2 = vectors2[:, :, wide + inner :]
    taps2, vectors2 = vectors2[:, :, :wide], vectors2[:, :, wide : wide + inner]

    u = lax.dynamic_slice_in_dim(inputs, me * batch, batch, 0).reshape(tokens, d_model)
    cot = lax.dynamic_slice_in_dim(cotangent, me * batch, batch, 0).reshape(tokens, d_model)

    kept = []
    layers = 2
    for l in range(layers):
        gain = gains2[l, 0:1]
        kernel, bias = taps2[l, 0:4], taps2[l, 4:5]
        skip, gate = vectors2[l, 0:1], vectors2[l, 1:2]
        dt_b, a_neg = vectors2[l, 2:3, :LANES], vectors2[l, 2:3, LANES : 2 * LANES]
        normed = normalise(u, gain)
        proj = dot(normed, w_in2[l]).reshape(batch, n, -1)
        rim = over_seq(proj[:, n - 3 :, inner : inner + wide].astype(BF), 1)
        halo = jnp.pad(rim, ((0, 0), (5, 0), (0, 0)))
        cx, dt, cum, own, decay = ssd_fwd1(proj, halo, kernel, bias, dt_b, a_neg, dims)
        state = chain(own, decay, True, seq_size)
        dyn = dot(cot, w_out2[l], NT).reshape(batch, n, inner) if l == layers - 1 else None
        y, gg, ssq = ssd_fwd2(cx, dt, cum, state, proj, skip, gate, dyn, dims)
        partial = dot(gg.reshape(tokens, inner), w_out2[l]).astype(BF)
        per = head_size // batch
        ssq = ssq.reshape(batch, 8, per, n // per).transpose(0, 2, 1, 3).reshape(head_size, 8, n // per)
        h, stats = head_fwd(partial, ssq, u, head_size, full)
        kept.append((u, gain, kernel, bias, skip, gate, dt_b, a_neg, normed, proj, halo, cx, dt, cum, decay, state, y, stats, dyn, h))
        u = h
    go, upper = cot, cot
    results = []
    for l in reversed(range(layers)):
        (u, gain, kernel, bias, skip, gate, dt_b, a_neg, normed, proj, halo, cx, dt, cum, decay, state, y, stats, dyn, h) = kept[l]
        last = l == layers - 1
        across = stats
        if not last:
            dyn = dot(go, w_out2[l], NT).reshape(batch, n, inner)
            z = proj[..., :inner]
            across = lax.psum(jnp.sum(dyn * gate * y * z * sigmoid(z), axis=-1), "head")
            across = jnp.broadcast_to(across.reshape(head_size, 1, -1), stats.shape)
        dy, dz, yn, ggg, d_state = ssd_bwd1(dyn, y, proj, cx, cum, stats, across, gate, dims, full)
        later = chain(d_state, decay, False, seq_size)
        dpre, gdt, conv_grads, small = ssd_bwd2(
            dy, proj, halo, cx, dt, cum, state, later, kernel, bias, dt_b, a_neg, skip, dims
        )
        rim = jnp.pad(over_seq(dpre[:, :3], -1), ((0, 0), (0, 5), (0, 0)))
        g_in = conv_bwd(dpre, rim, dz, gdt, kernel, dims).reshape(tokens, -1)
        partial = dot(g_in, w_in2[l], NT).astype(BF)
        du, upper_new, grad_gain = head_bwd(partial, upper, u, gain, head_size, last)
        pack = grad_pack(normed, g_in, yn.reshape(tokens, inner), go, conv_grads, small, ggg, grad_gain, dims, head_size)
        results.append((du, pack))
        go, upper = du, upper_new
    results = results[::-1]

    grads, shared = grad_sum(results[0][1], results[1][1], seq_size, head_size)
    plain = d_model + inner
    small = grads[plain : plain + OWN].astype(F32)
    shared = shared.reshape(-1, d_model)
    grad_bc = shared[: 2 * states].T.astype(F32)
    grad_gain = shared[2 * states].astype(F32)
    conv_b = shared[2 * states + 1 : 2 * states + 6, : 2 * states].astype(F32)

    def gather(first, second):
        pair = jnp.stack([first, second]).reshape(2, batch, n, d_model)
        got = swap(pair, 9)
        own = lax.dynamic_index_in_dim(pair, me, 0, False)
        out = jnp.zeros((micro, n, d_model), BF)
        out = lax.dynamic_update_slice_in_dim(out, own, me * batch, 0)
        return lax.dynamic_update_slice_in_dim(out, got, (1 - me) * batch, 0)[None]

    layer_outputs = gather(kept[0][19], kept[1][19])
    input_grads = gather(results[0][0], results[1][0])
    return (
        layer_outputs,
        input_grads,
        grad_gain[None],
        grads[None, :d_model, :inner].astype(F32),
        grads[None, :d_model, inner:].astype(F32),
        grad_bc[None],
        small[None, :heads].transpose(0, 2, 1),
        small[None, heads : heads + 4, :inner],
        small[None, heads, inner:],
        conv_b[None, :4],
        conv_b[None, 4],
        small[None, heads + 2, inner : inner + heads],
        small[None, heads + 2, inner + LANES : inner + LANES + heads],
        small[None, heads + 2, inner + 2 * LANES : inner + 2 * LANES + heads],
        small[None, heads + 1, inner:],
        grads[None, d_model:plain].astype(F32),
    )


def solution(mesh):
    in_specs = (
        P(None, "seq", None),
        P(None, "seq", None),
        P("section", None),
        P("section", None, "head"),
        P("section", None, "head"),
        P("section", None, None),
        P("section", None, "head"),
        P("section", None, "head"),
        P("section", "head"),
        P("section", None, None),
        P("section", None),
        P("section", "head"),
        P("section", "head"),
        P("section", "head"),
        P("section", "head"),
        P("section", "head", None),
    )
    out_specs = (
        P("section", None, "seq", None),
        P("section", None, "seq", None),
        P("section", None),
        P("section", None, "head"),
        P("section", None, "head"),
        P("section", None, None),
        P("section", None, "head"),
        P("section", None, "head"),
        P("section", "head"),
        P("section", None, None),
        P("section", None),
        P("section", "head"),
        P("section", "head"),
        P("section", "head"),
        P("section", "head"),
        P("section", "head", None),
    )
    return jax.shard_map(
        on_device, mesh=mesh, in_specs=in_specs, out_specs=out_specs, check_vma=False
    )
```

```python
import functools

import jax
import jax.numpy as jnp
from jax import lax
from jax.experimental import pallas as pl
from jax.experimental.pallas import tpu as pltpu
from jax.sharding import PartitionSpec as P

EPSILON = 1e-05
MESH = pl.DeviceIdType.MESH
HIGH = lax.Precision.HIGHEST
BF = jnp.bfloat16
F32 = jnp.float32
LANES = 128
VMEM_LIMIT = 56 * 2**20


def shape(dims, kind):
    return jax.ShapeDtypeStruct(dims, kind)


def dot(a, b, dims=((1,), (0,)), precision=None):
    return lax.dot_general(a, b, (dims, ((), ())), precision=precision, preferred_element_type=F32)


NT = ((1,), (1,))
TN = ((0,), (0,))


def halves(v):
    high = v.astype(BF)
    return high, (v - high.astype(F32)).astype(BF)


def dot_mask(v, mask, dims=((1,), (0,))):
    high, rest = halves(v)
    return dot(high, mask, dims) + dot(rest, mask, dims)


def dot3(a, b, dims=((1,), (0,))):
    a_high, a_rest = halves(a)
    b_high, b_rest = halves(b)
    return dot(a_high, b_high, dims) + dot(a_rest, b_high, dims) + dot(a_high, b_rest, dims)


def mask_dot(mask, v):
    high, rest = halves(v)
    return dot(mask, high) + dot(mask, rest)


def head_mask(width, heads):
    size = width // heads
    return (
        lax.broadcasted_iota(jnp.int32, (LANES, width), 0)
        == lax.broadcasted_iota(jnp.int32, (LANES, width), 1) // size
    ).astype(F32).astype(BF)


def order_mask(n, lower):
    rows = lax.broadcasted_iota(jnp.int32, (n, n), 0)
    columns = lax.broadcasted_iota(jnp.int32, (n, n), 1)
    return (rows >= columns) if lower else (rows <= columns)


def sigmoid(v):
    return 1.0 / (1.0 + jnp.exp(-v))


def softplus(v):
    return jnp.maximum(v, 0.0) + jnp.log1p(jnp.exp(-jnp.abs(v)))


def column(row_block):
    n = row_block.shape[1]
    return [
        jnp.transpose(jnp.broadcast_to(row_block[i : i + 1, :], (LANES, n))) for i in range(2)
    ]


def rows_of(columns):
    n = columns[0].shape[0]
    rows = [jnp.transpose(jnp.broadcast_to(c, (n, LANES)))[0:1] for c in columns]
    return jnp.concatenate(rows + [jnp.zeros((8 - len(rows), n), F32)], axis=0)


def conv_pre(ext, proj_xbc, halo, taps, bias):
    n = proj_xbc.shape[0]
    ext[0:8, :] = halo
    ext[8 : 8 + n, :] = proj_xbc
    pre = bias + taps[3:4, :] * proj_xbc
    for k in range(3):
        pre = pre + taps[k : k + 1, :] * ext[5 + k : 5 + k + n, :]
    return pre


def push(src, dst, send, recv, device):
    copy = pltpu.make_async_remote_copy(
        src_ref=src, dst_ref=dst, send_sem=send, recv_sem=recv, device_id=device, device_id_type=MESH
    )
    copy.start()
    return copy


def both_layers_kernel(places, *refs):
    count = len(places)
    ins, outs = refs[:count], refs[count:-3]
    send, recv, local = refs[-3:]
    me = lax.axis_index("section")
    other = {"section": 1 - me}
    barrier = pltpu.get_barrier_semaphore()
    pl.semaphore_signal(barrier, inc=1, device_id=other, device_id_type=MESH)
    pl.semaphore_wait(barrier, 1)
    copies = []
    for i, (which, start) in enumerate(places):
        target = outs[which].at[me, :, pl.ds(start, ins[i].shape[1])]
        copies.append(push(ins[i], target, send.at[i], recv.at[i], other))
        own = pltpu.make_async_copy(ins[i], target, local.at[i])
        own.start()
        copies.append(own)
    for copy in copies:
        copy.wait()


def both_layers(groups):
    places, flat, outs = [], [], []
    for i, group in enumerate(groups):
        start = 0
        for a in group:
            places.append((i, start))
            flat.append(a)
            start += a.shape[1]
        outs.append(shape((2, group[0].shape[0], start), group[0].dtype))
    count = len(flat)
    vm = pl.BlockSpec(memory_space=pltpu.VMEM)
    anywhere = pl.BlockSpec(memory_space=pl.ANY)
    return pl.pallas_call(
        functools.partial(both_layers_kernel, places),
        out_shape=tuple(outs),
        in_specs=[vm] * count,
        out_specs=(anywhere,) * len(outs),
        scratch_shapes=[pltpu.SemaphoreType.DMA((count,)) for _ in range(3)],
        compiler_params=pltpu.CompilerParams(
            collective_id=0, has_side_effects=True, vmem_limit_bytes=VMEM_LIMIT
        ),
        name="both_layers",
    )(*flat)


class Line:
    def __init__(self, forward, size, parts, outgoing, incoming, send, recv):
        self.me = lax.axis_index("seq")
        self.size, self.parts = size, parts
        self.outgoing, self.incoming, self.send, self.recv = outgoing, incoming, send, recv
        first, last = self.me == 0, self.me == size - 1
        self.starts, self.ends = (first, last) if forward else (last, first)
        self.place = self.me if forward else size - 1 - self.me
        step = 1 if forward else -1
        self.target, self.source = {"seq": self.me + step}, {"seq": self.me - step}

    def greet(self, barrier):
        @pl.when(jnp.logical_not(self.starts))
        def _():
            pl.semaphore_signal(barrier, inc=1, device_id=self.source, device_id_type=MESH)

    def met(self, barrier, others=0):
        @pl.when(jnp.logical_not(self.ends))
        def _():
            pl.semaphore_wait(barrier, others + 1)

        if others:

            @pl.when(self.ends)
            def _():
                pl.semaphore_wait(barrier, others)

    def copy(self, m, p):
        width = self.outgoing.shape[2] // self.parts
        at = pl.ds(p * width, width)
        return pltpu.make_async_remote_copy(
            src_ref=self.outgoing.at[m, :, at],
            dst_ref=self.incoming.at[m, :, at],
            send_sem=self.send.at[m * self.parts + p],
            recv_sem=self.recv.at[m * self.parts + p],
            device_id=self.target,
            device_id_type=MESH,
        )

    def begin(self, m, own):
        @pl.when(self.starts)
        def _():
            self.incoming[m] = jnp.zeros_like(self.incoming[m])
            self.outgoing[m] = own.astype(self.outgoing.dtype)
            for p in range(self.parts):
                self.copy(m, p).start()

    def relay(self, own, decay, at_step, steps, lag, apart):
        width = self.outgoing.shape[2] // self.parts
        for i in range(self.outgoing.shape[0] * self.parts):
            m, p = i // self.parts, i % self.parts
            at = slice(p * width, (p + 1) * width)
            due = jnp.minimum(self.place * lag + apart * i, steps - 1)

            @pl.when(jnp.logical_and(self.place > 0, due == at_step))
            def _():
                self.copy(m, p).wait_recv()

                @pl.when(jnp.logical_not(self.ends))
                def _():
                    passed = decay[m, 0:1, at] * self.incoming[m, :, at].astype(F32) + own[m, :, at]
                    self.outgoing[m, :, at] = passed.astype(self.outgoing.dtype)
                    self.copy(m, p).start()

    def finish(self):
        @pl.when(jnp.logical_not(self.ends))
        def _():
            for m in range(self.outgoing.shape[0]):
                for p in range(self.parts):
                    self.copy(m, p).wait_send()

    def halo(self, src, dst, m, send, recv):
        return pltpu.make_async_remote_copy(
            src_ref=src, dst_ref=dst, send_sem=send.at[m], recv_sem=recv.at[m],
            device_id=self.target, device_id_type=MESH,
        )


PARTS = 3


def ssd_fwd_kernel(dims, size, heads_axis, full, has_dyn, *refs):
    proj, taps, bias, dt_bias, a_neg, skip, gain = refs[:7]
    dyn = refs[7] if has_dyn else None
    (cx, dt_o, cum_o, state, halo, y_o, yn_o, stats_o,
     ext, own, decay, rim, outgoing, incoming, gates, square, square_got,
     send, recv, halo_send, halo_recv, stat_send, stat_recv) = refs[7 + has_dyn :]
    heads, inner, states = dims
    batch, n = proj.shape[0], proj.shape[1]
    wide = inner + 2 * states
    head_lanes = inner // heads
    columns = slice(inner, inner + wide)
    line = Line(True, size, PARTS, outgoing, incoming, send, recv)
    head = lax.axis_index("head")
    peers = [{"head": lax.rem(head + d, heads_axis)} for d in range(1, heads_axis)]
    barrier = pltpu.get_barrier_semaphore()
    line.greet(barrier)
    for peer in peers:
        pl.semaphore_signal(barrier, inc=1, device_id=peer, device_id_type=MESH)
    for m in range(batch):
        rim[m] = proj[m, n - 16 :, columns].astype(BF)
    line.met(barrier, len(peers))

    @pl.when(jnp.logical_not(line.ends))
    def _():
        for m in range(batch):
            line.halo(rim.at[m], halo.at[m], m, halo_send, halo_recv).start()

    @pl.when(line.starts)
    def _():
        halo[...] = jnp.zeros_like(halo)

    expand = head_mask(inner, heads)
    for m in range(batch):

        @pl.when(jnp.logical_not(line.starts))
        def _():
            line.halo(rim.at[m], halo.at[m], m, halo_send, halo_recv).wait_recv()

        xbc = proj[m, :, columns].astype(BF).astype(F32)
        pre = conv_pre(ext, xbc, halo[m, 8:].astype(F32), taps[...], bias[...])
        act = pre * sigmoid(pre)
        cx[m] = act
        dt = softplus(proj[m, :, inner + wide :] + dt_bias[...])
        cum = mask_dot(order_mask(n, True).astype(F32).astype(BF), dt * a_neg[...])
        dt_o[m] = dt
        cum_o[m] = cum
        last = cum[n - 1 : n, :]
        weight = dot_mask(jnp.exp(last - cum) * dt, expand)
        mine = dot3(act[:, inner : inner + states], act[:, :inner] * weight, TN)
        own[m] = mine
        decay[m] = dot_mask(jnp.broadcast_to(jnp.exp(last), (8, LANES)), expand)
        line.begin(m, mine)
    keep = order_mask(n, True)
    first = lax.broadcasted_iota(jnp.int32, (n, LANES), 1) < head_lanes
    pairs = heads // 2
    for m in range(batch):
        scores = dot3(cx[m, :, inner + states :], cx[m, :, inner : inner + states], NT)
        cums = cum_o[m]
        cums_t = jnp.transpose(cums)
        dt_wide = dot_mask(dt_o[m], expand)
        for p in range(pairs):

            line.relay(own, decay, m * pairs + p, batch * pairs, 4, 2)
            lanes = slice(p * LANES, (p + 1) * LANES)
            x = cx[m, :, lanes]
            dtx, dtx_rest = halves(x * dt_wide[:, lanes])
            both = []
            for h in (2 * p, 2 * p + 1):
                lag = jnp.where(keep, cums[:, h : h + 1] - cums_t[h : h + 1, :], -1e30)
                high, rest = halves(scores * jnp.exp(lag))
                both.append(dot(high, dtx) + dot(rest, dtx) + dot(high, dtx_rest))
            y_o[m, :, lanes] = skip[:, lanes] * x + jnp.where(first, both[0], both[1])
    for m in range(batch):
        entered = incoming[m]
        state[m] = entered
        y = y_o[m] + dot_mask(jnp.exp(cum_o[m]), expand) * dot3(cx[m, :, inner + states :], entered)
        y_o[m] = y
        z = proj[m, :, :inner]
        gated = y * z * sigmoid(z)
        gates[m] = gated
        stats = [jnp.sum(gated * gated, axis=1, keepdims=True)]
        if has_dyn:
            stats.append(jnp.sum(gated * gain[...] * dyn[m], axis=1, keepdims=True))
        square[m] = rows_of(stats)
    copies = [
        push(square, square_got.at[d], stat_send.at[d], stat_recv.at[d], peer) for d, peer in enumerate(peers)
    ]
    for copy in copies:
        copy.wait()
    for m in range(batch):
        total = square[m]
        for d in range(heads_axis - 1):
            total = total + square_got[d, m]
        gs = lax.rsqrt(total[0:1] / full + EPSILON)
        stats_o[m] = jnp.concatenate([gs, total[1:]], axis=0)
        yn_o[m] = (gates[m] * column(stats_o[m])[0][:, 0:1] * gain[...]).astype(BF)
    line.finish()

    @pl.when(jnp.logical_not(line.ends))
    def _():
        for m in range(batch):
            line.halo(rim.at[m], halo.at[m], m, halo_send, halo_recv).wait_send()


def ssd_fwd(proj, taps, bias, dt_bias, a_neg, skip, gain, dyn, dims, size, heads_axis, full):
    heads, inner, states = dims
    batch, n, _ = proj.shape
    wide = inner + 2 * states
    vm = pl.BlockSpec(memory_space=pltpu.VMEM)
    has_dyn = dyn is not None
    moved = (batch, states, inner)
    outs = (
        shape((batch, n, wide), F32),
        shape((batch, n, LANES), F32),
        shape((batch, n, LANES), F32),
        shape(moved, F32),
        shape((batch, 16, wide), BF),
        shape((batch, n, inner), F32),
        shape((batch, n, inner), BF),
        shape((batch, 8, n), F32),
    )
    return pl.pallas_call(
        functools.partial(ssd_fwd_kernel, dims, size, heads_axis, full, has_dyn),
        out_shape=outs,
        in_specs=[vm] * (7 + has_dyn),
        out_specs=(vm,) * len(outs),
        scratch_shapes=[
            pltpu.VMEM((n + 8, wide), F32),
            pltpu.VMEM(moved, F32),
            pltpu.VMEM((batch, 8, inner), F32),
            pltpu.VMEM((batch, 16, wide), BF),
            pltpu.VMEM(moved, F32),
            pltpu.VMEM(moved, F32),
            pltpu.VMEM((batch, n, inner), F32),
            pltpu.VMEM((batch, 8, n), F32),
            pltpu.VMEM((heads_axis - 1, batch, 8, n), F32),
            pltpu.SemaphoreType.DMA((batch * PARTS,)),
            pltpu.SemaphoreType.DMA((batch * PARTS,)),
            pltpu.SemaphoreType.DMA((batch,)),
            pltpu.SemaphoreType.DMA((batch,)),
            pltpu.SemaphoreType.DMA((heads_axis - 1,)),
            pltpu.SemaphoreType.DMA((heads_axis - 1,)),
        ],
        compiler_params=pltpu.CompilerParams(
            collective_id=1 + has_dyn, has_side_effects=True, vmem_limit_bytes=VMEM_LIMIT
        ),
        name="ssd_fwd",
    )(proj, taps, bias, dt_bias, a_neg, skip, gain, *([dyn] if has_dyn else []))


def ssd_bwd_kernel(
    dims, size, heads_axis, full, has_across,
    dyn, y, proj, halo, cx, dt, cum, state, stats, taps, bias, dt_bias, a_neg, skip, gain, *refs
):
    if has_across:
        h_rows, h_whole, h_o, *refs = refs[:2] + refs[6:7] + refs[2:6] + refs[7:]
        *refs, c_local, c_send, c_recv = refs
    (
    g_in, gate_o, conv_o, small_o,
    dy, dxw, dpre, own, decay, ext, rowq, colq, d_scores, outgoing, incoming, rim, square, square_got,
    send, recv, rim_send, rim_recv, stat_send, stat_recv,
    ) = refs
    heads, inner, states = dims
    batch, n = dyn.shape[0], dyn.shape[1]
    wide = inner + 2 * states
    columns = slice(inner, inner + wide)
    size_p = inner // heads
    pairs = heads // 2
    line = Line(False, size, PARTS, outgoing, incoming, send, recv)
    head = lax.axis_index("head")
    peers = [{"head": lax.rem(head + d, heads_axis)} for d in range(1, heads_axis)]
    barrier = pltpu.get_barrier_semaphore()
    line.greet(barrier)
    if has_across:
        outputs = Collect(1, heads_axis, h_rows, h_whole, h_o, c_local, c_send, c_recv)
        peers = outputs.greeted()
    for peer in peers:
        pl.semaphore_signal(barrier, inc=1, device_id=peer, device_id_type=MESH)
    if not has_across:
        for m in range(batch):
            z = proj[m, :, :inner]
            square[m] = rows_of([jnp.sum(dyn[m] * gain[...] * y[m] * z * sigmoid(z), axis=1, keepdims=True)])
    line.met(barrier, len(peers))
    if has_across:
        outputs.start()
    else:
        copies = [
            push(square, square_got.at[d], stat_send.at[d], stat_recv.at[d], peers[d])
            for d in range(heads_axis - 1)
        ]
    expand = head_mask(inner, heads)
    if not has_across:
        for copy in copies:
            copy.wait()
    for m in range(batch):
        gs, across = [v[:, 0:1] for v in column(stats[m])]
        if has_across:
            pass
        else:
            total = square[m]
            for d in range(heads_axis - 1):
                total = total + square_got[d, m]
            across = column(total)[0][:, 0:1]
        z = proj[m, :, :inner]
        sig = sigmoid(z)
        yv = y[m]
        gated = yv * z * sig
        dynv = dyn[m]
        scaled = gated * gs
        gate_o[m] = jnp.broadcast_to(jnp.sum(dynv * scaled, axis=0, keepdims=True), (8, inner))
        dgated = gs * gain[...] * dynv - gated * (gs * gs * gs * across / full)
        dyv = dgated * z * sig
        dy[m] = dyv
        g_in[m, :, :inner] = (dgated * yv * sig * (1.0 + z * (1.0 - sig))).astype(BF)
        cums = cum[m]
        moved = dot_mask(jnp.exp(cums), expand) * dyv
        mine = dot3(cx[m, :, inner + states :], moved, TN)
        own[m] = mine
        decay[m] = dot_mask(jnp.broadcast_to(jnp.exp(cums[n - 1 : n, :]), (8, LANES)), expand)
        line.begin(m, mine)
    keep = order_mask(n, False)
    lane = lax.broadcasted_iota(jnp.int32, (n, LANES), 1)
    first = lane < size_p
    rowq[...] = jnp.zeros_like(rowq)
    for m in range(batch):
        scores_t = dot3(cx[m, :, inner : inner + states], cx[m, :, inner + states :], NT)
        cums = cum[m]
        cums_t = jnp.transpose(cums)
        dt_wide = dot_mask(dt[m], expand)
        colq[m] = jnp.zeros_like(colq[m])
        d_scores[m] = jnp.zeros_like(d_scores[m])
        for p in range(pairs):

            line.relay(own, decay, m * pairs + p, batch * pairs, 2, 1)
            lanes = slice(p * LANES, (p + 1) * LANES)
            dtx = cx[m, :, lanes] * dt_wide[:, lanes]
            dyb, dy_rest = halves(dy[m, :, lanes])
            both = []
            for j, h in enumerate((2 * p, 2 * p + 1)):
                lag = jnp.where(keep, cums_t[h : h + 1, :] - cums[:, h : h + 1], -1e30)
                decays = jnp.exp(lag)
                weights = scores_t * decays
                mine, mine_rest = halves(jnp.where(first if j == 0 else jnp.logical_not(first), dtx, 0.0))
                d_weights = dot(mine, dyb, NT) + dot(mine, dy_rest, NT) + dot(mine_rest, dyb, NT)
                q = d_weights * weights
                d_scores[m] += d_weights * decays
                rowq[m, h : h + 1, :] = jnp.sum(q, axis=0, keepdims=True)
                colq[m] += jnp.where(lane == h, jnp.sum(q, axis=1, keepdims=True), 0.0)
                both.append(dot(weights.astype(BF), dyb))
            dxw[m, :, lanes] = jnp.where(first, both[0], both[1])
    fold = lambda v: dot_mask(v, expand, NT)
    for m in range(batch):
        x = cx[m, :, :inner]
        b = cx[m, :, inner : inner + states]
        c = cx[m, :, inner + states :]
        b_high, b_rest = halves(b)
        dyv, dxv, dtv, cums = dy[m], dxw[m], dt[m], cum[m]
        last = cums[n - 1 : n, :]
        entered, later_b = state[m], incoming[m]
        moved = dot_mask(jnp.exp(cums), expand) * dyv
        carried = dot3(c, entered)
        tail = jnp.exp(last - cums)
        weight = tail * dtv
        weight_wide = dot_mask(weight, expand)
        pulled = dot(b_high, later_b) + dot(b_rest, later_b)
        dx = dot_mask(dtv, expand) * dxv + weight_wide * pulled + skip[...] * dyv
        dw = fold(x * pulled)
        wdw = weight * dw
        change = jnp.transpose(rowq[m]) + fold(carried * moved) - colq[m] - wdw
        ends = jnp.sum(entered * later_b.astype(F32), axis=0, keepdims=True)
        ends = jnp.sum(wdw, axis=0, keepdims=True) + jnp.exp(last) * fold(jnp.broadcast_to(ends, (8, inner)))[0:1]
        log_grad = mask_dot(order_mask(n, False).astype(F32).astype(BF), change) + ends
        ddt = fold(x * dxv) + tail * dw + a_neg[...] * log_grad
        ddt_raw = ddt * sigmoid(proj[m, :, inner + wide :] + dt_bias[...])
        g_in[m, :, inner + wide :] = ddt_raw.astype(BF)
        small_o[m] = jnp.concatenate(
            [
                jnp.sum(ddt_raw, axis=0, keepdims=True),
                jnp.sum(dtv * log_grad, axis=0, keepdims=True) * a_neg[...],
                fold(jnp.broadcast_to(jnp.sum(x * dyv, axis=0, keepdims=True), (8, inner)))[0:1],
                jnp.zeros((5, LANES), F32),
            ],
            axis=0,
        )
        xw_high, xw_rest = halves(x * weight_wide)
        dc = dot3(d_scores[m], b, TN) + dot3(moved, entered, NT)
        db = dot3(d_scores[m], c) + dot(xw_high, later_b, NT) + dot(xw_rest, later_b, NT)
        xbc = proj[m, :, columns].astype(BF).astype(F32)
        pre = conv_pre(ext, xbc, halo[m, 8:].astype(F32), taps[...], bias[...])
        sig = sigmoid(pre)
        d_act = jnp.concatenate([dx, db, dc], axis=1) * sig * (1.0 + pre * (1.0 - sig))
        dpre[m, 0:n, :] = d_act
        rim_copy = line.halo(dpre.at[m, pl.ds(0, 8)], rim.at[m], m, rim_send, rim_recv)
        pl.when(jnp.logical_not(line.ends))(rim_copy.start)
        rows = [jnp.sum(d_act * ext[5 + k : 5 + k + n, :], axis=0, keepdims=True) for k in range(4)]
        rows.append(jnp.sum(d_act, axis=0, keepdims=True))
        conv_o[m] = jnp.concatenate(rows + [jnp.zeros((3, wide), F32)], axis=0)

    @pl.when(line.starts)
    def _():
        rim[...] = jnp.zeros_like(rim)

    for m in range(batch):
        rim_copy = line.halo(dpre.at[m, pl.ds(0, 8)], rim.at[m], m, rim_send, rim_recv)
        pl.when(jnp.logical_not(line.starts))(rim_copy.wait_recv)
        dpre[m, n : n + 8, :] = rim[m]
        total = taps[3:4, :] * dpre[m, 0:n, :]
        for k in range(3):
            total = total + taps[k : k + 1, :] * dpre[m, 3 - k : 3 - k + n, :]
        g_in[m, :, columns] = total.astype(BF)
        pl.when(jnp.logical_not(line.ends))(rim_copy.wait_send)
    line.finish()
    if has_across:
        outputs.finish()


def ssd_bwd(dyn, y, proj, halo, cx, dt, cum, state, stats, taps, bias, dt_bias, a_neg, skip, gain, outputs,
            dims, size, heads_axis, full):
    has_across = bool(outputs)
    heads, inner, states = dims
    batch, n, wide = cx.shape
    vm = pl.BlockSpec(memory_space=pltpu.VMEM)
    moved = (batch, states, inner)
    outs = (
        shape((batch, n, inner + wide + LANES), BF),
        shape((batch, 8, inner), F32),
        shape((batch, 8, wide), F32),
        shape((batch, 8, LANES), F32),
    ) + tuple(shape((2 * a.shape[0], a.shape[1]), BF) for a in outputs[1:])
    sems = lambda k: pltpu.SemaphoreType.DMA((k,))
    return pl.pallas_call(
        functools.partial(ssd_bwd_kernel, dims, size, heads_axis, full, has_across),
        out_shape=outs,
        in_specs=[vm] * (15 + len(outputs)),
        out_specs=(vm,) * 4 + (pl.BlockSpec(memory_space=pl.ANY),) * has_across,
        scratch_shapes=[
            pltpu.VMEM((batch, n, inner), F32),
            pltpu.VMEM((batch, n, inner), F32),
            pltpu.VMEM((batch, n + 8, wide), F32),
            pltpu.VMEM(moved, F32),
            pltpu.VMEM((batch, 8, inner), F32),
            pltpu.VMEM((n + 8, wide), F32),
            pltpu.VMEM((batch, LANES, n), F32),
            pltpu.VMEM((batch, n, LANES), F32),
            pltpu.VMEM((batch, n, n), F32),
            pltpu.VMEM(moved, BF),
            pltpu.VMEM(moved, BF),
            pltpu.VMEM((batch, 8, wide), F32),
            pltpu.VMEM((batch, 8, n), F32),
            pltpu.VMEM((heads_axis - 1, batch, 8, n), F32),
            sems(batch * PARTS),
            sems(batch * PARTS),
            sems(batch),
            sems(batch),
            sems(heads_axis - 1),
            sems(heads_axis - 1),
        ]
        + (collect_sems(heads_axis) if has_across else []),
        compiler_params=pltpu.CompilerParams(
            collective_id=10 + has_across, has_side_effects=True, vmem_limit_bytes=VMEM_LIMIT
        ),
        name="ssd_bwd",
    )(dyn, y, proj, halo, cx, dt, cum, state, stats, taps, bias, dt_bias, a_neg, skip, gain, *outputs)


def greet(size, core=False):
    me = lax.axis_index("head")
    barrier = pltpu.get_barrier_semaphore()
    peers = [{"head": lax.rem(me + d, size)} for d in range(1, size)]
    others = [{"section": 1 - lax.axis_index("section")}] if core else []
    for peer in peers + others:
        pl.semaphore_signal(barrier, inc=1, device_id=peer, device_id_type=MESH)
    pl.semaphore_wait(barrier, len(peers) + len(others))
    return me, peers


def block_of(index, rows):
    return pl.ds(pl.multiple_of(index * rows, rows), rows)


def normal(u, gain):
    uv = u.astype(F32)
    s = lax.rsqrt(jnp.sum(uv * uv, axis=1, keepdims=True) / uv.shape[1] + EPSILON)
    return (uv * s * gain).astype(BF)


def head_fwd_kernel(size, onward, yn, w_out, u, *refs):
    if onward:
        w_in, gain, h_o, normed_o, proj_o, out, got, send, recv = refs
    else:
        h_o, out, got, send, recv = refs
    rows = yn.shape[0] // size
    me, peers = greet(size)
    copies = []
    for d, peer in enumerate(peers):
        to = lax.rem(me + d + 1, size)
        out[d] = dot(yn[block_of(to, rows), :], w_out[...]).astype(out.dtype)
        copies.append(push(out.at[d], got.at[d], send.at[0, d], recv.at[0, d], peer))
    mine = block_of(me, rows)
    total = dot(yn[mine, :], w_out[...])
    for copy in copies:
        copy.wait()
    for d in range(size - 1):
        total = total + got[d].astype(F32)
    h = (u[mine, :].astype(F32) + total).astype(BF)
    if not onward:
        h_o[...] = h
        return
    h_o[mine, :] = h
    copies = [
        push(h_o.at[mine], h_o.at[mine], send.at[1, d], recv.at[1, d], peer) for d, peer in enumerate(peers)
    ]

    def project(at):
        normed = normal(h_o[at, :], gain[...])
        normed_o[at, :] = normed
        proj_o[at, :] = dot(normed, w_in[...])

    project(mine)
    for d, copy in enumerate(copies):
        copy.wait_recv()
        project(block_of(lax.rem(me + size - d - 1, size), rows))
    for copy in copies:
        copy.wait_send()


def head_fwd(yn, w_out, u, size, onward):
    n, d_model = u.shape
    rows = n // size
    vm = pl.BlockSpec(memory_space=pltpu.VMEM)
    kind = F32 if onward else BF
    outs = [shape((n if onward else rows, d_model), BF)]
    if onward:
        outs += [shape((n, d_model), BF), shape((n, onward[0].shape[1]), F32)]
    return pl.pallas_call(
        functools.partial(head_fwd_kernel, size, bool(onward)),
        out_shape=tuple(outs),
        in_specs=[vm] * (3 + len(onward)),
        out_specs=(vm,) * len(outs),
        scratch_shapes=[
            pltpu.VMEM((size - 1, rows, d_model), kind),
            pltpu.VMEM((size - 1, rows, d_model), kind),
            pltpu.SemaphoreType.DMA((2, size - 1)),
            pltpu.SemaphoreType.DMA((2, size - 1)),
        ],
        compiler_params=pltpu.CompilerParams(
            collective_id=3 if onward else 6, has_side_effects=True, vmem_limit_bytes=VMEM_LIMIT
        ),
        name="head_fwd",
    )(yn, w_out, u, *onward)


def input_gradient(dn, u, gain, above):
    uv = u.astype(F32)
    width = uv.shape[1]
    s = lax.rsqrt(jnp.sum(uv * uv, axis=1, keepdims=True) / width + EPSILON)
    scaled = dn * gain
    inner = jnp.sum(scaled * uv, axis=1, keepdims=True)
    return (
        above.astype(F32) + s * scaled - uv * (s * s * s * inner / width),
        jnp.sum(dn * uv * s, axis=0, keepdims=True),
    )


def body_tile(normed, g_in, yn, go, half, i):
    tile, count = 256, normed.shape[1] // 256
    wide = yn.shape[1]
    at = pl.ds(pl.multiple_of(half * wide, wide), wide)
    if i < count:
        return dot(normed[:, i * tile : (i + 1) * tile], g_in[:, at], TN)
    return dot(yn[:, (i - count) * tile : (i - count + 1) * tile], go[:, at], TN)


def head_bwd_kernel(size, g_in, w_in, upper, u, gain, w_out, normed, yn, du_o, mine_o, grad_o, dyn_o, body_o,
                    out, got, body_send, body_got, send, recv, body_ss, body_rs):
    rows = u.shape[0] // size
    me, peers = greet(size, core=True)
    layer = lax.axis_index("section")
    other = {"section": 1 - layer}
    copies = []
    for d, peer in enumerate(peers):
        to = lax.rem(me + d + 1, size)
        out[d] = dot(g_in[block_of(to, rows), :], w_in[...], NT).astype(BF)
        copies.append(push(out.at[d], got.at[d], send.at[0, d], recv.at[0, d], peer))
    mine = block_of(me, rows)
    dn = dot(g_in[mine, :], w_in[...], NT)
    tiles = body_o.shape[0] // 256
    body_copies = []
    for i in range(tiles):
        at = pl.ds(i * 256, 256)
        body_send[at, :] = body_tile(normed, g_in, yn, upper, 1 - layer, i).astype(BF)
        body_copies.append(push(body_send.at[at], body_got.at[at], body_ss.at[i], body_rs.at[i], other))
    for i in range(tiles):
        body_o[i * 256 : (i + 1) * 256, :] = body_tile(normed, g_in, yn, upper, layer, i).astype(BF)
    for copy in copies:
        copy.wait()
    for d in range(size - 1):
        dn = dn + got[d].astype(F32)
    du, grad = input_gradient(dn, u[mine, :], gain[...], upper[mine, :])
    grad_o[...] = jnp.broadcast_to(grad, grad_o.shape)
    mine_o[...] = du
    du_o[mine, :] = du.astype(BF)
    copies = [
        push(du_o.at[mine], du_o.at[mine], send.at[1, d], recv.at[1, d], peer) for d, peer in enumerate(peers)
    ]
    for i in range(tiles):
        at = slice(i * 256, (i + 1) * 256)
        body_copies[i].wait()
        body_o[at, :] = (body_o[at, :].astype(F32) + body_got[at, :].astype(F32)).astype(BF)
    dyn_o[mine, :] = dot(du_o[mine, :], w_out[...], NT)
    for d, copy in enumerate(copies):
        copy.wait_recv()
        at = block_of(lax.rem(me + size - d - 1, size), rows)
        dyn_o[at, :] = dot(du_o[at, :], w_out[...], NT)
    for copy in copies:
        copy.wait_send()


def head_bwd(g_in, w_in, upper, u, gain, w_out, normed, yn, size):
    n, d_model = u.shape
    inner = yn.shape[1]
    rows = n // size
    tiles = (d_model + inner) // 256
    body = (d_model + inner, d_model // 2)
    vm = pl.BlockSpec(memory_space=pltpu.VMEM)
    return pl.pallas_call(
        functools.partial(head_bwd_kernel, size),
        out_shape=(
            shape((n, d_model), BF),
            shape((rows, d_model), F32),
            shape((8, d_model), F32),
            shape((n, inner), F32),
            shape(body, BF),
        ),
        in_specs=[vm] * 8,
        out_specs=(vm,) * 5,
        scratch_shapes=[
            pltpu.VMEM((size - 1, rows, d_model), BF),
            pltpu.VMEM((size - 1, rows, d_model), BF),
            pltpu.VMEM(body, BF),
            pltpu.VMEM(body, BF),
            pltpu.SemaphoreType.DMA((2, size - 1)),
            pltpu.SemaphoreType.DMA((2, size - 1)),
            pltpu.SemaphoreType.DMA((tiles,)),
            pltpu.SemaphoreType.DMA((tiles,)),
        ],
        compiler_params=pltpu.CompilerParams(
            collective_id=5, has_side_effects=True, vmem_limit_bytes=VMEM_LIMIT
        ),
        name="head_bwd",
    )(g_in, w_in, upper, u, gain, w_out, normed, yn)


class Collect:
    def __init__(self, by_rows, size, rows, whole, out, local, send, recv):
        self.by_rows, self.size = by_rows, size
        self.rows, self.whole, self.out = rows, whole, out
        self.local, self.send, self.recv = local, send, recv
        self.core, self.head = lax.axis_index("section"), lax.axis_index("head")
        count = rows.shape[0]
        self.row_part = pl.ds(pl.multiple_of(self.core * whole.shape[0] + self.head * count, count), count)
        self.whole_part = block_of(self.core, whole.shape[0])

    def greeted(self):
        return [
            {"section": lax.rem(self.core + c, 2), "head": lax.rem(self.head + d, self.size)}
            for c in range(2)
            for d in range(self.size)
            if c or d
        ]

    def row_copy(self, sender, d):
        return pltpu.make_async_remote_copy(
            src_ref=self.rows, dst_ref=self.out.at[self.row_part],
            send_sem=self.send.at[d], recv_sem=self.recv.at[sender * self.size + d],
            device_id={"section": self.by_rows, "head": lax.rem(self.head + d, self.size)}, device_id_type=MESH,
        )

    def whole_copy(self):
        return pltpu.make_async_remote_copy(
            src_ref=self.whole, dst_ref=self.out.at[self.whole_part],
            send_sem=self.send.at[self.size], recv_sem=self.recv.at[2 * self.size],
            device_id={"section": 1 - self.by_rows}, device_id_type=MESH,
        )

    def start(self):
        @pl.when(self.core == self.by_rows)
        def _():
            pltpu.make_async_copy(self.rows, self.out.at[self.row_part], self.local).start()
            for d in range(1, self.size):
                self.row_copy(self.by_rows, d).start()
            self.whole_copy().start()

        @pl.when(self.core != self.by_rows)
        def _():
            pltpu.make_async_copy(self.whole, self.out.at[self.whole_part], self.local).start()
            for d in range(self.size):
                self.row_copy(1 - self.by_rows, d).start()

    def finish(self):
        @pl.when(self.core == self.by_rows)
        def _():
            pltpu.make_async_copy(self.rows, self.out.at[self.row_part], self.local).wait()
            for d in range(1, self.size):
                self.row_copy(self.by_rows, d).wait()
            for d in range(self.size):
                self.row_copy(1 - self.by_rows, d).wait_recv()
            self.whole_copy().wait_send()

        @pl.when(self.core != self.by_rows)
        def _():
            pltpu.make_async_copy(self.whole, self.out.at[self.whole_part], self.local).wait()
            for d in range(self.size):
                self.row_copy(1 - self.by_rows, d).wait_send()
            self.whole_copy().wait_recv()


def collect_sems(size):
    return [
        pltpu.SemaphoreType.DMA,
        pltpu.SemaphoreType.DMA((size + 1,)),
        pltpu.SemaphoreType.DMA((2 * size + 1,)),
    ]


OWN = 32
SHARED = 160
PIECE = 32
TAIL = (OWN + SHARED) // PIECE
FEW = 16


def grad_tail_kernel(dims, normed, g_in, conv, scalars, gate, gain, tail, few):
    heads, inner, states = dims
    half = normed.shape[1] // 2
    split = 2 * inner + 2 * states
    rest = dot(g_in[:, 2 * inner :], normed[...], TN).astype(BF)
    step = (tail.shape[0] - OWN) // 2
    tail[...] = jnp.zeros_like(tail)
    for i in range(2):
        lanes = slice(i * half, (i + 1) * half)
        tail[i * OWN // 2 : (i + 1) * OWN // 2, :] = rest[2 * states : 2 * states + OWN // 2, lanes]
        tail[OWN + i * step : OWN + i * step + 2 * states, :] = rest[: 2 * states, lanes]
    conv_sum, scalar_sum, gate_sum = conv[0], scalars[0], gate[0]
    for i in range(1, conv.shape[0]):
        conv_sum, scalar_sum, gate_sum = conv_sum + conv[i], scalar_sum + scalars[i], gate_sum + gate[i]
    few[...] = jnp.zeros_like(few)
    few[0:5, :] = conv_sum[0:5, :inner]
    few[5:6, :] = gate_sum[0:1]
    for i in range(3):
        few[6:7, i * LANES : (i + 1) * LANES] = scalar_sum[i : i + 1]
    few[8:9, :] = gain[0:1, :half]
    few[9:10, :] = gain[0:1, half:]
    few[10:15, 0 : 2 * states] = conv_sum[0:5, inner:]


def grad_tail(normed, g_in, conv, scalars, gate, gain, dims, head_size):
    heads, inner, states = dims
    width = normed.shape[1]
    vm = pl.BlockSpec(memory_space=pltpu.VMEM)
    return pl.pallas_call(
        functools.partial(grad_tail_kernel, dims),
        out_shape=(shape((OWN + head_size * SHARED, width // 2), BF), shape((FEW, width // 2), F32)),
        in_specs=[vm] * 6,
        out_specs=(vm, vm),
        compiler_params=pltpu.CompilerParams(vmem_limit_bytes=VMEM_LIMIT),
        name="grad_tail",
    )(normed, g_in, conv, scalars, gate, gain)


def grad_sum_kernel(size, heads, skew, g_in, w_in, above, u, gain, normed, yn, go, tail0, tail1, few0, few1, done,
                    out, shared_o, few_o, traded, du_o,
                    own, core, got, shared, shared_core, shared_got, few_core, few_seq, few_head,
                    body_send, du_out, du_got, du_rows, few_mine,
                    cs, cr, rs, rr, bs, br, ts, tr, hs, hr, xs, fs, fr, gs, gr, ds, dr, c_local, c_send, c_recv):
    me, layer, head = lax.axis_index("seq"), lax.axis_index("section"), lax.axis_index("head")
    rows = out.shape[0]
    plain = rows - SHARED
    half = rows // 2
    parts = half // PIECE
    up, down, other = {"seq": me + 1}, {"seq": me - 1}, {"section": 1 - layer}
    peers = [{"head": lax.rem(head + d, heads)} for d in range(1, heads)]
    blocks = [{"seq": lax.rem(me + d, size)} for d in range(1, size)]
    low_end, high_end = me == 0, me == size - 1
    barrier = pltpu.get_barrier_semaphore()
    inputs = Collect(0, heads, du_rows, go, du_o, c_local, c_send, c_recv)
    plane = inputs.greeted()
    for peer in plane + blocks:
        pl.semaphore_signal(barrier, inc=1, device_id=peer, device_id_type=MESH)
    pl.semaphore_wait(barrier, len(plane) + len(blocks))
    rows_here = u.shape[0] // heads
    du_copies = []
    for d, peer in enumerate(peers):
        to = block_of(lax.rem(head + d + 1, heads), rows_here)
        du_out[d] = dot(g_in[to, :], w_in[...], NT).astype(BF)
        du_copies.append(push(du_out.at[d], du_got.at[d], ds.at[d], dr.at[d], peer))
    tiles = body_send.shape[0] // 256
    body_copies = []
    for i in range(tiles):
        at = pl.ds(i * 256, 256)
        body_send[at, :] = body_tile(normed, g_in, yn, go, 1 - layer, i).astype(BF)
        body_copies.append(push(body_send.at[at], core.at[at], cs.at[i], cr.at[i], other))
    for i in range(tiles):
        own[i * 256 : (i + 1) * 256, :] = body_tile(normed, g_in, yn, go, layer, i).astype(BF)
    here = block_of(head, rows_here)
    dn = dot(g_in[here, :], w_in[...], NT)
    for d in range(heads - 1):
        du_copies[d].wait()
        dn = dn + du_got[d].astype(F32)
    du, grad = input_gradient(dn, u[here, :], gain[...], above[...])
    du_rows[...] = du.astype(BF)
    inputs.start()
    few_mine[...] = few0[...]
    wide = few0.shape[1]
    for i in range(2):
        few_mine[8 + i : 9 + i, :] = grad[:, i * wide : (i + 1) * wide]
    for i in range(tiles):
        at = slice(i * 256, (i + 1) * 256)
        body_copies[i].wait()
        own[at, :] = (own[at, :].astype(F32) + core[at, :].astype(F32)).astype(BF)

    def fetch_tail(ours, others):
        return (
            pltpu.make_async_copy(ours, shared, xs.at[0]),
            pltpu.make_async_remote_copy(
                src_ref=others, dst_ref=shared_core, send_sem=xs.at[1], recv_sem=xs.at[2],
                device_id=other, device_id_type=MESH,
            ),
        )

    def start_all(copies):
        for copy in copies:
            copy.start()

    pl.when(layer == 0)(lambda: start_all(fetch_tail(tail0, tail1)))
    pl.when(layer == 1)(lambda: start_all(fetch_tail(tail1, tail0)))

    def few_to_core(src):
        return pltpu.make_async_remote_copy(
            src_ref=src, dst_ref=few_core, send_sem=xs.at[3], recv_sem=xs.at[4],
            device_id=other, device_id_type=MESH,
        )

    few_to_seq = lambda d: pltpu.make_async_remote_copy(
        src_ref=few_seq.at[me], dst_ref=few_seq.at[me], send_sem=fs.at[d], recv_sem=fr.at[d],
        device_id=blocks[d], device_id_type=MESH,
    )
    few_to_head = lambda d: pltpu.make_async_remote_copy(
        src_ref=few_head.at[head], dst_ref=few_head.at[head], send_sem=gs.at[d], recv_sem=gr.at[d],
        device_id=peers[d], device_id_type=MESH,
    )
    give_all = pltpu.make_async_remote_copy(
        src_ref=done, dst_ref=traded, send_sem=xs.at[5], recv_sem=xs.at[6],
        device_id=other, device_id_type=MESH,
    )
    pl.when(layer == 0)(lambda: few_to_core(few1).start())
    pl.when(layer == 1)(lambda: few_to_core(few_mine).start())
    pl.when(layer == 0)(give_all.start)

    shift = parts * 3 // 5

    def order(side, p):
        return lax.rem(p + (shift if side else 0), parts)

    def place(side, p):
        return pl.ds(pl.multiple_of(side * half + order(side, p) * PIECE, PIECE), PIECE)

    def unless_tail(side, p, act):
        if side:
            pl.when(order(side, p) < parts - TAIL)(act)
        else:
            act()

    for copy in fetch_tail(tail0, tail1):
        copy.wait()
    shared[...] = (shared[...].astype(F32) + shared_core[...].astype(F32)).astype(BF)
    block = lambda i: pl.ds(pl.multiple_of(OWN + i * SHARED, 32), SHARED)
    scatter = lambda d: pltpu.make_async_remote_copy(
        src_ref=shared.at[block(lax.rem(head + d + 1, heads))], dst_ref=shared_got.at[d],
        send_sem=hs.at[0, d], recv_sem=hr.at[0, d], device_id=peers[d], device_id_type=MESH,
    )
    gather = lambda d: pltpu.make_async_remote_copy(
        src_ref=shared_o.at[head], dst_ref=shared_o.at[head],
        send_sem=hs.at[1, d], recv_sem=hr.at[1, d], device_id=peers[d], device_id_type=MESH,
    )
    for d in range(heads - 1):
        scatter(d).start()

    def sending(side, p, back, source):
        at = place(side, p)
        towards = down if (side == 0) != back else up
        target, send, recv = (out, bs, br) if back else (got, rs, rr)
        return pltpu.make_async_remote_copy(
            src_ref=source.at[at], dst_ref=target.at[at], send_sem=send.at[side, p],
            recv_sem=recv.at[side, p], device_id=towards, device_id_type=MESH,
        )

    def give(side, p):
        at = place(side, p)
        return pltpu.make_async_remote_copy(
            src_ref=out.at[at], dst_ref=traded.at[at], send_sem=ts.at[side, p], recv_sem=tr.at[side, p],
            device_id=other, device_id_type=MESH,
        )

    def start_give(side, p):
        unless_tail(side, p, lambda: pl.when(layer == 1)(give(side, p).start))

    def reduce(side, p):
        start, end = (high_end, low_end) if side == 0 else (low_end, high_end)
        at = place(side, p)

        @pl.when(start)
        def _():
            sending(side, p, False, own).start()

        @pl.when(jnp.logical_not(start))
        def _():
            sending(side, p, False, got).wait_recv()
            summed = (own[at, :].astype(F32) + got[at, :].astype(F32)).astype(BF)

            @pl.when(end)
            def _():
                out[at, :] = summed
                sending(side, p, True, out).start()
                start_give(side, p)

            @pl.when(jnp.logical_not(end))
            def _():
                got[at, :] = summed
                sending(side, p, False, got).start()

    def back(side, p):
        start, end = (high_end, low_end) if side == 0 else (low_end, high_end)

        @pl.when(jnp.logical_not(end))
        def _():
            sending(side, p, True, out).wait_recv()

            @pl.when(jnp.logical_not(start))
            def _():
                sending(side, p, True, out).start()

            start_give(side, p)

    def guarded(act, side, p):
        @pl.when(jnp.logical_and(p >= 0, p < parts))
        def _():
            act(side, p)

    far = size - 1
    ready = parts - shift - TAIL - 1
    finished = parts - shift + skew * (2 * far - me)

    def step(t, _):
        @pl.when(t == 2)
        def _():
            few_to_core(few_mine).wait()
            pl.when(layer == 0)(lambda: few_seq.__setitem__(me, few_mine[...] + few_core[...]))
            pl.when(layer == 1)(lambda: few_seq.__setitem__(me, few1[...] + few_core[...]))
            for d in range(size - 1):
                few_to_seq(d).start()

        @pl.when(t == 8)
        def _():
            for d in range(size - 1):
                few_to_seq(d).wait()
            total = few_seq[0]
            for i in range(1, size):
                total = total + few_seq[i]
            few_o[0 : FEW // 2, :] = total[0 : FEW // 2]
            few_head[head] = total[FEW // 2 :]
            for d in range(heads - 1):
                few_to_head(d).start()

        @pl.when(t == 14)
        def _():
            for d in range(heads - 1):
                few_to_head(d).wait()
            total = few_head[0]
            for i in range(1, heads):
                total = total + few_head[i]
            few_o[FEW // 2 :, :] = total

        @pl.when(t == ready)
        def _():
            total = shared[block(head), :].astype(F32)
            for d in range(heads - 1):
                scatter(d).wait()
                total = total + shared_got[d].astype(F32)
            own[plain : plain + SHARED, :] = total.astype(BF)
            own[plain - OWN : plain, :] = shared[0:OWN, :]

        guarded(reduce, 0, t - skew * (far - me))
        guarded(reduce, 1, t - skew * me)
        guarded(back, 0, t - skew * (far + me))
        guarded(back, 1, t - skew * (2 * far - me))

        @pl.when(t == finished)
        def _():
            shared_o[head] = out[plain:rows, :]
            for d in range(heads - 1):
                gather(d).start()

        return 0

    lax.fori_loop(0, parts + 2 * skew * far, step, 0)

    def drain(p, _):
        for side in range(2):
            start, end = (high_end, low_end) if side == 0 else (low_end, high_end)

            @pl.when(jnp.logical_not(end))
            def _():
                sending(side, p, False, got).wait_send()

            @pl.when(jnp.logical_not(start))
            def _():
                sending(side, p, True, out).wait_send()

        return 0

    lax.fori_loop(0, parts, drain, 0)
    for d in range(heads - 1):
        gather(d).wait()

    def drain_trade(p, _):
        for side in range(2):
            unless_tail(side, p, lambda: pl.when(layer == 0)(give(side, p).wait_recv))
            unless_tail(side, p, lambda: pl.when(layer == 1)(give(side, p).wait_send))
        return 0

    lax.fori_loop(0, parts, drain_trade, 0)
    pl.when(layer == 0)(give_all.wait_send)
    pl.when(layer == 1)(give_all.wait_recv)
    inputs.finish()


def grad_sum(layer0, tails, fews, done, size, heads, skew=2):
    width = done.shape[1]
    rows = done.shape[0] + OWN + SHARED
    parts = rows // 2 // PIECE
    n, d_model = layer0[3].shape
    vm = pl.BlockSpec(memory_space=pltpu.VMEM)
    anywhere = pl.BlockSpec(memory_space=pl.ANY)
    pair = pltpu.SemaphoreType.DMA((2, parts))
    sems = lambda *k: pltpu.SemaphoreType.DMA(k)
    tiles = done.shape[0] // 256
    return pl.pallas_call(
        functools.partial(grad_sum_kernel, size, heads, skew),
        out_shape=(
            shape((rows, width), BF),
            shape((heads, SHARED, width), BF),
            shape((FEW, width), F32),
            shape(done.shape, BF),
            shape((2 * n, d_model), BF),
        ),
        in_specs=[vm] * 8 + [anywhere] * 2 + [vm] * 2 + [anywhere],
        out_specs=(vm, vm, vm, anywhere, anywhere),
        scratch_shapes=[pltpu.VMEM((rows, width), BF) for _ in range(3)]
        + [pltpu.VMEM((OWN + heads * SHARED, width), BF) for _ in range(2)]
        + [pltpu.VMEM((heads - 1, SHARED, width), BF)]
        + [pltpu.VMEM((FEW, width), F32), pltpu.VMEM((size, FEW, width), F32)]
        + [pltpu.VMEM((heads, FEW // 2, width), F32)]
        + [pltpu.VMEM(done.shape, BF)]
        + [pltpu.VMEM((heads - 1, n // heads, d_model), BF) for _ in range(2)]
        + [pltpu.VMEM((n // heads, d_model), BF), pltpu.VMEM((FEW, width), F32)]
        + [sems(tiles)] * 2
        + [pair] * 6
        + [sems(2, heads - 1)] * 2
        + [sems(7)]
        + [sems(size - 1)] * 2
        + [sems(heads - 1)] * 4
        + collect_sems(heads),
        compiler_params=pltpu.CompilerParams(
            collective_id=8, has_side_effects=True, vmem_limit_bytes=VMEM_LIMIT
        ),
        name="grad_sum",
    )(*layer0, *tails, *fews, done)


def unpack_kernel(dims, mine, traded, done, mine_low, traded_low, done_low, own, shared, few,
                  z_o, x_o, out_o, bc_o, dt_o, conv_o, conv_bias_o, bc_conv_o, bc_bias_o,
                  dt_bias_o, a_log_o, skip_o, gate_o, gain_o):
    heads, inner, states = dims
    layer = lax.axis_index("section")
    half = own.shape[1]

    @pl.when(layer == 0)
    def _():
        z_o[...] = mine[...].astype(F32)
        x_o[...] = traded[...].astype(F32)
        out_o[:, :half] = mine_low[...].astype(F32)
        out_o[:, half:] = traded_low[...].astype(F32)

    @pl.when(layer == 1)
    def _():
        z_o[...] = traded[...].astype(F32)
        x_o[...] = done[...].astype(F32)
        out_o[:, :half] = traded_low[...].astype(F32)
        out_o[:, half:] = done_low[...].astype(F32)

    @pl.when(pl.program_id(0) == 0)
    def _():
        blocks = jnp.concatenate([shared[i] for i in range(shared.shape[0])], axis=0)
        step = blocks.shape[0] // 2
        for i in range(2):
            rows = slice(i * half, (i + 1) * half)
            bc_o[rows, :] = jnp.transpose(blocks[i * step : i * step + 2 * states].astype(F32))
            dts = own[i * OWN // 2 : (i + 1) * OWN // 2, :].astype(F32)
            dts = jnp.concatenate([dts, jnp.zeros((LANES - OWN // 2, half), F32)], axis=0)
            dt_o[rows, :] = jnp.transpose(dts)[:, :heads]
            gain_o[:, rows] = few[8 + i : 9 + i, :]
        conv_o[...] = few[0:4, :]
        conv_bias_o[...] = few[4:5, :]
        gate_o[...] = few[5:6, :]
        bc_conv_o[...] = few[10:14, 0 : 2 * states]
        bc_bias_o[...] = few[14:15, 0 : 2 * states]
        dt_bias_o[...] = few[6:7, 0:heads]
        a_log_o[...] = few[6:7, LANES : LANES + heads]
        skip_o[...] = few[6:7, 2 * LANES : 2 * LANES + heads]


def unpack(grads, traded, done, shared, few, dims, steps=6):
    heads, inner, states = dims
    half = grads.shape[1]
    width = 2 * half
    tall, low = width // steps, inner // steps
    upper = pl.BlockSpec((tall, half), lambda i: (i, 0))
    lower = pl.BlockSpec((low, half), lambda i: (width // low + i, 0))
    whole = lambda a: pl.BlockSpec(a.shape, lambda i: (0,) * len(a.shape))
    outs = [
        ((width, inner), (tall, inner)),
        ((width, inner), (tall, inner)),
        ((inner, width), (low, width)),
    ]
    fixed = [
        (width, 2 * states), (width, heads), (4, inner), (1, inner), (4, 2 * states), (1, 2 * states),
        (1, heads), (1, heads), (1, heads), (1, inner), (1, width),
    ]
    return pl.pallas_call(
        functools.partial(unpack_kernel, dims),
        grid=(steps,),
        out_shape=[shape(a, F32) for a, _ in outs] + [shape(a, F32) for a in fixed],
        in_specs=[upper] * 3
        + [lower] * 3
        + [pl.BlockSpec((OWN, half), lambda i: ((width + inner) // OWN, 0)), whole(shared), whole(few)],
        out_specs=[pl.BlockSpec(b, lambda i: (i, 0)) for _, b in outs]
        + [pl.BlockSpec(a, lambda i: (0, 0)) for a in fixed],
        compiler_params=pltpu.CompilerParams(vmem_limit_bytes=VMEM_LIMIT),
        name="unpack",
    )(grads, traded, done, grads, traded, done, grads, shared, few)


def normalise(u, gain):
    uv = u.astype(F32)
    s = lax.rsqrt(jnp.mean(uv * uv, axis=-1, keepdims=True) + EPSILON)
    return (uv * s * gain).astype(BF)


def on_device(
    inputs, cotangent, norm_gain, w_z, w_x, w_bc, w_dt, conv_x, conv_x_bias, conv_bc, conv_bc_bias,
    dt_bias, a_log, d_skip, gate_gain, w_out,
):
    me = lax.axis_index("section")
    seq_size, head_size = lax.axis_size("seq"), lax.axis_size("head")
    micro, n, d_model = inputs.shape
    batch = micro // 2
    tokens = batch * n
    inner, heads, states = w_z.shape[2], w_dt.shape[2], w_bc.shape[2] // 2
    wide = inner + 2 * states
    full = inner * head_size
    dims = (heads, inner, states)
    pad_heads = lambda a: jnp.pad(a, ((0, 0),) * (a.ndim - 1) + ((0, LANES - heads),))

    taps_x = jnp.concatenate([conv_x[0], conv_x_bias, jnp.zeros((3, inner), F32)], axis=0)
    taps_bc = jnp.concatenate([conv_bc[0], conv_bc_bias, jnp.zeros((3, 2 * states), F32)], axis=0)
    taps = jnp.concatenate([taps_x, taps_bc], axis=1)
    scalars = pad_heads(jnp.concatenate([dt_bias, -jnp.exp(a_log)], axis=0)).reshape(1, -1)
    vectors = jnp.concatenate(
        [
            jnp.repeat(d_skip[0], inner // heads)[None],
            gate_gain,
            jnp.pad(scalars, ((0, 0), (0, inner - 2 * LANES))),
            jnp.zeros((5, inner), F32),
        ],
        axis=0,
    )
    gains = jnp.broadcast_to(norm_gain, (8, d_model))
    w_in2, w_out2, vectors2 = both_layers(
        [[w_z[0], w_x[0], w_bc[0], pad_heads(w_dt[0])], [w_out[0]], [taps, vectors, gains]]
    )
    gains2 = vectors2[:, :, wide + inner :]
    taps2, vectors2 = vectors2[:, :, :wide], vectors2[:, :, wide : wide + inner]

    u = lax.dynamic_slice_in_dim(inputs, me * batch, batch, 0).reshape(tokens, d_model)
    cot = lax.dynamic_slice_in_dim(cotangent, me * batch, batch, 0).reshape(tokens, d_model)

    consts = []
    for l in range(2):
        gain = gains2[l, 0:1]
        kernel, bias = taps2[l, 0:4], taps2[l, 4:5]
        skip, gate = vectors2[l, 0:1], vectors2[l, 1:2]
        dt_b, a_neg = vectors2[l, 2:3, :LANES], vectors2[l, 2:3, LANES : 2 * LANES]
        consts.append((gain, kernel, bias, dt_b, a_neg, skip, gate))
    flat = lambda a: a.reshape(tokens, -1)
    stacked = lambda a: a.reshape(batch, n, -1)

    normed0 = normalise(u, consts[0][0])
    proj0 = stacked(dot(normed0, w_in2[0]))
    cx0, dt0, cum0, state0, halo0, y0, yn0, stats0 = ssd_fwd(
        proj0, *consts[0][1:], None, dims, seq_size, head_size, full
    )
    h0, normed1, proj1 = head_fwd(flat(yn0), w_out2[0], u, head_size, [w_in2[1], consts[1][0]])
    proj1 = stacked(proj1)
    dyn1 = stacked(dot(cot, w_out2[1], NT))
    cx1, dt1, cum1, state1, halo1, y1, yn1, stats1 = ssd_fwd(
        proj1, *consts[1][1:], dyn1, dims, seq_size, head_size, full
    )
    (h1_rows,) = head_fwd(flat(yn1), w_out2[1], h0, head_size, [])

    g_in1, gate1, conv1, small1, layer_outputs = ssd_bwd(
        dyn1, y1, proj1, halo1, cx1, dt1, cum1, state1, stats1, *consts[1][1:], [h1_rows, h0],
        dims, seq_size, head_size, full,
    )
    g_in1 = flat(g_in1)
    du1, du1_rows, gain1, dyn0, body1 = head_bwd(
        g_in1, w_in2[1], cot, h0, consts[1][0], w_out2[0], normed1, flat(yn1), head_size
    )
    done = lax.psum(body1, "seq")
    tail1, few1 = grad_tail(normed1, g_in1, conv1, small1, gate1, gain1, dims, head_size)
    g_in0, gate0, conv0, small0 = ssd_bwd(
        stacked(dyn0), y0, proj0, halo0, cx0, dt0, cum0, state0, stats0, *consts[0][1:], [],
        dims, seq_size, head_size, full,
    )
    g_in0 = flat(g_in0)
    tail0, few0 = grad_tail(normed0, g_in0, conv0, small0, gate0, jnp.zeros_like(gain1), dims, head_size)
    grads, shared, few, traded, input_grads = grad_sum(
        (g_in0, w_in2[0], du1_rows, u, consts[0][0], normed0, flat(yn0), du1),
        (tail0, tail1), (few0, few1), done, seq_size, head_size,
    )
    g_z, g_x, g_out, g_bc, g_dt, g_conv, g_conv_bias, g_bc_conv, g_bc_bias, *scalars, g_gate, g_gain = unpack(
        grads, traded, done, shared, few, dims
    )

    return (
        layer_outputs.reshape(1, micro, n, d_model),
        input_grads.reshape(1, micro, n, d_model),
        g_gain,
        g_z[None],
        g_x[None],
        g_bc[None],
        g_dt[None],
        g_conv[None],
        g_conv_bias,
        g_bc_conv[None],
        g_bc_bias,
        *scalars,
        g_gate,
        g_out[None],
    )


def solution(mesh):
    in_specs = (
        P(None, "seq", None),
        P(None, "seq", None),
        P("section", None),
        P("section", None, "head"),
        P("section", None, "head"),
        P("section", None, None),
        P("section", None, "head"),
        P("section", None, "head"),
        P("section", "head"),
        P("section", None, None),
        P("section", None),
        P("section", "head"),
        P("section", "head"),
        P("section", "head"),
        P("section", "head"),
        P("section", "head", None),
    )
    out_specs = (
        P("section", None, "seq", None),
        P("section", None, "seq", None),
        P("section", None),
        P("section", None, "head"),
        P("section", None, "head"),
        P("section", None, None),
        P("section", None, "head"),
        P("section", None, "head"),
        P("section", "head"),
        P("section", None, None),
        P("section", None),
        P("section", "head"),
        P("section", "head"),
        P("section", "head"),
        P("section", "head"),
        P("section", "head", None),
    )
    return jax.shard_map(
        on_device, mesh=mesh, in_specs=in_specs, out_specs=out_specs, check_vma=False
    )
```

```python
import functools

import jax
import jax.numpy as jnp
from jax import lax
from jax.experimental import pallas as pl
from jax.experimental.pallas import tpu as pltpu
from jax.sharding import PartitionSpec as P

EPSILON = 1e-05
MESH = pl.DeviceIdType.MESH
HIGH = lax.Precision.HIGHEST
BF = jnp.bfloat16
F32 = jnp.float32
LANES = 128
VMEM_LIMIT = 56 * 2**20


def shape(dims, kind):
    return jax.ShapeDtypeStruct(dims, kind)


def dot(a, b, dims=((1,), (0,)), precision=None):
    return lax.dot_general(a, b, (dims, ((), ())), precision=precision, preferred_element_type=F32)


NT = ((1,), (1,))
TN = ((0,), (0,))


def halves(v):
    high = v.astype(BF)
    return high, (v - high.astype(F32)).astype(BF)


def dot_mask(v, mask, dims=((1,), (0,))):
    high, rest = halves(v)
    return dot(high, mask, dims) + dot(rest, mask, dims)


def dot3(a, b, dims=((1,), (0,))):
    a_high, a_rest = halves(a)
    b_high, b_rest = halves(b)
    return dot(a_high, b_high, dims) + dot(a_rest, b_high, dims) + dot(a_high, b_rest, dims)


def mask_dot(mask, v):
    high, rest = halves(v)
    return dot(mask, high) + dot(mask, rest)


def head_mask(width, heads):
    size = width // heads
    return (
        lax.broadcasted_iota(jnp.int32, (LANES, width), 0)
        == lax.broadcasted_iota(jnp.int32, (LANES, width), 1) // size
    ).astype(F32).astype(BF)


def order_mask(n, lower):
    rows = lax.broadcasted_iota(jnp.int32, (n, n), 0)
    columns = lax.broadcasted_iota(jnp.int32, (n, n), 1)
    return (rows >= columns) if lower else (rows <= columns)


def sigmoid(v):
    return 1.0 / (1.0 + jnp.exp(-v))


def softplus(v):
    return jnp.maximum(v, 0.0) + jnp.log1p(jnp.exp(-jnp.abs(v)))


def column(row_block):
    n = row_block.shape[1]
    return [
        jnp.transpose(jnp.broadcast_to(row_block[i : i + 1, :], (LANES, n))) for i in range(2)
    ]


def rows_of(columns):
    n = columns[0].shape[0]
    rows = [jnp.transpose(jnp.broadcast_to(c, (n, LANES)))[0:1] for c in columns]
    return jnp.concatenate(rows + [jnp.zeros((8 - len(rows), n), F32)], axis=0)


def conv_pre(ext, proj_xbc, halo, taps, bias):
    n = proj_xbc.shape[0]
    ext[0:8, :] = halo
    ext[8 : 8 + n, :] = proj_xbc
    pre = bias + taps[3:4, :] * proj_xbc
    for k in range(3):
        pre = pre + taps[k : k + 1, :] * ext[5 + k : 5 + k + n, :]
    return pre


def push(src, dst, send, recv, device):
    copy = pltpu.make_async_remote_copy(
        src_ref=src, dst_ref=dst, send_sem=send, recv_sem=recv, device_id=device, device_id_type=MESH
    )
    copy.start()
    return copy


def both_layers_kernel(places, *refs):
    count = len(places)
    groups = places[-1][0] + 1
    ins, outs = refs[:count], refs[count:-3]
    send, recv, local = refs[-3:]
    me = lax.axis_index("section")
    other = {"section": 1 - me}
    barrier = pltpu.get_barrier_semaphore()
    pl.semaphore_signal(barrier, inc=1, device_id=other, device_id_type=MESH)
    pl.semaphore_wait(barrier, 1)

    def copies(i, which, start, layer):
        target = outs[layer * groups + which].at[:, pl.ds(start, ins[i].shape[1])]
        return (
            pltpu.make_async_remote_copy(
                src_ref=ins[i], dst_ref=target, send_sem=send.at[i], recv_sem=recv.at[i],
                device_id=other, device_id_type=MESH,
            ),
            pltpu.make_async_copy(ins[i], target, local.at[i]),
        )

    for layer in range(2):

        @pl.when(me == layer)
        def _():
            for i, (which, start) in enumerate(places):
                for copy in copies(i, which, start, layer):
                    copy.start()

    for i, (which, start) in enumerate(places):
        for copy in copies(i, which, start, 0):
            copy.wait()


def both_layers(groups):
    places, flat, outs = [], [], []
    for i, group in enumerate(groups):
        start = 0
        for a in group:
            places.append((i, start))
            flat.append(a)
            start += a.shape[1]
        outs.append(shape((group[0].shape[0], start), group[0].dtype))
    count = len(flat)
    vm = pl.BlockSpec(memory_space=pltpu.VMEM)
    anywhere = pl.BlockSpec(memory_space=pl.ANY)
    return pl.pallas_call(
        functools.partial(both_layers_kernel, places),
        out_shape=tuple(outs) * 2,
        in_specs=[vm] * count,
        out_specs=(anywhere,) * (2 * len(outs)),
        scratch_shapes=[pltpu.SemaphoreType.DMA((count,)) for _ in range(3)],
        compiler_params=pltpu.CompilerParams(
            collective_id=0, has_side_effects=True, vmem_limit_bytes=VMEM_LIMIT
        ),
        name="both_layers",
    )(*flat)


def constants(block, dims):
    heads, inner, states = dims
    wide = inner + 2 * states
    return (
        block.at[0:4, 0:wide],
        block.at[4:5, 0:wide],
        block.at[2:3, wide : wide + LANES],
        block.at[2:3, wide + LANES : wide + 2 * LANES],
        block.at[0:1, wide : wide + inner],
        block.at[1:2, wide : wide + inner],
    )


def norm_gain_of(block, d_model):
    return block.at[0:1, block.shape[1] - d_model :]


class Line:
    def __init__(self, forward, size, parts, outgoing, incoming, send, recv):
        self.me = lax.axis_index("seq")
        self.size, self.parts = size, parts
        self.outgoing, self.incoming, self.send, self.recv = outgoing, incoming, send, recv
        first, last = self.me == 0, self.me == size - 1
        self.starts, self.ends = (first, last) if forward else (last, first)
        self.place = self.me if forward else size - 1 - self.me
        step = 1 if forward else -1
        self.target, self.source = {"seq": self.me + step}, {"seq": self.me - step}

    def greet(self, barrier):
        @pl.when(jnp.logical_not(self.starts))
        def _():
            pl.semaphore_signal(barrier, inc=1, device_id=self.source, device_id_type=MESH)

    def met(self, barrier, others=0):
        @pl.when(jnp.logical_not(self.ends))
        def _():
            pl.semaphore_wait(barrier, others + 1)

        if others:

            @pl.when(self.ends)
            def _():
                pl.semaphore_wait(barrier, others)

    def copy(self, m, p):
        width = self.outgoing.shape[2] // self.parts
        at = pl.ds(p * width, width)
        return pltpu.make_async_remote_copy(
            src_ref=self.outgoing.at[m, :, at],
            dst_ref=self.incoming.at[m, :, at],
            send_sem=self.send.at[m * self.parts + p],
            recv_sem=self.recv.at[m * self.parts + p],
            device_id=self.target,
            device_id_type=MESH,
        )

    def begin(self, m, own):
        @pl.when(self.starts)
        def _():
            self.incoming[m] = jnp.zeros_like(self.incoming[m])
            self.outgoing[m] = own.astype(self.outgoing.dtype)
            for p in range(self.parts):
                self.copy(m, p).start()

    def relay(self, own, decay, at_step, steps, lag, apart):
        width = self.outgoing.shape[2] // self.parts
        for i in range(self.outgoing.shape[0] * self.parts):
            m, p = i // self.parts, i % self.parts
            at = slice(p * width, (p + 1) * width)
            due = jnp.minimum(self.place * lag + apart * i, steps - 1)

            @pl.when(jnp.logical_and(self.place > 0, due == at_step))
            def _():
                self.copy(m, p).wait_recv()

                @pl.when(jnp.logical_not(self.ends))
                def _():
                    passed = decay[m, 0:1, at] * self.incoming[m, :, at].astype(F32) + own[m, :, at]
                    self.outgoing[m, :, at] = passed.astype(self.outgoing.dtype)
                    self.copy(m, p).start()

    def finish(self):
        @pl.when(jnp.logical_not(self.ends))
        def _():
            for m in range(self.outgoing.shape[0]):
                for p in range(self.parts):
                    self.copy(m, p).wait_send()

    def halo(self, src, dst, m, send, recv):
        return pltpu.make_async_remote_copy(
            src_ref=src, dst_ref=dst, send_sem=send.at[m], recv_sem=recv.at[m],
            device_id=self.target, device_id_type=MESH,
        )


PARTS = 3


def ssd_fwd_kernel(dims, size, heads_axis, full, has_dyn, *refs):
    proj, block = refs[:2]
    taps, bias, dt_bias, a_neg, skip, gain = constants(block, dims)
    dyn = refs[2] if has_dyn else None
    (cx, dt_o, cum_o, state, halo, y_o, yn_o, stats_o,
     ext, own, decay, rim, outgoing, incoming, gates, square, square_got,
     send, recv, halo_send, halo_recv, stat_send, stat_recv) = refs[2 + has_dyn :]
    heads, inner, states = dims
    batch, n = proj.shape[0], proj.shape[1]
    wide = inner + 2 * states
    head_lanes = inner // heads
    columns = slice(inner, inner + wide)
    line = Line(True, size, PARTS, outgoing, incoming, send, recv)
    head = lax.axis_index("head")
    peers = [{"head": lax.rem(head + d, heads_axis)} for d in range(1, heads_axis)]
    barrier = pltpu.get_barrier_semaphore()
    line.greet(barrier)
    for peer in peers:
        pl.semaphore_signal(barrier, inc=1, device_id=peer, device_id_type=MESH)
    for m in range(batch):
        rim[m] = proj[m, n - 16 :, columns].astype(BF)
    line.met(barrier, len(peers))

    @pl.when(jnp.logical_not(line.ends))
    def _():
        for m in range(batch):
            line.halo(rim.at[m], halo.at[m], m, halo_send, halo_recv).start()

    @pl.when(line.starts)
    def _():
        halo[...] = jnp.zeros_like(halo)

    expand = head_mask(inner, heads)
    for m in range(batch):

        @pl.when(jnp.logical_not(line.starts))
        def _():
            line.halo(rim.at[m], halo.at[m], m, halo_send, halo_recv).wait_recv()

        xbc = proj[m, :, columns].astype(BF).astype(F32)
        pre = conv_pre(ext, xbc, halo[m, 8:].astype(F32), taps[...], bias[...])
        act = pre * sigmoid(pre)
        cx[m] = act
        dt = softplus(proj[m, :, inner + wide :] + dt_bias[...])
        cum = mask_dot(order_mask(n, True).astype(F32).astype(BF), dt * a_neg[...])
        dt_o[m] = dt
        cum_o[m] = cum
        last = cum[n - 1 : n, :]
        weight = dot_mask(jnp.exp(last - cum) * dt, expand)
        mine = dot3(act[:, inner : inner + states], act[:, :inner] * weight, TN)
        own[m] = mine
        decay[m] = dot_mask(jnp.broadcast_to(jnp.exp(last), (8, LANES)), expand)
        line.begin(m, mine)
    keep = order_mask(n, True)
    first = lax.broadcasted_iota(jnp.int32, (n, LANES), 1) < head_lanes
    pairs = heads // 2
    for m in range(batch):
        scores = dot3(cx[m, :, inner + states :], cx[m, :, inner : inner + states], NT)
        cums = cum_o[m]
        cums_t = jnp.transpose(cums)
        dt_wide = dot_mask(dt_o[m], expand)
        for p in range(pairs):

            line.relay(own, decay, m * pairs + p, batch * pairs, 4, 2)
            lanes = slice(p * LANES, (p + 1) * LANES)
            x = cx[m, :, lanes]
            dtx, dtx_rest = halves(x * dt_wide[:, lanes])
            both = []
            for h in (2 * p, 2 * p + 1):
                sums = []
                for low, high in ((0, n // 2), (n // 2, n)):
                    lag = cums[low:high, h : h + 1] - cums_t[h : h + 1, 0:high]
                    lag = jnp.where(keep[low:high, 0:high], lag, -1e30)
                    top, rest = halves(scores[low:high, 0:high] * jnp.exp(lag))
                    sums.append(dot(top, dtx[0:high]) + dot(rest, dtx[0:high]) + dot(top, dtx_rest[0:high]))
                both.append(jnp.concatenate(sums, axis=0))
            y_o[m, :, lanes] = skip[:, lanes] * x + jnp.where(first, both[0], both[1])
    for m in range(batch):
        entered = incoming[m]
        state[m] = entered
        y = y_o[m] + dot_mask(jnp.exp(cum_o[m]), expand) * dot3(cx[m, :, inner + states :], entered)
        y_o[m] = y
        z = proj[m, :, :inner]
        gated = y * z * sigmoid(z)
        gates[m] = gated
        stats = [jnp.sum(gated * gated, axis=1, keepdims=True)]
        if has_dyn:
            stats.append(jnp.sum(gated * gain[...] * dyn[m], axis=1, keepdims=True))
        square[m] = rows_of(stats)
    copies = [
        push(square, square_got.at[d], stat_send.at[d], stat_recv.at[d], peer) for d, peer in enumerate(peers)
    ]
    for copy in copies:
        copy.wait()
    for m in range(batch):
        total = square[m]
        for d in range(heads_axis - 1):
            total = total + square_got[d, m]
        gs = lax.rsqrt(total[0:1] / full + EPSILON)
        stats_o[m] = jnp.concatenate([gs, total[1:]], axis=0)
        yn_o[m] = (gates[m] * column(stats_o[m])[0][:, 0:1] * gain[...]).astype(BF)
    line.finish()

    @pl.when(jnp.logical_not(line.ends))
    def _():
        for m in range(batch):
            line.halo(rim.at[m], halo.at[m], m, halo_send, halo_recv).wait_send()


def ssd_fwd(proj, block, dyn, dims, size, heads_axis, full):
    heads, inner, states = dims
    batch, n, _ = proj.shape
    wide = inner + 2 * states
    vm = pl.BlockSpec(memory_space=pltpu.VMEM)
    has_dyn = dyn is not None
    moved = (batch, states, inner)
    outs = (
        shape((batch, n, wide), F32),
        shape((batch, n, LANES), F32),
        shape((batch, n, LANES), F32),
        shape(moved, F32),
        shape((batch, 16, wide), BF),
        shape((batch, n, inner), F32),
        shape((batch, n, inner), BF),
        shape((batch, 8, n), F32),
    )
    return pl.pallas_call(
        functools.partial(ssd_fwd_kernel, dims, size, heads_axis, full, has_dyn),
        out_shape=outs,
        in_specs=[vm] * (2 + has_dyn),
        out_specs=(vm,) * len(outs),
        scratch_shapes=[
            pltpu.VMEM((n + 8, wide), F32),
            pltpu.VMEM(moved, F32),
            pltpu.VMEM((batch, 8, inner), F32),
            pltpu.VMEM((batch, 16, wide), BF),
            pltpu.VMEM(moved, F32),
            pltpu.VMEM(moved, F32),
            pltpu.VMEM((batch, n, inner), F32),
            pltpu.VMEM((batch, 8, n), F32),
            pltpu.VMEM((heads_axis - 1, batch, 8, n), F32),
            pltpu.SemaphoreType.DMA((batch * PARTS,)),
            pltpu.SemaphoreType.DMA((batch * PARTS,)),
            pltpu.SemaphoreType.DMA((batch,)),
            pltpu.SemaphoreType.DMA((batch,)),
            pltpu.SemaphoreType.DMA((heads_axis - 1,)),
            pltpu.SemaphoreType.DMA((heads_axis - 1,)),
        ],
        compiler_params=pltpu.CompilerParams(
            collective_id=1 + has_dyn, has_side_effects=True, vmem_limit_bytes=VMEM_LIMIT
        ),
        name="ssd_fwd",
    )(proj, block, *([dyn] if has_dyn else []))


def ssd_bwd_kernel(
    dims, size, heads_axis, full, has_across,
    dyn, y, proj, halo, cx, dt, cum, state, stats, block, *refs
):
    taps, bias, dt_bias, a_neg, skip, gain = constants(block, dims)
    if has_across:
        h_rows, h_whole, h_o, *refs = refs[:2] + refs[6:7] + refs[2:6] + refs[7:]
        *refs, c_local, c_send, c_recv = refs
    (
    g_in, gate_o, conv_o, small_o,
    dy, dxw, dpre, own, decay, ext, rowq, colq, d_scores, outgoing, incoming, rim, square, square_got,
    send, recv, rim_send, rim_recv, stat_send, stat_recv,
    ) = refs
    heads, inner, states = dims
    batch, n = dyn.shape[0], dyn.shape[1]
    wide = inner + 2 * states
    columns = slice(inner, inner + wide)
    size_p = inner // heads
    pairs = heads // 2
    line = Line(False, size, PARTS, outgoing, incoming, send, recv)
    head = lax.axis_index("head")
    peers = [{"head": lax.rem(head + d, heads_axis)} for d in range(1, heads_axis)]
    barrier = pltpu.get_barrier_semaphore()
    line.greet(barrier)
    if has_across:
        outputs = Collect(1, heads_axis, h_rows, h_whole, h_o, c_local, c_send, c_recv)
        peers = outputs.greeted()
    for peer in peers:
        pl.semaphore_signal(barrier, inc=1, device_id=peer, device_id_type=MESH)
    if not has_across:
        for m in range(batch):
            z = proj[m, :, :inner]
            square[m] = rows_of([jnp.sum(dyn[m] * gain[...] * y[m] * z * sigmoid(z), axis=1, keepdims=True)])
    line.met(barrier, len(peers))
    if has_across:
        outputs.start()
    else:
        copies = [
            push(square, square_got.at[d], stat_send.at[d], stat_recv.at[d], peers[d])
            for d in range(heads_axis - 1)
        ]
    expand = head_mask(inner, heads)
    if not has_across:
        for copy in copies:
            copy.wait()
    for m in range(batch):
        gs, across = [v[:, 0:1] for v in column(stats[m])]
        if has_across:
            pass
        else:
            total = square[m]
            for d in range(heads_axis - 1):
                total = total + square_got[d, m]
            across = column(total)[0][:, 0:1]
        z = proj[m, :, :inner]
        sig = sigmoid(z)
        yv = y[m]
        gated = yv * z * sig
        dynv = dyn[m]
        scaled = gated * gs
        gate_o[m] = jnp.broadcast_to(jnp.sum(dynv * scaled, axis=0, keepdims=True), (8, inner))
        dgated = gs * gain[...] * dynv - gated * (gs * gs * gs * across / full)
        dyv = dgated * z * sig
        dy[m] = dyv
        g_in[m, :, :inner] = (dgated * yv * sig * (1.0 + z * (1.0 - sig))).astype(BF)
        cums = cum[m]
        moved = dot_mask(jnp.exp(cums), expand) * dyv
        mine = dot3(cx[m, :, inner + states :], moved, TN)
        own[m] = mine
        decay[m] = dot_mask(jnp.broadcast_to(jnp.exp(cums[n - 1 : n, :]), (8, LANES)), expand)
        line.begin(m, mine)
    keep = order_mask(n, False)
    lane = lax.broadcasted_iota(jnp.int32, (n, LANES), 1)
    first = lane < size_p
    rowq[...] = jnp.zeros_like(rowq)
    for m in range(batch):
        scores_t = dot3(cx[m, :, inner : inner + states], cx[m, :, inner + states :], NT)
        cums = cum[m]
        cums_t = jnp.transpose(cums)
        dt_wide = dot_mask(dt[m], expand)
        colq[m] = jnp.zeros_like(colq[m])
        d_scores[m] = jnp.zeros_like(d_scores[m])
        for p in range(pairs):

            line.relay(own, decay, m * pairs + p, batch * pairs, 2, 1)
            lanes = slice(p * LANES, (p + 1) * LANES)
            dtx, dtx_rest = halves(cx[m, :, lanes] * dt_wide[:, lanes])
            dyb, dy_rest = halves(dy[m, :, lanes])
            both, gathered = [], [0.0, 0.0]
            for j, h in enumerate((2 * p, 2 * p + 1)):
                side = first if j == 0 else jnp.logical_not(first)
                mine, mine_rest = [jnp.where(side, v, jnp.zeros((), BF)) for v in (dtx, dtx_rest)]
                sums, row_sums, column_sums = [], [], []
                for i, (low, high) in enumerate(((0, n // 2), (n // 2, n))):
                    lag = jnp.where(
                        keep[low:high, low:n], cums_t[h : h + 1, low:n] - cums[low:high, h : h + 1], -1e30
                    )
                    decays = jnp.exp(lag)
                    weights = scores_t[low:high, low:n] * decays
                    d_weights = (
                        dot(mine[low:high], dyb[low:n], NT)
                        + dot(mine[low:high], dy_rest[low:n], NT)
                        + dot(mine_rest[low:high], dyb[low:n], NT)
                    )
                    q = d_weights * weights
                    gathered[i] = gathered[i] + d_weights * decays
                    row_sums.append(jnp.sum(q, axis=0, keepdims=True))
                    column_sums.append(jnp.sum(q, axis=1, keepdims=True))
                    sums.append(dot(weights.astype(BF), dyb[low:n]))
                rowq[m, h : h + 1, :] = row_sums[0]
                rowq[m, h : h + 1, n // 2 :] += row_sums[1]
                colq[m] += jnp.where(lane == h, jnp.concatenate(column_sums, axis=0), 0.0)
                both.append(jnp.concatenate(sums, axis=0))
            d_scores[m, 0 : n // 2, :] += gathered[0]
            d_scores[m, n // 2 :, n // 2 :] += gathered[1]
            dxw[m, :, lanes] = jnp.where(first, both[0], both[1])
    fold = lambda v: dot_mask(v, expand, NT)
    for m in range(batch):
        x = cx[m, :, :inner]
        b = cx[m, :, inner : inner + states]
        c = cx[m, :, inner + states :]
        b_high, b_rest = halves(b)
        dyv, dxv, dtv, cums = dy[m], dxw[m], dt[m], cum[m]
        last = cums[n - 1 : n, :]
        entered, later_b = state[m], incoming[m]
        moved = dot_mask(jnp.exp(cums), expand) * dyv
        carried = dot3(c, entered)
        tail = jnp.exp(last - cums)
        weight = tail * dtv
        weight_wide = dot_mask(weight, expand)
        pulled = dot(b_high, later_b) + dot(b_rest, later_b)
        dx = dot_mask(dtv, expand) * dxv + weight_wide * pulled + skip[...] * dyv
        dw = fold(x * pulled)
        wdw = weight * dw
        change = jnp.transpose(rowq[m]) + fold(carried * moved) - colq[m] - wdw
        ends = jnp.sum(entered * later_b.astype(F32), axis=0, keepdims=True)
        ends = jnp.sum(wdw, axis=0, keepdims=True) + jnp.exp(last) * fold(jnp.broadcast_to(ends, (8, inner)))[0:1]
        log_grad = mask_dot(order_mask(n, False).astype(F32).astype(BF), change) + ends
        ddt = fold(x * dxv) + tail * dw + a_neg[...] * log_grad
        ddt_raw = ddt * sigmoid(proj[m, :, inner + wide :] + dt_bias[...])
        g_in[m, :, inner + wide :] = ddt_raw.astype(BF)
        small_o[m] = jnp.concatenate(
            [
                jnp.sum(ddt_raw, axis=0, keepdims=True),
                jnp.sum(dtv * log_grad, axis=0, keepdims=True) * a_neg[...],
                fold(jnp.broadcast_to(jnp.sum(x * dyv, axis=0, keepdims=True), (8, inner)))[0:1],
                jnp.zeros((5, LANES), F32),
            ],
            axis=0,
        )
        xw_high, xw_rest = halves(x * weight_wide)
        dc = dot3(d_scores[m], b, TN) + dot3(moved, entered, NT)
        db = dot3(d_scores[m], c) + dot(xw_high, later_b, NT) + dot(xw_rest, later_b, NT)
        xbc = proj[m, :, columns].astype(BF).astype(F32)
        pre = conv_pre(ext, xbc, halo[m, 8:].astype(F32), taps[...], bias[...])
        sig = sigmoid(pre)
        d_act = jnp.concatenate([dx, db, dc], axis=1) * sig * (1.0 + pre * (1.0 - sig))
        dpre[m, 0:n, :] = d_act
        rim_copy = line.halo(dpre.at[m, pl.ds(0, 8)], rim.at[m], m, rim_send, rim_recv)
        pl.when(jnp.logical_not(line.ends))(rim_copy.start)
        rows = [jnp.sum(d_act * ext[5 + k : 5 + k + n, :], axis=0, keepdims=True) for k in range(4)]
        rows.append(jnp.sum(d_act, axis=0, keepdims=True))
        conv_o[m] = jnp.concatenate(rows + [jnp.zeros((3, wide), F32)], axis=0)

    @pl.when(line.starts)
    def _():
        rim[...] = jnp.zeros_like(rim)

    for m in range(batch):
        rim_copy = line.halo(dpre.at[m, pl.ds(0, 8)], rim.at[m], m, rim_send, rim_recv)
        pl.when(jnp.logical_not(line.starts))(rim_copy.wait_recv)
        dpre[m, n : n + 8, :] = rim[m]
        total = taps[3:4, :] * dpre[m, 0:n, :]
        for k in range(3):
            total = total + taps[k : k + 1, :] * dpre[m, 3 - k : 3 - k + n, :]
        g_in[m, :, columns] = total.astype(BF)
        pl.when(jnp.logical_not(line.ends))(rim_copy.wait_send)
    line.finish()
    if has_across:
        outputs.finish()


def ssd_bwd(dyn, y, proj, halo, cx, dt, cum, state, stats, block, outputs,
            dims, size, heads_axis, full):
    has_across = bool(outputs)
    heads, inner, states = dims
    batch, n, wide = cx.shape
    vm = pl.BlockSpec(memory_space=pltpu.VMEM)
    moved = (batch, states, inner)
    outs = (
        shape((batch, n, inner + wide + LANES), BF),
        shape((batch, 8, inner), F32),
        shape((batch, 8, wide), F32),
        shape((batch, 8, LANES), F32),
    ) + tuple(shape((2 * a.shape[0], a.shape[1]), BF) for a in outputs[1:])
    sems = lambda k: pltpu.SemaphoreType.DMA((k,))
    return pl.pallas_call(
        functools.partial(ssd_bwd_kernel, dims, size, heads_axis, full, has_across),
        out_shape=outs,
        in_specs=[vm] * (10 + len(outputs)),
        out_specs=(vm,) * 4 + (pl.BlockSpec(memory_space=pl.ANY),) * has_across,
        scratch_shapes=[
            pltpu.VMEM((batch, n, inner), F32),
            pltpu.VMEM((batch, n, inner), F32),
            pltpu.VMEM((batch, n + 8, wide), F32),
            pltpu.VMEM(moved, F32),
            pltpu.VMEM((batch, 8, inner), F32),
            pltpu.VMEM((n + 8, wide), F32),
            pltpu.VMEM((batch, LANES, n), F32),
            pltpu.VMEM((batch, n, LANES), F32),
            pltpu.VMEM((batch, n, n), F32),
            pltpu.VMEM(moved, BF),
            pltpu.VMEM(moved, BF),
            pltpu.VMEM((batch, 8, wide), F32),
            pltpu.VMEM((batch, 8, n), F32),
            pltpu.VMEM((heads_axis - 1, batch, 8, n), F32),
            sems(batch * PARTS),
            sems(batch * PARTS),
            sems(batch),
            sems(batch),
            sems(heads_axis - 1),
            sems(heads_axis - 1),
        ]
        + (collect_sems(heads_axis) if has_across else []),
        compiler_params=pltpu.CompilerParams(
            collective_id=10 + has_across, has_side_effects=True, vmem_limit_bytes=VMEM_LIMIT
        ),
        name="ssd_bwd",
    )(dyn, y, proj, halo, cx, dt, cum, state, stats, block, *outputs)


def greet(size, core=False):
    me = lax.axis_index("head")
    barrier = pltpu.get_barrier_semaphore()
    peers = [{"head": lax.rem(me + d, size)} for d in range(1, size)]
    others = [{"section": 1 - lax.axis_index("section")}] if core else []
    for peer in peers + others:
        pl.semaphore_signal(barrier, inc=1, device_id=peer, device_id_type=MESH)
    pl.semaphore_wait(barrier, len(peers) + len(others))
    return me, peers


def block_of(index, rows):
    return pl.ds(pl.multiple_of(index * rows, rows), rows)


def normal(u, gain):
    uv = u.astype(F32)
    s = lax.rsqrt(jnp.sum(uv * uv, axis=1, keepdims=True) / uv.shape[1] + EPSILON)
    return (uv * s * gain).astype(BF)


def head_fwd_kernel(size, onward, yn, w_out, u, *refs):
    if onward:
        w_in, block, h_o, normed_o, proj_o, out, got, send, recv = refs
        gain = norm_gain_of(block, u.shape[1])
    else:
        go, h_o, body_o, out, got, body_send, body_got, send, recv, body_ss, body_rs = refs
    rows = yn.shape[0] // size
    me, peers = greet(size, core=not onward)
    copies = []
    for d, peer in enumerate(peers):
        to = lax.rem(me + d + 1, size)
        out[d] = dot(yn[block_of(to, rows), :], w_out[...]).astype(out.dtype)
        copies.append(push(out.at[d], got.at[d], send.at[0, d], recv.at[0, d], peer))
    mine = block_of(me, rows)
    total = dot(yn[mine, :], w_out[...])
    if not onward:
        body = body_halves(lambda which, i: body_tile(None, None, yn, go, which, i), body_o, body_send, body_got, body_ss, body_rs)
    for copy in copies:
        copy.wait()
    for d in range(size - 1):
        total = total + got[d].astype(F32)
    h = (u[mine, :].astype(F32) + total).astype(BF)
    if not onward:
        h_o[...] = h
        add_halves(body, body_o, body_got)
        return
    h_o[mine, :] = h
    copies = [
        push(h_o.at[mine], h_o.at[mine], send.at[1, d], recv.at[1, d], peer) for d, peer in enumerate(peers)
    ]

    def project(at):
        normed = normal(h_o[at, :], gain[...])
        normed_o[at, :] = normed
        proj_o[at, :] = dot(normed, w_in[...])

    project(mine)
    for d, copy in enumerate(copies):
        copy.wait_recv()
        project(block_of(lax.rem(me + size - d - 1, size), rows))
    for copy in copies:
        copy.wait_send()


def head_fwd(yn, w_out, u, size, onward, go=None):
    n, d_model = u.shape
    body = (yn.shape[1], d_model // 2)
    tiles = body[0] // 256
    rows = n // size
    vm = pl.BlockSpec(memory_space=pltpu.VMEM)
    kind = F32 if onward else BF
    outs = [shape((n if onward else rows, d_model), BF)]
    if onward:
        outs += [shape((n, d_model), BF), shape((n, onward[0].shape[1]), F32)]
    else:
        outs += [shape(body, BF)]
        onward = [go]
    more = go is not None
    return pl.pallas_call(
        functools.partial(head_fwd_kernel, size, not more),
        out_shape=tuple(outs),
        in_specs=[vm] * (3 + len(onward)),
        out_specs=(vm,) * len(outs),
        scratch_shapes=[
            pltpu.VMEM((size - 1, rows, d_model), kind),
            pltpu.VMEM((size - 1, rows, d_model), kind),
        ]
        + [pltpu.VMEM(body, BF)] * (2 * more)
        + [pltpu.SemaphoreType.DMA((2, size - 1))] * 2
        + [pltpu.SemaphoreType.DMA((tiles,))] * (2 * more),
        compiler_params=pltpu.CompilerParams(
            collective_id=6 if more else 3, has_side_effects=True, vmem_limit_bytes=VMEM_LIMIT
        ),
        name="head_fwd",
    )(yn, w_out, u, *onward)


def input_gradient(dn, u, gain, above):
    uv = u.astype(F32)
    width = uv.shape[1]
    s = lax.rsqrt(jnp.sum(uv * uv, axis=1, keepdims=True) / width + EPSILON)
    scaled = dn * gain
    inner = jnp.sum(scaled * uv, axis=1, keepdims=True)
    return (
        above.astype(F32) + s * scaled - uv * (s * s * s * inner / width),
        jnp.sum(dn * uv * s, axis=0, keepdims=True),
    )


def body_tile(normed, g_in, yn, go, half, i):
    left, right = (yn, go) if normed is None else (normed, g_in)
    wide = yn.shape[1]
    at = pl.ds(pl.multiple_of(half * wide, wide), wide)
    return dot(left[:, i * 256 : (i + 1) * 256], right[:, at], TN)


def body_halves(make, out, sent, got, send, recv):
    layer = lax.axis_index("section")
    copies = []
    for i in range(out.shape[0] // 256):
        at = pl.ds(i * 256, 256)
        sent[at, :] = make(1 - layer, i).astype(BF)
        copies.append(push(sent.at[at], got.at[at], send.at[i], recv.at[i], {"section": 1 - layer}))
    for i in range(out.shape[0] // 256):
        out[i * 256 : (i + 1) * 256, :] = make(layer, i).astype(BF)
    return copies


def add_halves(copies, out, got):
    for i, copy in enumerate(copies):
        at = slice(i * 256, (i + 1) * 256)
        copy.wait()
        out[at, :] = (out[at, :].astype(F32) + got[at, :].astype(F32)).astype(BF)


def head_bwd_kernel(size, g_in, w_in, upper, u, block, w_out, normed, yn, du_o, mine_o, grad_o, dyn_o, body_o,
                    out, got, body_send, body_got, send, recv, body_ss, body_rs):
    rows = u.shape[0] // size
    gain = norm_gain_of(block, u.shape[1])
    me, peers = greet(size, core=True)
    copies = []
    for d, peer in enumerate(peers):
        to = lax.rem(me + d + 1, size)
        out[d] = dot(g_in[block_of(to, rows), :], w_in[...], NT).astype(BF)
        copies.append(push(out.at[d], got.at[d], send.at[0, d], recv.at[0, d], peer))
    mine = block_of(me, rows)
    dn = dot(g_in[mine, :], w_in[...], NT)
    make = lambda which, i: body_tile(normed, g_in, yn, upper, which, i)
    body = body_halves(make, body_o, body_send, body_got, body_ss, body_rs)
    for copy in copies:
        copy.wait()
    for d in range(size - 1):
        dn = dn + got[d].astype(F32)
    du, grad = input_gradient(dn, u[mine, :], gain[...], upper[mine, :])
    grad_o[...] = jnp.broadcast_to(grad, grad_o.shape)
    mine_o[...] = du
    du_o[mine, :] = du.astype(BF)
    copies = [
        push(du_o.at[mine], du_o.at[mine], send.at[1, d], recv.at[1, d], peer) for d, peer in enumerate(peers)
    ]
    add_halves(body, body_o, body_got)
    dyn_o[mine, :] = dot(du_o[mine, :], w_out[...], NT)
    for d, copy in enumerate(copies):
        copy.wait_recv()
        at = block_of(lax.rem(me + size - d - 1, size), rows)
        dyn_o[at, :] = dot(du_o[at, :], w_out[...], NT)
    for copy in copies:
        copy.wait_send()


def head_bwd(g_in, w_in, upper, u, gain, w_out, normed, yn, size):
    n, d_model = u.shape
    inner = yn.shape[1]
    rows = n // size
    tiles = d_model // 256
    body = (d_model, d_model // 2)
    vm = pl.BlockSpec(memory_space=pltpu.VMEM)
    return pl.pallas_call(
        functools.partial(head_bwd_kernel, size),
        out_shape=(
            shape((n, d_model), BF),
            shape((rows, d_model), F32),
            shape((8, d_model), F32),
            shape((n, inner), F32),
            shape(body, BF),
        ),
        in_specs=[vm] * 8,
        out_specs=(vm,) * 5,
        scratch_shapes=[
            pltpu.VMEM((size - 1, rows, d_model), BF),
            pltpu.VMEM((size - 1, rows, d_model), BF),
            pltpu.VMEM(body, BF),
            pltpu.VMEM(body, BF),
            pltpu.SemaphoreType.DMA((2, size - 1)),
            pltpu.SemaphoreType.DMA((2, size - 1)),
            pltpu.SemaphoreType.DMA((tiles,)),
            pltpu.SemaphoreType.DMA((tiles,)),
        ],
        compiler_params=pltpu.CompilerParams(
            collective_id=5, has_side_effects=True, vmem_limit_bytes=VMEM_LIMIT
        ),
        name="head_bwd",
    )(g_in, w_in, upper, u, gain, w_out, normed, yn)


class Collect:
    def __init__(self, by_rows, size, rows, whole, out, local, send, recv):
        self.by_rows, self.size = by_rows, size
        self.rows, self.whole, self.out = rows, whole, out
        self.local, self.send, self.recv = local, send, recv
        self.core, self.head = lax.axis_index("section"), lax.axis_index("head")
        count = rows.shape[0]
        self.row_part = pl.ds(pl.multiple_of(self.core * whole.shape[0] + self.head * count, count), count)
        self.whole_part = block_of(self.core, whole.shape[0])

    def greeted(self):
        return [
            {"section": lax.rem(self.core + c, 2), "head": lax.rem(self.head + d, self.size)}
            for c in range(2)
            for d in range(self.size)
            if c or d
        ]

    def row_copy(self, sender, d):
        return pltpu.make_async_remote_copy(
            src_ref=self.rows, dst_ref=self.out.at[self.row_part],
            send_sem=self.send.at[d], recv_sem=self.recv.at[sender * self.size + d],
            device_id={"section": self.by_rows, "head": lax.rem(self.head + d, self.size)}, device_id_type=MESH,
        )

    def whole_copy(self):
        return pltpu.make_async_remote_copy(
            src_ref=self.whole, dst_ref=self.out.at[self.whole_part],
            send_sem=self.send.at[self.size], recv_sem=self.recv.at[2 * self.size],
            device_id={"section": 1 - self.by_rows}, device_id_type=MESH,
        )

    def start(self):
        @pl.when(self.core == self.by_rows)
        def _():
            pltpu.make_async_copy(self.rows, self.out.at[self.row_part], self.local).start()
            for d in range(1, self.size):
                self.row_copy(self.by_rows, d).start()
            self.whole_copy().start()

        @pl.when(self.core != self.by_rows)
        def _():
            pltpu.make_async_copy(self.whole, self.out.at[self.whole_part], self.local).start()
            for d in range(self.size):
                self.row_copy(1 - self.by_rows, d).start()

    def finish(self):
        @pl.when(self.core == self.by_rows)
        def _():
            pltpu.make_async_copy(self.rows, self.out.at[self.row_part], self.local).wait()
            for d in range(1, self.size):
                self.row_copy(self.by_rows, d).wait()
            for d in range(self.size):
                self.row_copy(1 - self.by_rows, d).wait_recv()
            self.whole_copy().wait_send()

        @pl.when(self.core != self.by_rows)
        def _():
            pltpu.make_async_copy(self.whole, self.out.at[self.whole_part], self.local).wait()
            for d in range(self.size):
                self.row_copy(1 - self.by_rows, d).wait_send()
            self.whole_copy().wait_recv()


def collect_sems(size):
    return [
        pltpu.SemaphoreType.DMA,
        pltpu.SemaphoreType.DMA((size + 1,)),
        pltpu.SemaphoreType.DMA((2 * size + 1,)),
    ]


OWN = 32
SHARED = 160
PIECE = 48
TAIL = (OWN + SHARED) // PIECE
LATE = 6
FEW = 16


def grad_tail_kernel(dims, normed, g_in, conv, scalars, gate, gain, tail, few):
    heads, inner, states = dims
    half = normed.shape[1] // 2
    split = 2 * inner + 2 * states
    rest = dot(g_in[:, 2 * inner :], normed[...], TN).astype(BF)
    step = (tail.shape[0] - OWN) // 2
    tail[...] = jnp.zeros_like(tail)
    for i in range(2):
        lanes = slice(i * half, (i + 1) * half)
        tail[i * OWN // 2 : (i + 1) * OWN // 2, :] = rest[2 * states : 2 * states + OWN // 2, lanes]
        tail[OWN + i * step : OWN + i * step + 2 * states, :] = rest[: 2 * states, lanes]
    conv_sum, scalar_sum, gate_sum = conv[0], scalars[0], gate[0]
    for i in range(1, conv.shape[0]):
        conv_sum, scalar_sum, gate_sum = conv_sum + conv[i], scalar_sum + scalars[i], gate_sum + gate[i]
    few[...] = jnp.zeros_like(few)
    few[0:5, :] = conv_sum[0:5, :inner]
    few[5:6, :] = gate_sum[0:1]
    for i in range(3):
        few[6:7, i * LANES : (i + 1) * LANES] = scalar_sum[i : i + 1]
    few[8:9, :] = gain[0:1, :half]
    few[9:10, :] = gain[0:1, half:]
    few[10:15, 0 : 2 * states] = conv_sum[0:5, inner:]


def grad_tail(normed, g_in, conv, scalars, gate, gain, dims, head_size):
    heads, inner, states = dims
    width = normed.shape[1]
    vm = pl.BlockSpec(memory_space=pltpu.VMEM)
    return pl.pallas_call(
        functools.partial(grad_tail_kernel, dims),
        out_shape=(shape((OWN + head_size * SHARED, width // 2), BF), shape((FEW, width // 2), F32)),
        in_specs=[vm] * 6,
        out_specs=(vm, vm),
        compiler_params=pltpu.CompilerParams(vmem_limit_bytes=VMEM_LIMIT),
        name="grad_tail",
    )(normed, g_in, conv, scalars, gate, gain)


def grad_sum_kernel(size, heads, skew, g_in, w_in, above, u, block, normed, yn, go, body1, tail0, tail1, few0, few1, done, done_out,
                    first_o, second_o, tail_o, shared_o, few_o, du_o,
                    own, core, got, out, shared, shared_core, shared_got, few_core, few_seq, few_head,
                    body_send, body_own, du_out, du_got, du_rows, few_mine,
                    cs, cr, rs, rr, bs, br, ts, tr, ls, hs, hr, xs, fs, fr, gs, gr, ds, dr, c_local, c_send, c_recv):
    me, layer, head = lax.axis_index("seq"), lax.axis_index("section"), lax.axis_index("head")
    half = out.shape[0] // 2
    parts = half // PIECE
    total0 = body_own.shape[0]
    early = done.shape[0]
    cut = (parts - LATE) * PIECE
    far = size - 1
    up, down, other = {"seq": me + 1}, {"seq": me - 1}, {"section": 1 - layer}
    peers = [{"head": lax.rem(head + d, heads)} for d in range(1, heads)]
    blocks = [{"seq": lax.rem(me + d, size)} for d in range(1, size)]
    low_end, high_end = me == 0, me == size - 1
    barrier = pltpu.get_barrier_semaphore()
    inputs = Collect(0, heads, du_rows, go, du_o, c_local, c_send, c_recv)
    plane = inputs.greeted()
    for peer in plane + blocks:
        pl.semaphore_signal(barrier, inc=1, device_id=peer, device_id_type=MESH)
    pl.semaphore_wait(barrier, len(plane) + len(blocks))

    late = [
        pltpu.make_async_copy(
            body1.at[pl.ds(early + side * LATE * PIECE, LATE * PIECE)],
            own.at[pl.ds(side * half, LATE * PIECE)],
            xs.at[7 + side],
        )
        for side in range(2)
    ]
    for copy in late:
        copy.start()

    ready = [(done, pl.ds(0, early)), (done_out, pl.ds(normed.shape[1], done_out.shape[0]))]
    given = [
        pltpu.make_async_remote_copy(
            src_ref=src, dst_ref=first_o.at[at], send_sem=xs.at[9 + i], recv_sem=xs.at[5 + i],
            device_id=other, device_id_type=MESH,
        )
        for i, (src, at) in enumerate(ready)
    ]
    kept = [pltpu.make_async_copy(src, second_o.at[at], xs.at[9 + i]) for i, (src, at) in enumerate(ready)]

    def all_of(copies, act):
        for copy in copies:
            act(copy)

    pl.when(layer == 0)(lambda: all_of(given, lambda copy: copy.start()))
    pl.when(layer == 1)(lambda: all_of(kept, lambda copy: copy.start()))

    def fetch_tail(ours, others):
        return (
            pltpu.make_async_copy(ours, shared, xs.at[0]),
            pltpu.make_async_remote_copy(
                src_ref=others, dst_ref=shared_core, send_sem=xs.at[1], recv_sem=xs.at[2],
                device_id=other, device_id_type=MESH,
            ),
        )

    def start_all(copies):
        for copy in copies:
            copy.start()

    pl.when(layer == 0)(lambda: start_all(fetch_tail(tail0, tail1)))
    pl.when(layer == 1)(lambda: start_all(fetch_tail(tail1, tail0)))

    rows_here = u.shape[0] // heads
    du_copy = lambda d: pltpu.make_async_remote_copy(
        src_ref=du_out.at[d], dst_ref=du_got.at[d], send_sem=ds.at[d], recv_sem=dr.at[d],
        device_id=peers[d], device_id_type=MESH,
    )

    def few_to_core(src):
        return pltpu.make_async_remote_copy(
            src_ref=src, dst_ref=few_core, send_sem=xs.at[3], recv_sem=xs.at[4],
            device_id=other, device_id_type=MESH,
        )

    few_to_seq = lambda d: pltpu.make_async_remote_copy(
        src_ref=few_seq.at[me], dst_ref=few_seq.at[me], send_sem=fs.at[d], recv_sem=fr.at[d],
        device_id=blocks[d], device_id_type=MESH,
    )
    few_to_head = lambda d: pltpu.make_async_remote_copy(
        src_ref=few_head.at[head], dst_ref=few_head.at[head], send_sem=gs.at[d], recv_sem=gr.at[d],
        device_id=peers[d], device_id_type=MESH,
    )
    shared_block = lambda i: pl.ds(pl.multiple_of(OWN + i * SHARED, 32), SHARED)
    scatter = lambda d: pltpu.make_async_remote_copy(
        src_ref=shared.at[shared_block(lax.rem(head + d + 1, heads))], dst_ref=shared_got.at[d],
        send_sem=hs.at[0, d], recv_sem=hr.at[0, d], device_id=peers[d], device_id_type=MESH,
    )
    gather = lambda d: pltpu.make_async_remote_copy(
        src_ref=shared_o.at[head], dst_ref=shared_o.at[head],
        send_sem=hs.at[1, d], recv_sem=hr.at[1, d], device_id=peers[d], device_id_type=MESH,
    )

    for copy in fetch_tail(tail0, tail1):
        copy.wait()
    shared[...] = (shared[...].astype(F32) + shared_core[...].astype(F32)).astype(BF)
    for d in range(heads - 1):
        scatter(d).start()
    for d in range(heads - 1):
        to = block_of(lax.rem(head + d + 1, heads), rows_here)
        du_out[d] = dot(g_in[to, :], w_in[...], NT).astype(BF)
        du_copy(d).start()

    tile = 256
    in_tiles = normed.shape[1] // tile
    tiles = total0 // tile

    def body_copy(i):
        at = block_of(i, tile)
        return pltpu.make_async_remote_copy(
            src_ref=body_send.at[at], dst_ref=core.at[at], send_sem=cs.at[i], recv_sem=cr.at[i],
            device_id=other, device_id_type=MESH,
        )

    def make_tile(i, left, right):
        at = block_of(i, tile)
        wide = yn.shape[1]
        for which, target in ((1 - layer, body_send), (layer, body_own)):
            columns = pl.ds(pl.multiple_of(which * wide, wide), wide)
            target[at, :] = dot(left, right[:, columns], TN).astype(BF)
        body_copy(i).start()

    place = lambda side, p: pl.ds(pl.multiple_of(side * half + p * PIECE, PIECE), PIECE)
    is_late = lambda p: p < LATE
    is_tail = lambda side, p: jnp.logical_and(side == 1, jnp.logical_and(p >= LATE, p < LATE + TAIL))
    start0 = lambda side, p: (p - LATE) * PIECE + (cut - TAIL * PIECE) * side
    start1 = lambda side, p: early + side * LATE * PIECE + p * PIECE

    def sending(side, p, back, source):
        at = place(side, p)
        towards = down if (side == 0) != back else up
        target, send, recv = (out, bs, br) if back else (got, rs, rr)
        return pltpu.make_async_remote_copy(
            src_ref=source.at[at], dst_ref=target.at[at], send_sem=send.at[side, p],
            recv_sem=recv.at[side, p], device_id=towards, device_id_type=MESH,
        )

    def give(side, p, target, at):
        return pltpu.make_async_remote_copy(
            src_ref=out.at[place(side, p)], dst_ref=target.at[at], send_sem=ts.at[side, p],
            recv_sem=tr.at[side, p], device_id=other, device_id_type=MESH,
        )

    def keep(side, p, target, at):
        return pltpu.make_async_copy(out.at[place(side, p)], target.at[at], ls.at[side, p])

    def final(side, p, act_keep, act_give):
        at0 = lambda: pl.ds(pl.multiple_of(start0(side, p), PIECE), PIECE)
        at1 = lambda: pl.ds(pl.multiple_of(start1(side, p), PIECE), PIECE)
        late_piece = is_late(p)
        body0 = jnp.logical_not(jnp.logical_or(late_piece, is_tail(side, p)))
        pl.when(jnp.logical_and(body0, layer == 0))(lambda: act_keep(keep(side, p, first_o, at0())))
        pl.when(jnp.logical_and(body0, layer == 1))(lambda: act_give(give(side, p, second_o, at0())))
        pl.when(jnp.logical_and(late_piece, layer == 0))(lambda: act_give(give(side, p, first_o, at1())))
        pl.when(jnp.logical_and(late_piece, layer == 1))(lambda: act_keep(keep(side, p, second_o, at1())))

    begin = lambda copy: copy.start()

    def reduce(side, p):
        start, end = (high_end, low_end) if side == 0 else (low_end, high_end)
        at = place(side, p)

        @pl.when(jnp.logical_not(jnp.logical_or(is_late(p), is_tail(side, p))))
        def _():
            mine = pl.ds(pl.multiple_of(start0(side, p), PIECE), PIECE)
            own[at, :] = (body_own[mine, :].astype(F32) + core[mine, :].astype(F32)).astype(BF)

        @pl.when(start)
        def _():
            sending(side, p, False, own).start()

        @pl.when(jnp.logical_not(start))
        def _():
            sending(side, p, False, got).wait_recv()
            summed = (own[at, :].astype(F32) + got[at, :].astype(F32)).astype(BF)

            @pl.when(end)
            def _():
                out[at, :] = summed
                sending(side, p, True, out).start()
                final(side, p, begin, begin)

            @pl.when(jnp.logical_not(end))
            def _():
                got[at, :] = summed
                sending(side, p, False, got).start()

    def back(side, p):
        start, end = (high_end, low_end) if side == 0 else (low_end, high_end)

        @pl.when(jnp.logical_not(end))
        def _():
            sending(side, p, True, out).wait_recv()

            @pl.when(jnp.logical_not(start))
            def _():
                sending(side, p, True, out).start()

            final(side, p, begin, begin)

    def guarded(act, side, p):
        @pl.when(jnp.logical_and(p >= 0, p < parts))
        def _():
            act(side, p)

    tail_at = half + LATE * PIECE
    finished = LATE + TAIL + skew * (2 * far - me)
    for copy in late:
        copy.wait()

    def step(t, _):
        def one_tile(k, _):
            i = 2 * t + k

            @pl.when(i < in_tiles)
            def _():
                make_tile(i, normed[:, block_of(i, tile)], g_in)

            @pl.when(jnp.logical_and(i >= in_tiles, i < tiles))
            def _():
                make_tile(i, yn[:, block_of(i - in_tiles, tile)], go)

            pl.when(jnp.logical_and(i >= 2, i < tiles + 2))(lambda: body_copy(i - 2).wait())
            return 0

        lax.fori_loop(0, 2, one_tile, 0)

        @pl.when(t == 5)
        def _():
            here = block_of(head, rows_here)
            dn = dot(g_in[here, :], w_in[...], NT)
            for d in range(heads - 1):
                du_copy(d).wait()
                dn = dn + du_got[d].astype(F32)
            du, grad = input_gradient(dn, u[here, :], norm_gain_of(block, u.shape[1])[...], above[...])
            du_rows[...] = du.astype(BF)
            inputs.start()
            few_mine[...] = few0[...]
            wide = few0.shape[1]
            for i in range(2):
                few_mine[8 + i : 9 + i, :] = grad[:, i * wide : (i + 1) * wide]
            pl.when(layer == 0)(lambda: few_to_core(few1).start())
            pl.when(layer == 1)(lambda: few_to_core(few_mine).start())

        @pl.when(t == 7)
        def _():
            few_to_core(few_mine).wait()
            pl.when(layer == 0)(lambda: few_seq.__setitem__(me, few_mine[...] + few_core[...]))
            pl.when(layer == 1)(lambda: few_seq.__setitem__(me, few1[...] + few_core[...]))
            for d in range(size - 1):
                few_to_seq(d).start()

        @pl.when(t == 11)
        def _():
            for d in range(size - 1):
                few_to_seq(d).wait()
            total = few_seq[0]
            for i in range(1, size):
                total = total + few_seq[i]
            few_o[0 : FEW // 2, :] = total[0 : FEW // 2]
            few_head[head] = total[FEW // 2 :]
            for d in range(heads - 1):
                few_to_head(d).start()

        @pl.when(t == 16)
        def _():
            for d in range(heads - 1):
                few_to_head(d).wait()
            total = few_head[0]
            for i in range(1, heads):
                total = total + few_head[i]
            few_o[FEW // 2 :, :] = total

        @pl.when(t == 4)
        def _():
            total = shared[shared_block(head), :].astype(F32)
            for d in range(heads - 1):
                scatter(d).wait()
                total = total + shared_got[d].astype(F32)
            own[tail_at + OWN : tail_at + OWN + SHARED, :] = total.astype(BF)
            own[tail_at : tail_at + OWN, :] = shared[0:OWN, :]

        guarded(reduce, 0, t - skew * (far - me))
        guarded(reduce, 1, t - skew * me)
        guarded(back, 0, t - skew * (far + me))
        guarded(back, 1, t - skew * (2 * far - me))

        @pl.when(t == finished)
        def _():
            tail_o[...] = out[tail_at : tail_at + OWN, :]
            shared_o[head] = out[tail_at + OWN : tail_at + OWN + SHARED, :]
            for d in range(heads - 1):
                gather(d).start()

        return 0

    lax.fori_loop(0, parts + 2 * skew * far, step, 0)

    def drain(p, _):
        for side in range(2):
            start, end = (high_end, low_end) if side == 0 else (low_end, high_end)

            @pl.when(jnp.logical_not(end))
            def _():
                sending(side, p, False, got).wait_send()

            @pl.when(jnp.logical_not(start))
            def _():
                sending(side, p, True, out).wait_send()

            final(side, p, lambda copy: copy.wait(), lambda copy: copy.wait_send())
            final(side, p, lambda copy: give(side, p, first_o, pl.ds(0, PIECE)).wait_recv(), lambda copy: None)
        return 0

    lax.fori_loop(0, parts, drain, 0)
    for d in range(heads - 1):
        gather(d).wait()
    pl.when(layer == 0)(lambda: all_of(given, lambda copy: copy.wait_send()))
    pl.when(layer == 1)(lambda: all_of(kept, lambda copy: copy.wait()))
    pl.when(layer == 1)(lambda: all_of(given, lambda copy: copy.wait_recv()))

    inputs.finish()


def grad_sum(layer0, body1, tails, fews, done, size, heads, skew=2):
    width = body1.shape[1]
    total = body1.shape[0] + done[1].shape[0]
    n, d_model = layer0[3].shape
    half = LATE * PIECE + (total + OWN + SHARED) // 2
    parts = half // PIECE
    vm = pl.BlockSpec(memory_space=pltpu.VMEM)
    anywhere = pl.BlockSpec(memory_space=pl.ANY)
    pair = pltpu.SemaphoreType.DMA((2, parts))
    sems = lambda *k: pltpu.SemaphoreType.DMA(k)
    tiles = total // 256
    big = pltpu.VMEM((2 * half, width), BF)
    body = pltpu.VMEM((total, width), BF)
    return pl.pallas_call(
        functools.partial(grad_sum_kernel, size, heads, skew),
        out_shape=(
            shape((total, width), BF),
            shape((total, width), BF),
            shape((OWN, width), BF),
            shape((heads, SHARED, width), BF),
            shape((FEW, width), F32),
            shape((2 * n, d_model), BF),
        ),
        in_specs=[vm] * 8 + [anywhere] * 3 + [vm] * 2 + [anywhere] * 2,
        out_specs=(anywhere, anywhere, vm, vm, vm, anywhere),
        scratch_shapes=[big, body, big, big]
        + [pltpu.VMEM((OWN + heads * SHARED, width), BF) for _ in range(2)]
        + [pltpu.VMEM((heads - 1, SHARED, width), BF)]
        + [pltpu.VMEM((FEW, width), F32), pltpu.VMEM((size, FEW, width), F32)]
        + [pltpu.VMEM((heads, FEW // 2, width), F32)]
        + [body] * 2
        + [pltpu.VMEM((heads - 1, n // heads, d_model), BF) for _ in range(2)]
        + [pltpu.VMEM((n // heads, d_model), BF), pltpu.VMEM((FEW, width), F32)]
        + [sems(tiles)] * 2
        + [pair] * 7
        + [sems(2, heads - 1)] * 2
        + [sems(11)]
        + [sems(size - 1)] * 2
        + [sems(heads - 1)] * 4
        + collect_sems(heads),
        compiler_params=pltpu.CompilerParams(
            collective_id=8, has_side_effects=True, vmem_limit_bytes=VMEM_LIMIT
        ),
        name="grad_sum",
    )(*layer0, body1, *tails, *fews, *done)


def unpack_kernel(dims, first, second, first_low, second_low, own, shared, few,
                  z_o, x_o, out_o, bc_o, dt_o, conv_o, conv_bias_o, bc_conv_o, bc_bias_o,
                  dt_bias_o, a_log_o, skip_o, gate_o, gain_o):
    heads, inner, states = dims
    half = own.shape[1]
    z_o[...] = first[...].astype(F32)
    x_o[...] = second[...].astype(F32)
    out_o[:, :half] = first_low[...].astype(F32)
    out_o[:, half:] = second_low[...].astype(F32)

    @pl.when(pl.program_id(0) == 0)
    def _():
        blocks = jnp.concatenate([shared[i] for i in range(shared.shape[0])], axis=0)
        step = blocks.shape[0] // 2
        for i in range(2):
            rows = slice(i * half, (i + 1) * half)
            bc_o[rows, :] = jnp.transpose(blocks[i * step : i * step + 2 * states].astype(F32))
            dts = own[i * OWN // 2 : (i + 1) * OWN // 2, :].astype(F32)
            dts = jnp.concatenate([dts, jnp.zeros((LANES - OWN // 2, half), F32)], axis=0)
            dt_o[rows, :] = jnp.transpose(dts)[:, :heads]
            gain_o[:, rows] = few[8 + i : 9 + i, :]
        conv_o[...] = few[0:4, :]
        conv_bias_o[...] = few[4:5, :]
        gate_o[...] = few[5:6, :]
        bc_conv_o[...] = few[10:14, 0 : 2 * states]
        bc_bias_o[...] = few[14:15, 0 : 2 * states]
        dt_bias_o[...] = few[6:7, 0:heads]
        a_log_o[...] = few[6:7, LANES : LANES + heads]
        skip_o[...] = few[6:7, 2 * LANES : 2 * LANES + heads]


def unpack(first, second, own, shared, few, dims, steps=6):
    heads, inner, states = dims
    half = first.shape[1]
    width = 2 * half
    tall, low = width // steps, inner // steps
    upper = pl.BlockSpec((tall, half), lambda i: (i, 0))
    lower = pl.BlockSpec((low, half), lambda i: (width // low + i, 0))
    whole = lambda a: pl.BlockSpec(a.shape, lambda i: (0,) * len(a.shape))
    outs = [
        ((width, inner), (tall, inner)),
        ((width, inner), (tall, inner)),
        ((inner, width), (low, width)),
    ]
    fixed = [
        (width, 2 * states), (width, heads), (4, inner), (1, inner), (4, 2 * states), (1, 2 * states),
        (1, heads), (1, heads), (1, heads), (1, inner), (1, width),
    ]
    return pl.pallas_call(
        functools.partial(unpack_kernel, dims),
        grid=(steps,),
        out_shape=[shape(a, F32) for a, _ in outs] + [shape(a, F32) for a in fixed],
        in_specs=[upper] * 2 + [lower] * 2 + [whole(own), whole(shared), whole(few)],
        out_specs=[pl.BlockSpec(b, lambda i: (i, 0)) for _, b in outs]
        + [pl.BlockSpec(a, lambda i: (0, 0)) for a in fixed],
        compiler_params=pltpu.CompilerParams(vmem_limit_bytes=VMEM_LIMIT),
        name="unpack",
    )(first, second, first, second, own, shared, few)


def normalise(u, gain):
    uv = u.astype(F32)
    s = lax.rsqrt(jnp.mean(uv * uv, axis=-1, keepdims=True) + EPSILON)
    return (uv * s * gain).astype(BF)


def on_device(
    inputs, cotangent, norm_gain, w_z, w_x, w_bc, w_dt, conv_x, conv_x_bias, conv_bc, conv_bc_bias,
    dt_bias, a_log, d_skip, gate_gain, w_out,
):
    me = lax.axis_index("section")
    seq_size, head_size = lax.axis_size("seq"), lax.axis_size("head")
    micro, n, d_model = inputs.shape
    batch = micro // 2
    tokens = batch * n
    inner, heads, states = w_z.shape[2], w_dt.shape[2], w_bc.shape[2] // 2
    wide = inner + 2 * states
    full = inner * head_size
    dims = (heads, inner, states)
    pad_heads = lambda a: jnp.pad(a, ((0, 0),) * (a.ndim - 1) + ((0, LANES - heads),))

    taps_x = jnp.concatenate([conv_x[0], conv_x_bias, jnp.zeros((3, inner), F32)], axis=0)
    taps_bc = jnp.concatenate([conv_bc[0], conv_bc_bias, jnp.zeros((3, 2 * states), F32)], axis=0)
    taps = jnp.concatenate([taps_x, taps_bc], axis=1)
    scalars = pad_heads(jnp.concatenate([dt_bias, -jnp.exp(a_log)], axis=0)).reshape(1, -1)
    vectors = jnp.concatenate(
        [
            jnp.repeat(d_skip[0], inner // heads)[None],
            gate_gain,
            jnp.pad(scalars, ((0, 0), (0, inner - 2 * LANES))),
            jnp.zeros((5, inner), F32),
        ],
        axis=0,
    )
    gains = jnp.broadcast_to(norm_gain, (8, d_model))
    w_in0, w_out0, block0, w_in1, w_out1, block1 = both_layers(
        [[w_z[0], w_x[0], w_bc[0], pad_heads(w_dt[0])], [w_out[0]], [taps, vectors, gains]]
    )

    u = lax.dynamic_slice_in_dim(inputs, me * batch, batch, 0).reshape(tokens, d_model)
    cot = lax.dynamic_slice_in_dim(cotangent, me * batch, batch, 0).reshape(tokens, d_model)

    flat = lambda a: a.reshape(tokens, -1)
    stacked = lambda a: a.reshape(batch, n, -1)

    normed0 = normalise(u, block0[0:1, block0.shape[1] - d_model :])
    proj0 = stacked(dot(normed0, w_in0))
    cx0, dt0, cum0, state0, halo0, y0, yn0, stats0 = ssd_fwd(
        proj0, block0, None, dims, seq_size, head_size, full
    )
    h0, normed1, proj1 = head_fwd(flat(yn0), w_out0, u, head_size, [w_in1, block1])
    proj1 = stacked(proj1)
    dyn1 = stacked(dot(cot, w_out1, NT))
    cx1, dt1, cum1, state1, halo1, y1, yn1, stats1 = ssd_fwd(
        proj1, block1, dyn1, dims, seq_size, head_size, full
    )
    h1_rows, body1_out = head_fwd(flat(yn1), w_out1, h0, head_size, [], cot)
    done_out = lax.psum(body1_out, "seq")

    g_in1, gate1, conv1, small1, layer_outputs = ssd_bwd(
        dyn1, y1, proj1, halo1, cx1, dt1, cum1, state1, stats1, block1, [h1_rows, h0],
        dims, seq_size, head_size, full,
    )
    g_in1 = flat(g_in1)
    du1, du1_rows, gain1, dyn0, body1 = head_bwd(
        g_in1, w_in1, cot, h0, block1, w_out0, normed1, flat(yn1), head_size
    )
    body1_early, done_out = lax.optimization_barrier((body1[: d_model - 2 * LATE * PIECE], done_out))
    done = lax.psum(body1_early, "seq")
    tail1, few1 = grad_tail(normed1, g_in1, conv1, small1, gate1, gain1, dims, head_size)
    g_in0, gate0, conv0, small0 = ssd_bwd(
        stacked(dyn0), y0, proj0, halo0, cx0, dt0, cum0, state0, stats0, block0, [],
        dims, seq_size, head_size, full,
    )
    g_in0 = flat(g_in0)
    tail0, few0 = grad_tail(normed0, g_in0, conv0, small0, gate0, jnp.zeros_like(gain1), dims, head_size)
    first, second, own, shared, few, input_grads = grad_sum(
        (g_in0, w_in0, du1_rows, u, block0, normed0, flat(yn0), du1),
        body1, (tail0, tail1), (few0, few1), (done, done_out), seq_size, head_size,
    )
    g_z, g_x, g_out, g_bc, g_dt, g_conv, g_conv_bias, g_bc_conv, g_bc_bias, *scalars, g_gate, g_gain = unpack(
        first, second, own, shared, few, dims
    )

    return (
        layer_outputs.reshape(1, micro, n, d_model),
        input_grads.reshape(1, micro, n, d_model),
        g_gain,
        g_z[None],
        g_x[None],
        g_bc[None],
        g_dt[None],
        g_conv[None],
        g_conv_bias,
        g_bc_conv[None],
        g_bc_bias,
        *scalars,
        g_gate,
        g_out[None],
    )


def solution(mesh):
    in_specs = (
        P(None, "seq", None),
        P(None, "seq", None),
        P("section", None),
        P("section", None, "head"),
        P("section", None, "head"),
        P("section", None, None),
        P("section", None, "head"),
        P("section", None, "head"),
        P("section", "head"),
        P("section", None, None),
        P("section", None),
        P("section", "head"),
        P("section", "head"),
        P("section", "head"),
        P("section", "head"),
        P("section", "head", None),
    )
    out_specs = (
        P("section", None, "seq", None),
        P("section", None, "seq", None),
        P("section", None),
        P("section", None, "head"),
        P("section", None, "head"),
        P("section", None, None),
        P("section", None, "head"),
        P("section", None, "head"),
        P("section", "head"),
        P("section", None, None),
        P("section", None),
        P("section", "head"),
        P("section", "head"),
        P("section", "head"),
        P("section", "head"),
        P("section", "head", None),
    )
    return jax.shard_map(
        on_device, mesh=mesh, in_specs=in_specs, out_specs=out_specs, check_vma=False
    )
```

```python
import functools

import jax
import jax.numpy as jnp
from jax import lax
from jax.experimental import pallas as pl
from jax.experimental.pallas import tpu as pltpu
from jax.sharding import PartitionSpec as P

EPSILON = 1e-05
MESH = pl.DeviceIdType.MESH
HIGH = lax.Precision.HIGHEST
BF = jnp.bfloat16
F32 = jnp.float32
LANES = 128
VMEM_LIMIT = 56 * 2**20


def shape(dims, kind):
    return jax.ShapeDtypeStruct(dims, kind)


def dot(a, b, dims=((1,), (0,)), precision=None):
    return lax.dot_general(a, b, (dims, ((), ())), precision=precision, preferred_element_type=F32)


NT = ((1,), (1,))
TN = ((0,), (0,))


def halves(v):
    high = v.astype(BF)
    return high, (v - high.astype(F32)).astype(BF)


def dot_mask(v, mask, dims=((1,), (0,))):
    high, rest = halves(v)
    return dot(high, mask, dims) + dot(rest, mask, dims)


def dot3(a, b, dims=((1,), (0,))):
    a_high, a_rest = halves(a)
    b_high, b_rest = halves(b)
    return dot(a_high, b_high, dims) + dot(a_rest, b_high, dims) + dot(a_high, b_rest, dims)


def mask_dot(mask, v):
    high, rest = halves(v)
    return dot(mask, high) + dot(mask, rest)


def head_mask(width, heads):
    size = width // heads
    return (
        lax.broadcasted_iota(jnp.int32, (LANES, width), 0)
        == lax.broadcasted_iota(jnp.int32, (LANES, width), 1) // size
    ).astype(F32).astype(BF)


def order_mask(n, lower):
    rows = lax.broadcasted_iota(jnp.int32, (n, n), 0)
    columns = lax.broadcasted_iota(jnp.int32, (n, n), 1)
    return (rows >= columns) if lower else (rows <= columns)


def sigmoid(v):
    return 1.0 / (1.0 + jnp.exp(-v))


def softplus(v):
    return jnp.maximum(v, 0.0) + jnp.log1p(jnp.exp(-jnp.abs(v)))


def column(row_block):
    n = row_block.shape[1]
    return [
        jnp.transpose(jnp.broadcast_to(row_block[i : i + 1, :], (LANES, n))) for i in range(2)
    ]


def rows_of(columns):
    n = columns[0].shape[0]
    rows = [jnp.transpose(jnp.broadcast_to(c, (n, LANES)))[0:1] for c in columns]
    return jnp.concatenate(rows + [jnp.zeros((8 - len(rows), n), F32)], axis=0)


def conv_pre(ext, proj_xbc, halo, taps, bias):
    n = proj_xbc.shape[0]
    ext[0:8, :] = halo
    ext[8 : 8 + n, :] = proj_xbc
    pre = bias + taps[3:4, :] * proj_xbc
    for k in range(3):
        pre = pre + taps[k : k + 1, :] * ext[5 + k : 5 + k + n, :]
    return pre


def push(src, dst, send, recv, device):
    copy = pltpu.make_async_remote_copy(
        src_ref=src, dst_ref=dst, send_sem=send, recv_sem=recv, device_id=device, device_id_type=MESH
    )
    copy.start()
    return copy


def both_layers_kernel(places, *refs):
    count = len(places)
    groups = places[-1][0] + 1
    ins, outs = refs[:count], refs[count:-3]
    send, recv, local = refs[-3:]
    me = lax.axis_index("section")
    other = {"section": 1 - me}
    barrier = pltpu.get_barrier_semaphore()
    pl.semaphore_signal(barrier, inc=1, device_id=other, device_id_type=MESH)
    pl.semaphore_wait(barrier, 1)

    def copies(i, which, start, layer):
        target = outs[layer * groups + which].at[:, pl.ds(start, ins[i].shape[1])]
        return (
            pltpu.make_async_remote_copy(
                src_ref=ins[i], dst_ref=target, send_sem=send.at[i], recv_sem=recv.at[i],
                device_id=other, device_id_type=MESH,
            ),
            pltpu.make_async_copy(ins[i], target, local.at[i]),
        )

    for layer in range(2):

        @pl.when(me == layer)
        def _():
            for i, (which, start) in enumerate(places):
                for copy in copies(i, which, start, layer):
                    copy.start()

    for i, (which, start) in enumerate(places):
        for copy in copies(i, which, start, 0):
            copy.wait()


def both_layers(groups):
    places, flat, outs = [], [], []
    for i, group in enumerate(groups):
        start = 0
        for a in group:
            places.append((i, start))
            flat.append(a)
            start += a.shape[1]
        outs.append(shape((group[0].shape[0], start), group[0].dtype))
    count = len(flat)
    vm = pl.BlockSpec(memory_space=pltpu.VMEM)
    anywhere = pl.BlockSpec(memory_space=pl.ANY)
    return pl.pallas_call(
        functools.partial(both_layers_kernel, places),
        out_shape=tuple(outs) * 2,
        in_specs=[vm] * count,
        out_specs=(anywhere,) * (2 * len(outs)),
        scratch_shapes=[pltpu.SemaphoreType.DMA((count,)) for _ in range(3)],
        compiler_params=pltpu.CompilerParams(
            collective_id=0, has_side_effects=True, vmem_limit_bytes=VMEM_LIMIT
        ),
        name="both_layers",
    )(*flat)


def constants(block, dims):
    heads, inner, states = dims
    wide = inner + 2 * states
    return (
        block.at[0:4, 0:wide],
        block.at[4:5, 0:wide],
        block.at[2:3, wide : wide + LANES],
        block.at[2:3, wide + LANES : wide + 2 * LANES],
        block.at[0:1, wide : wide + inner],
        block.at[1:2, wide : wide + inner],
    )


def norm_gain_of(block, d_model):
    return block.at[0:1, block.shape[1] - d_model :]


class Line:
    def __init__(self, forward, size, parts, outgoing, incoming, send, recv):
        self.me = lax.axis_index("seq")
        self.size, self.parts = size, parts
        self.outgoing, self.incoming, self.send, self.recv = outgoing, incoming, send, recv
        first, last = self.me == 0, self.me == size - 1
        self.starts, self.ends = (first, last) if forward else (last, first)
        self.place = self.me if forward else size - 1 - self.me
        step = 1 if forward else -1
        self.target, self.source = {"seq": self.me + step}, {"seq": self.me - step}

    def greet(self, barrier):
        @pl.when(jnp.logical_not(self.starts))
        def _():
            pl.semaphore_signal(barrier, inc=1, device_id=self.source, device_id_type=MESH)

    def met(self, barrier, others=0):
        @pl.when(jnp.logical_not(self.ends))
        def _():
            pl.semaphore_wait(barrier, others + 1)

        if others:

            @pl.when(self.ends)
            def _():
                pl.semaphore_wait(barrier, others)

    def copy(self, m, p):
        width = self.outgoing.shape[2] // self.parts
        at = pl.ds(p * width, width)
        return pltpu.make_async_remote_copy(
            src_ref=self.outgoing.at[m, :, at],
            dst_ref=self.incoming.at[m, :, at],
            send_sem=self.send.at[m * self.parts + p],
            recv_sem=self.recv.at[m * self.parts + p],
            device_id=self.target,
            device_id_type=MESH,
        )

    def begin(self, m, own):
        @pl.when(self.starts)
        def _():
            self.incoming[m] = jnp.zeros_like(self.incoming[m])
            self.outgoing[m] = own.astype(self.outgoing.dtype)
            for p in range(self.parts):
                self.copy(m, p).start()

    def relay(self, own, decay, at_step, steps, lag, apart):
        width = self.outgoing.shape[2] // self.parts
        for i in range(self.outgoing.shape[0] * self.parts):
            m, p = i // self.parts, i % self.parts
            at = slice(p * width, (p + 1) * width)
            due = jnp.minimum(self.place * lag + apart * i, steps - 1)

            @pl.when(jnp.logical_and(self.place > 0, due == at_step))
            def _():
                self.copy(m, p).wait_recv()

                @pl.when(jnp.logical_not(self.ends))
                def _():
                    passed = decay[m, 0:1, at] * self.incoming[m, :, at].astype(F32) + own[m, :, at]
                    self.outgoing[m, :, at] = passed.astype(self.outgoing.dtype)
                    self.copy(m, p).start()

    def finish(self):
        @pl.when(jnp.logical_not(self.ends))
        def _():
            for m in range(self.outgoing.shape[0]):
                for p in range(self.parts):
                    self.copy(m, p).wait_send()

    def halo(self, src, dst, m, send, recv):
        return pltpu.make_async_remote_copy(
            src_ref=src, dst_ref=dst, send_sem=send.at[m], recv_sem=recv.at[m],
            device_id=self.target, device_id_type=MESH,
        )


PARTS = 3


def ssd_fwd_kernel(dims, size, heads_axis, full, has_dyn, *refs):
    proj, block = refs[:2]
    taps, bias, dt_bias, a_neg, skip, gain = constants(block, dims)
    dyn = refs[2] if has_dyn else None
    (cx, dt_o, cum_o, state, halo, y_o, yn_o, stats_o,
     ext, own, decay, rim, outgoing, incoming, gates, square, square_got,
     send, recv, halo_send, halo_recv, stat_send, stat_recv) = refs[2 + has_dyn :]
    heads, inner, states = dims
    batch, n = proj.shape[0], proj.shape[1]
    wide = inner + 2 * states
    head_lanes = inner // heads
    columns = slice(inner, inner + wide)
    line = Line(True, size, PARTS, outgoing, incoming, send, recv)
    head = lax.axis_index("head")
    peers = [{"head": lax.rem(head + d, heads_axis)} for d in range(1, heads_axis)]
    barrier = pltpu.get_barrier_semaphore()
    line.greet(barrier)
    for peer in peers:
        pl.semaphore_signal(barrier, inc=1, device_id=peer, device_id_type=MESH)
    for m in range(batch):
        rim[m] = proj[m, n - 16 :, columns].astype(BF)
    line.met(barrier, len(peers))

    @pl.when(jnp.logical_not(line.ends))
    def _():
        for m in range(batch):
            line.halo(rim.at[m], halo.at[m], m, halo_send, halo_recv).start()

    @pl.when(line.starts)
    def _():
        halo[...] = jnp.zeros_like(halo)

    expand = head_mask(inner, heads)
    for m in range(batch):

        @pl.when(jnp.logical_not(line.starts))
        def _():
            line.halo(rim.at[m], halo.at[m], m, halo_send, halo_recv).wait_recv()

        xbc = proj[m, :, columns].astype(BF).astype(F32)
        pre = conv_pre(ext, xbc, halo[m, 8:].astype(F32), taps[...], bias[...])
        act = pre * sigmoid(pre)
        cx[m] = act
        dt = softplus(proj[m, :, inner + wide :] + dt_bias[...])
        cum = mask_dot(order_mask(n, True).astype(F32).astype(BF), dt * a_neg[...])
        dt_o[m] = dt
        cum_o[m] = cum
        last = cum[n - 1 : n, :]
        weight = dot_mask(jnp.exp(last - cum) * dt, expand)
        mine = dot3(act[:, inner : inner + states], act[:, :inner] * weight, TN)
        own[m] = mine
        decay[m] = dot_mask(jnp.broadcast_to(jnp.exp(last), (8, LANES)), expand)
        line.begin(m, mine)
    keep = order_mask(n, True)
    first = lax.broadcasted_iota(jnp.int32, (n, LANES), 1) < head_lanes
    pairs = heads // 2
    for m in range(batch):
        scores = dot3(cx[m, :, inner + states :], cx[m, :, inner : inner + states], NT)
        cums = cum_o[m]
        cums_t = jnp.transpose(cums)
        dt_wide = dot_mask(dt_o[m], expand)
        for p in range(pairs):

            line.relay(own, decay, m * pairs + p, batch * pairs, 4, 2)
            lanes = slice(p * LANES, (p + 1) * LANES)
            x = cx[m, :, lanes]
            dtx, dtx_rest = halves(x * dt_wide[:, lanes])
            both = []
            for h in (2 * p, 2 * p + 1):
                sums = []
                for low, high in ((0, n // 2), (n // 2, n)):
                    lag = cums[low:high, h : h + 1] - cums_t[h : h + 1, 0:high]
                    lag = jnp.where(keep[low:high, 0:high], lag, -1e30)
                    top, rest = halves(scores[low:high, 0:high] * jnp.exp(lag))
                    sums.append(dot(top, dtx[0:high]) + dot(rest, dtx[0:high]) + dot(top, dtx_rest[0:high]))
                both.append(jnp.concatenate(sums, axis=0))
            y_o[m, :, lanes] = skip[:, lanes] * x + jnp.where(first, both[0], both[1])
    for m in range(batch):
        entered = incoming[m]
        state[m] = entered
        y = y_o[m] + dot_mask(jnp.exp(cum_o[m]), expand) * dot3(cx[m, :, inner + states :], entered)
        y_o[m] = y
        z = proj[m, :, :inner]
        gated = y * z * sigmoid(z)
        gates[m] = gated
        stats = [jnp.sum(gated * gated, axis=1, keepdims=True)]
        if has_dyn:
            stats.append(jnp.sum(gated * gain[...] * dyn[m], axis=1, keepdims=True))
        square[m] = rows_of(stats)
    copies = [
        push(square, square_got.at[d], stat_send.at[d], stat_recv.at[d], peer) for d, peer in enumerate(peers)
    ]
    for copy in copies:
        copy.wait()
    for m in range(batch):
        total = square[m]
        for d in range(heads_axis - 1):
            total = total + square_got[d, m]
        gs = lax.rsqrt(total[0:1] / full + EPSILON)
        stats_o[m] = jnp.concatenate([gs, total[1:]], axis=0)
        yn_o[m] = (gates[m] * column(stats_o[m])[0][:, 0:1] * gain[...]).astype(BF)
    line.finish()

    @pl.when(jnp.logical_not(line.ends))
    def _():
        for m in range(batch):
            line.halo(rim.at[m], halo.at[m], m, halo_send, halo_recv).wait_send()


def ssd_fwd(proj, block, dyn, dims, size, heads_axis, full):
    heads, inner, states = dims
    batch, n, _ = proj.shape
    wide = inner + 2 * states
    vm = pl.BlockSpec(memory_space=pltpu.VMEM)
    has_dyn = dyn is not None
    moved = (batch, states, inner)
    outs = (
        shape((batch, n, wide), F32),
        shape((batch, n, LANES), F32),
        shape((batch, n, LANES), F32),
        shape(moved, F32),
        shape((batch, 16, wide), BF),
        shape((batch, n, inner), F32),
        shape((batch, n, inner), BF),
        shape((batch, 8, n), F32),
    )
    return pl.pallas_call(
        functools.partial(ssd_fwd_kernel, dims, size, heads_axis, full, has_dyn),
        out_shape=outs,
        in_specs=[vm] * (2 + has_dyn),
        out_specs=(vm,) * len(outs),
        scratch_shapes=[
            pltpu.VMEM((n + 8, wide), F32),
            pltpu.VMEM(moved, F32),
            pltpu.VMEM((batch, 8, inner), F32),
            pltpu.VMEM((batch, 16, wide), BF),
            pltpu.VMEM(moved, F32),
            pltpu.VMEM(moved, F32),
            pltpu.VMEM((batch, n, inner), F32),
            pltpu.VMEM((batch, 8, n), F32),
            pltpu.VMEM((heads_axis - 1, batch, 8, n), F32),
            pltpu.SemaphoreType.DMA((batch * PARTS,)),
            pltpu.SemaphoreType.DMA((batch * PARTS,)),
            pltpu.SemaphoreType.DMA((batch,)),
            pltpu.SemaphoreType.DMA((batch,)),
            pltpu.SemaphoreType.DMA((heads_axis - 1,)),
            pltpu.SemaphoreType.DMA((heads_axis - 1,)),
        ],
        compiler_params=pltpu.CompilerParams(
            collective_id=1 + has_dyn, has_side_effects=True, vmem_limit_bytes=VMEM_LIMIT
        ),
        name="ssd_fwd",
    )(proj, block, *([dyn] if has_dyn else []))


def ssd_bwd_kernel(
    dims, size, heads_axis, full, has_across,
    dyn, y, proj, halo, cx, dt, cum, state, stats, block, *refs
):
    taps, bias, dt_bias, a_neg, skip, gain = constants(block, dims)
    if has_across:
        h_rows, h_whole, h_o, *refs = refs[:2] + refs[6:7] + refs[2:6] + refs[7:]
        *refs, c_local, c_send, c_recv = refs
    (
    g_in, gate_o, conv_o, small_o,
    dy, dxw, dpre, own, decay, ext, rowq, colq, d_scores, outgoing, incoming, rim, square, square_got,
    send, recv, rim_send, rim_recv, stat_send, stat_recv,
    ) = refs
    heads, inner, states = dims
    batch, n = dyn.shape[0], dyn.shape[1]
    wide = inner + 2 * states
    columns = slice(inner, inner + wide)
    size_p = inner // heads
    pairs = heads // 2
    line = Line(False, size, PARTS, outgoing, incoming, send, recv)
    head = lax.axis_index("head")
    peers = [{"head": lax.rem(head + d, heads_axis)} for d in range(1, heads_axis)]
    barrier = pltpu.get_barrier_semaphore()
    line.greet(barrier)
    if has_across:
        outputs = Collect(1, heads_axis, h_rows, h_whole, h_o, c_local, c_send, c_recv)
        peers = outputs.greeted()
    for peer in peers:
        pl.semaphore_signal(barrier, inc=1, device_id=peer, device_id_type=MESH)
    if not has_across:
        for m in range(batch):
            z = proj[m, :, :inner]
            square[m] = rows_of([jnp.sum(dyn[m] * gain[...] * y[m] * z * sigmoid(z), axis=1, keepdims=True)])
    line.met(barrier, len(peers))
    if has_across:
        outputs.start()
    else:
        copies = [
            push(square, square_got.at[d], stat_send.at[d], stat_recv.at[d], peers[d])
            for d in range(heads_axis - 1)
        ]
    expand = head_mask(inner, heads)
    if not has_across:
        for copy in copies:
            copy.wait()
    for m in range(batch):
        gs, across = [v[:, 0:1] for v in column(stats[m])]
        if has_across:
            pass
        else:
            total = square[m]
            for d in range(heads_axis - 1):
                total = total + square_got[d, m]
            across = column(total)[0][:, 0:1]
        z = proj[m, :, :inner]
        sig = sigmoid(z)
        yv = y[m]
        gated = yv * z * sig
        dynv = dyn[m]
        scaled = gated * gs
        gate_o[m] = jnp.broadcast_to(jnp.sum(dynv * scaled, axis=0, keepdims=True), (8, inner))
        dgated = gs * gain[...] * dynv - gated * (gs * gs * gs * across / full)
        dyv = dgated * z * sig
        dy[m] = dyv
        g_in[m, :, :inner] = (dgated * yv * sig * (1.0 + z * (1.0 - sig))).astype(BF)
        cums = cum[m]
        moved = dot_mask(jnp.exp(cums), expand) * dyv
        mine = dot3(cx[m, :, inner + states :], moved, TN)
        own[m] = mine
        decay[m] = dot_mask(jnp.broadcast_to(jnp.exp(cums[n - 1 : n, :]), (8, LANES)), expand)
        line.begin(m, mine)
    keep = order_mask(n, False)
    lane = lax.broadcasted_iota(jnp.int32, (n, LANES), 1)
    first = lane < size_p
    rowq[...] = jnp.zeros_like(rowq)
    for m in range(batch):
        scores_t = dot3(cx[m, :, inner : inner + states], cx[m, :, inner + states :], NT)
        cums = cum[m]
        cums_t = jnp.transpose(cums)
        dt_wide = dot_mask(dt[m], expand)
        colq[m] = jnp.zeros_like(colq[m])
        d_scores[m] = jnp.zeros_like(d_scores[m])
        for p in range(pairs):

            line.relay(own, decay, m * pairs + p, batch * pairs, 2, 1)
            lanes = slice(p * LANES, (p + 1) * LANES)
            dtx, dtx_rest = halves(cx[m, :, lanes] * dt_wide[:, lanes])
            dyb, dy_rest = halves(dy[m, :, lanes])
            both, gathered = [], [0.0, 0.0]
            for j, h in enumerate((2 * p, 2 * p + 1)):
                side = first if j == 0 else jnp.logical_not(first)
                mine, mine_rest = [jnp.where(side, v, jnp.zeros((), BF)) for v in (dtx, dtx_rest)]
                sums, row_sums, column_sums = [], [], []
                for i, (low, high) in enumerate(((0, n // 2), (n // 2, n))):
                    lag = jnp.where(
                        keep[low:high, low:n], cums_t[h : h + 1, low:n] - cums[low:high, h : h + 1], -1e30
                    )
                    decays = jnp.exp(lag)
                    weights = scores_t[low:high, low:n] * decays
                    d_weights = (
                        dot(mine[low:high], dyb[low:n], NT)
                        + dot(mine[low:high], dy_rest[low:n], NT)
                        + dot(mine_rest[low:high], dyb[low:n], NT)
                    )
                    q = d_weights * weights
                    gathered[i] = gathered[i] + d_weights * decays
                    row_sums.append(jnp.sum(q, axis=0, keepdims=True))
                    column_sums.append(jnp.sum(q, axis=1, keepdims=True))
                    sums.append(dot(weights.astype(BF), dyb[low:n]))
                rowq[m, h : h + 1, :] = row_sums[0]
                rowq[m, h : h + 1, n // 2 :] += row_sums[1]
                colq[m] += jnp.where(lane == h, jnp.concatenate(column_sums, axis=0), 0.0)
                both.append(jnp.concatenate(sums, axis=0))
            d_scores[m, 0 : n // 2, :] += gathered[0]
            d_scores[m, n // 2 :, n // 2 :] += gathered[1]
            dxw[m, :, lanes] = jnp.where(first, both[0], both[1])
    fold = lambda v: dot_mask(v, expand, NT)
    for m in range(batch):
        x = cx[m, :, :inner]
        b = cx[m, :, inner : inner + states]
        c = cx[m, :, inner + states :]
        b_high, b_rest = halves(b)
        dyv, dxv, dtv, cums = dy[m], dxw[m], dt[m], cum[m]
        last = cums[n - 1 : n, :]
        entered, later_b = state[m], incoming[m]
        moved = dot_mask(jnp.exp(cums), expand) * dyv
        carried = dot3(c, entered)
        tail = jnp.exp(last - cums)
        weight = tail * dtv
        weight_wide = dot_mask(weight, expand)
        pulled = dot(b_high, later_b) + dot(b_rest, later_b)
        dx = dot_mask(dtv, expand) * dxv + weight_wide * pulled + skip[...] * dyv
        dw = fold(x * pulled)
        wdw = weight * dw
        change = jnp.transpose(rowq[m]) + fold(carried * moved) - colq[m] - wdw
        ends = jnp.sum(entered * later_b.astype(F32), axis=0, keepdims=True)
        ends = jnp.sum(wdw, axis=0, keepdims=True) + jnp.exp(last) * fold(jnp.broadcast_to(ends, (8, inner)))[0:1]
        log_grad = mask_dot(order_mask(n, False).astype(F32).astype(BF), change) + ends
        ddt = fold(x * dxv) + tail * dw + a_neg[...] * log_grad
        ddt_raw = ddt * sigmoid(proj[m, :, inner + wide :] + dt_bias[...])
        g_in[m, :, inner + wide :] = ddt_raw.astype(BF)
        small_o[m] = jnp.concatenate(
            [
                jnp.sum(ddt_raw, axis=0, keepdims=True),
                jnp.sum(dtv * log_grad, axis=0, keepdims=True) * a_neg[...],
                fold(jnp.broadcast_to(jnp.sum(x * dyv, axis=0, keepdims=True), (8, inner)))[0:1],
                jnp.zeros((5, LANES), F32),
            ],
            axis=0,
        )
        xw_high, xw_rest = halves(x * weight_wide)
        dc = dot3(d_scores[m], b, TN) + dot3(moved, entered, NT)
        db = dot3(d_scores[m], c) + dot(xw_high, later_b, NT) + dot(xw_rest, later_b, NT)
        xbc = proj[m, :, columns].astype(BF).astype(F32)
        pre = conv_pre(ext, xbc, halo[m, 8:].astype(F32), taps[...], bias[...])
        sig = sigmoid(pre)
        d_act = jnp.concatenate([dx, db, dc], axis=1) * sig * (1.0 + pre * (1.0 - sig))
        dpre[m, 0:n, :] = d_act
        rim_copy = line.halo(dpre.at[m, pl.ds(0, 8)], rim.at[m], m, rim_send, rim_recv)
        pl.when(jnp.logical_not(line.ends))(rim_copy.start)
        rows = [jnp.sum(d_act * ext[5 + k : 5 + k + n, :], axis=0, keepdims=True) for k in range(4)]
        rows.append(jnp.sum(d_act, axis=0, keepdims=True))
        conv_o[m] = jnp.concatenate(rows + [jnp.zeros((3, wide), F32)], axis=0)

    @pl.when(line.starts)
    def _():
        rim[...] = jnp.zeros_like(rim)

    for m in range(batch):
        rim_copy = line.halo(dpre.at[m, pl.ds(0, 8)], rim.at[m], m, rim_send, rim_recv)
        pl.when(jnp.logical_not(line.starts))(rim_copy.wait_recv)
        dpre[m, n : n + 8, :] = rim[m]
        total = taps[3:4, :] * dpre[m, 0:n, :]
        for k in range(3):
            total = total + taps[k : k + 1, :] * dpre[m, 3 - k : 3 - k + n, :]
        g_in[m, :, columns] = total.astype(BF)
        pl.when(jnp.logical_not(line.ends))(rim_copy.wait_send)
    line.finish()
    if has_across:
        outputs.finish()


def ssd_bwd(dyn, y, proj, halo, cx, dt, cum, state, stats, block, outputs,
            dims, size, heads_axis, full):
    has_across = bool(outputs)
    heads, inner, states = dims
    batch, n, wide = cx.shape
    vm = pl.BlockSpec(memory_space=pltpu.VMEM)
    moved = (batch, states, inner)
    outs = (
        shape((batch, n, inner + wide + LANES), BF),
        shape((batch, 8, inner), F32),
        shape((batch, 8, wide), F32),
        shape((batch, 8, LANES), F32),
    ) + tuple(shape((2 * a.shape[0], a.shape[1]), BF) for a in outputs[1:])
    sems = lambda k: pltpu.SemaphoreType.DMA((k,))
    return pl.pallas_call(
        functools.partial(ssd_bwd_kernel, dims, size, heads_axis, full, has_across),
        out_shape=outs,
        in_specs=[vm] * (10 + len(outputs)),
        out_specs=(vm,) * 4 + (pl.BlockSpec(memory_space=pl.ANY),) * has_across,
        scratch_shapes=[
            pltpu.VMEM((batch, n, inner), F32),
            pltpu.VMEM((batch, n, inner), F32),
            pltpu.VMEM((batch, n + 8, wide), F32),
            pltpu.VMEM(moved, F32),
            pltpu.VMEM((batch, 8, inner), F32),
            pltpu.VMEM((n + 8, wide), F32),
            pltpu.VMEM((batch, LANES, n), F32),
            pltpu.VMEM((batch, n, LANES), F32),
            pltpu.VMEM((batch, n, n), F32),
            pltpu.VMEM(moved, BF),
            pltpu.VMEM(moved, BF),
            pltpu.VMEM((batch, 8, wide), F32),
            pltpu.VMEM((batch, 8, n), F32),
            pltpu.VMEM((heads_axis - 1, batch, 8, n), F32),
            sems(batch * PARTS),
            sems(batch * PARTS),
            sems(batch),
            sems(batch),
            sems(heads_axis - 1),
            sems(heads_axis - 1),
        ]
        + (collect_sems(heads_axis) if has_across else []),
        compiler_params=pltpu.CompilerParams(
            collective_id=10 + has_across, has_side_effects=True, vmem_limit_bytes=VMEM_LIMIT
        ),
        name="ssd_bwd",
    )(dyn, y, proj, halo, cx, dt, cum, state, stats, block, *outputs)


def greet(size, core=False):
    me = lax.axis_index("head")
    barrier = pltpu.get_barrier_semaphore()
    peers = [{"head": lax.rem(me + d, size)} for d in range(1, size)]
    others = [{"section": 1 - lax.axis_index("section")}] if core else []
    for peer in peers + others:
        pl.semaphore_signal(barrier, inc=1, device_id=peer, device_id_type=MESH)
    pl.semaphore_wait(barrier, len(peers) + len(others))
    return me, peers


def block_of(index, rows):
    return pl.ds(pl.multiple_of(index * rows, rows), rows)


def normal(u, gain):
    uv = u.astype(F32)
    s = lax.rsqrt(jnp.sum(uv * uv, axis=1, keepdims=True) / uv.shape[1] + EPSILON)
    return (uv * s * gain).astype(BF)


def head_fwd_kernel(size, onward, yn, w_out, u, *refs):
    if onward:
        w_in, block, h_o, normed_o, proj_o, out, got, send, recv = refs
        gain = norm_gain_of(block, u.shape[1])
    else:
        go, h_o, body_o, out, got, body_send, body_got, send, recv, body_ss, body_rs = refs
    rows = yn.shape[0] // size
    me, peers = greet(size, core=not onward)
    copies = []
    for d, peer in enumerate(peers):
        to = lax.rem(me + d + 1, size)
        out[d] = dot(yn[block_of(to, rows), :], w_out[...]).astype(out.dtype)
        copies.append(push(out.at[d], got.at[d], send.at[0, d], recv.at[0, d], peer))
    mine = block_of(me, rows)
    total = dot(yn[mine, :], w_out[...])
    if not onward:
        body = body_halves(lambda which, i: body_tile(None, None, yn, go, which, i), body_o, body_send, body_got, body_ss, body_rs)
    for copy in copies:
        copy.wait()
    for d in range(size - 1):
        total = total + got[d].astype(F32)
    h = (u[mine, :].astype(F32) + total).astype(BF)
    if not onward:
        h_o[...] = h
        add_halves(body, body_o, body_got)
        return
    h_o[mine, :] = h
    copies = [
        push(h_o.at[mine], h_o.at[mine], send.at[1, d], recv.at[1, d], peer) for d, peer in enumerate(peers)
    ]

    def project(at):
        normed = normal(h_o[at, :], gain[...])
        normed_o[at, :] = normed
        proj_o[at, :] = dot(normed, w_in[...])

    project(mine)
    for d, copy in enumerate(copies):
        copy.wait_recv()
        project(block_of(lax.rem(me + size - d - 1, size), rows))
    for copy in copies:
        copy.wait_send()


def head_fwd(yn, w_out, u, size, onward, go=None):
    n, d_model = u.shape
    body = (yn.shape[1], d_model // 2)
    tiles = body[0] // 256
    rows = n // size
    vm = pl.BlockSpec(memory_space=pltpu.VMEM)
    kind = F32 if onward else BF
    outs = [shape((n if onward else rows, d_model), BF)]
    if onward:
        outs += [shape((n, d_model), BF), shape((n, onward[0].shape[1]), F32)]
    else:
        outs += [shape(body, BF)]
        onward = [go]
    more = go is not None
    return pl.pallas_call(
        functools.partial(head_fwd_kernel, size, not more),
        out_shape=tuple(outs),
        in_specs=[vm] * (3 + len(onward)),
        out_specs=(vm,) * len(outs),
        scratch_shapes=[
            pltpu.VMEM((size - 1, rows, d_model), kind),
            pltpu.VMEM((size - 1, rows, d_model), kind),
        ]
        + [pltpu.VMEM(body, BF)] * (2 * more)
        + [pltpu.SemaphoreType.DMA((2, size - 1))] * 2
        + [pltpu.SemaphoreType.DMA((tiles,))] * (2 * more),
        compiler_params=pltpu.CompilerParams(
            collective_id=6 if more else 3, has_side_effects=True, vmem_limit_bytes=VMEM_LIMIT
        ),
        name="head_fwd",
    )(yn, w_out, u, *onward)


def input_gradient(dn, u, gain, above):
    uv = u.astype(F32)
    width = uv.shape[1]
    s = lax.rsqrt(jnp.sum(uv * uv, axis=1, keepdims=True) / width + EPSILON)
    scaled = dn * gain
    inner = jnp.sum(scaled * uv, axis=1, keepdims=True)
    return (
        above.astype(F32) + s * scaled - uv * (s * s * s * inner / width),
        jnp.sum(dn * uv * s, axis=0, keepdims=True),
    )


def body_tile(normed, g_in, yn, go, half, i):
    left, right = (yn, go) if normed is None else (normed, g_in)
    wide = yn.shape[1]
    at = pl.ds(pl.multiple_of(half * wide, wide), wide)
    return dot(left[:, i * 256 : (i + 1) * 256], right[:, at], TN)


def body_halves(make, out, sent, got, send, recv):
    layer = lax.axis_index("section")
    copies = []
    for i in range(out.shape[0] // 256):
        at = pl.ds(i * 256, 256)
        sent[at, :] = make(1 - layer, i).astype(BF)
        copies.append(push(sent.at[at], got.at[at], send.at[i], recv.at[i], {"section": 1 - layer}))
    for i in range(out.shape[0] // 256):
        out[i * 256 : (i + 1) * 256, :] = make(layer, i).astype(BF)
    return copies


def add_halves(copies, out, got):
    for i, copy in enumerate(copies):
        at = slice(i * 256, (i + 1) * 256)
        copy.wait()
        out[at, :] = (out[at, :].astype(F32) + got[at, :].astype(F32)).astype(BF)


def head_bwd_kernel(size, g_in, w_in, upper, u, block, w_out, normed, yn, du_o, mine_o, grad_o, dyn_o, body_o,
                    out, got, body_send, body_got, send, recv, body_ss, body_rs):
    rows = u.shape[0] // size
    gain = norm_gain_of(block, u.shape[1])
    me, peers = greet(size, core=True)
    copies = []
    for d, peer in enumerate(peers):
        to = lax.rem(me + d + 1, size)
        out[d] = dot(g_in[block_of(to, rows), :], w_in[...], NT).astype(BF)
        copies.append(push(out.at[d], got.at[d], send.at[0, d], recv.at[0, d], peer))
    mine = block_of(me, rows)
    dn = dot(g_in[mine, :], w_in[...], NT)
    make = lambda which, i: body_tile(normed, g_in, yn, upper, which, i)
    body = body_halves(make, body_o, body_send, body_got, body_ss, body_rs)
    for copy in copies:
        copy.wait()
    for d in range(size - 1):
        dn = dn + got[d].astype(F32)
    du, grad = input_gradient(dn, u[mine, :], gain[...], upper[mine, :])
    grad_o[...] = jnp.broadcast_to(grad, grad_o.shape)
    mine_o[...] = du
    du_o[mine, :] = du.astype(BF)
    copies = [
        push(du_o.at[mine], du_o.at[mine], send.at[1, d], recv.at[1, d], peer) for d, peer in enumerate(peers)
    ]
    add_halves(body, body_o, body_got)
    dyn_o[mine, :] = dot(du_o[mine, :], w_out[...], NT)
    for d, copy in enumerate(copies):
        copy.wait_recv()
        at = block_of(lax.rem(me + size - d - 1, size), rows)
        dyn_o[at, :] = dot(du_o[at, :], w_out[...], NT)
    for copy in copies:
        copy.wait_send()


def head_bwd(g_in, w_in, upper, u, gain, w_out, normed, yn, size):
    n, d_model = u.shape
    inner = yn.shape[1]
    rows = n // size
    tiles = d_model // 256
    body = (d_model, d_model // 2)
    vm = pl.BlockSpec(memory_space=pltpu.VMEM)
    return pl.pallas_call(
        functools.partial(head_bwd_kernel, size),
        out_shape=(
            shape((n, d_model), BF),
            shape((rows, d_model), F32),
            shape((8, d_model), F32),
            shape((n, inner), F32),
            shape(body, BF),
        ),
        in_specs=[vm] * 8,
        out_specs=(vm,) * 5,
        scratch_shapes=[
            pltpu.VMEM((size - 1, rows, d_model), BF),
            pltpu.VMEM((size - 1, rows, d_model), BF),
            pltpu.VMEM(body, BF),
            pltpu.VMEM(body, BF),
            pltpu.SemaphoreType.DMA((2, size - 1)),
            pltpu.SemaphoreType.DMA((2, size - 1)),
            pltpu.SemaphoreType.DMA((tiles,)),
            pltpu.SemaphoreType.DMA((tiles,)),
        ],
        compiler_params=pltpu.CompilerParams(
            collective_id=5, has_side_effects=True, vmem_limit_bytes=VMEM_LIMIT
        ),
        name="head_bwd",
    )(g_in, w_in, upper, u, gain, w_out, normed, yn)


class Collect:
    def __init__(self, by_rows, size, rows, whole, out, local, send, recv):
        self.by_rows, self.size = by_rows, size
        self.rows, self.whole, self.out = rows, whole, out
        self.local, self.send, self.recv = local, send, recv
        self.core, self.head = lax.axis_index("section"), lax.axis_index("head")
        count = rows.shape[0]
        self.row_part = pl.ds(pl.multiple_of(self.core * whole.shape[0] + self.head * count, count), count)
        self.whole_part = block_of(self.core, whole.shape[0])

    def greeted(self):
        return [
            {"section": lax.rem(self.core + c, 2), "head": lax.rem(self.head + d, self.size)}
            for c in range(2)
            for d in range(self.size)
            if c or d
        ]

    def row_copy(self, sender, d):
        return pltpu.make_async_remote_copy(
            src_ref=self.rows, dst_ref=self.out.at[self.row_part],
            send_sem=self.send.at[d], recv_sem=self.recv.at[sender * self.size + d],
            device_id={"section": self.by_rows, "head": lax.rem(self.head + d, self.size)}, device_id_type=MESH,
        )

    def whole_copy(self):
        return pltpu.make_async_remote_copy(
            src_ref=self.whole, dst_ref=self.out.at[self.whole_part],
            send_sem=self.send.at[self.size], recv_sem=self.recv.at[2 * self.size],
            device_id={"section": 1 - self.by_rows}, device_id_type=MESH,
        )

    def start(self):
        @pl.when(self.core == self.by_rows)
        def _():
            pltpu.make_async_copy(self.rows, self.out.at[self.row_part], self.local).start()
            for d in range(1, self.size):
                self.row_copy(self.by_rows, d).start()
            self.whole_copy().start()

        @pl.when(self.core != self.by_rows)
        def _():
            pltpu.make_async_copy(self.whole, self.out.at[self.whole_part], self.local).start()
            for d in range(self.size):
                self.row_copy(1 - self.by_rows, d).start()

    def finish(self):
        @pl.when(self.core == self.by_rows)
        def _():
            pltpu.make_async_copy(self.rows, self.out.at[self.row_part], self.local).wait()
            for d in range(1, self.size):
                self.row_copy(self.by_rows, d).wait()
            for d in range(self.size):
                self.row_copy(1 - self.by_rows, d).wait_recv()
            self.whole_copy().wait_send()

        @pl.when(self.core != self.by_rows)
        def _():
            pltpu.make_async_copy(self.whole, self.out.at[self.whole_part], self.local).wait()
            for d in range(self.size):
                self.row_copy(1 - self.by_rows, d).wait_send()
            self.whole_copy().wait_recv()


def collect_sems(size):
    return [
        pltpu.SemaphoreType.DMA,
        pltpu.SemaphoreType.DMA((size + 1,)),
        pltpu.SemaphoreType.DMA((2 * size + 1,)),
    ]


OWN = 32
SHARED = 160
PIECE = 96
TAIL = (OWN + SHARED) // PIECE
LATE = 4
FEW = 16


def grad_tail_kernel(dims, normed, g_in, conv, scalars, gate, gain, tail, few):
    heads, inner, states = dims
    half = normed.shape[1] // 2
    split = 2 * inner + 2 * states
    rest = dot(g_in[:, 2 * inner :], normed[...], TN).astype(BF)
    step = (tail.shape[0] - OWN) // 2
    tail[...] = jnp.zeros_like(tail)
    for i in range(2):
        lanes = slice(i * half, (i + 1) * half)
        tail[i * OWN // 2 : (i + 1) * OWN // 2, :] = rest[2 * states : 2 * states + OWN // 2, lanes]
        tail[OWN + i * step : OWN + i * step + 2 * states, :] = rest[: 2 * states, lanes]
    conv_sum, scalar_sum, gate_sum = conv[0], scalars[0], gate[0]
    for i in range(1, conv.shape[0]):
        conv_sum, scalar_sum, gate_sum = conv_sum + conv[i], scalar_sum + scalars[i], gate_sum + gate[i]
    few[...] = jnp.zeros_like(few)
    few[0:5, :] = conv_sum[0:5, :inner]
    few[5:6, :] = gate_sum[0:1]
    for i in range(3):
        few[6:7, i * LANES : (i + 1) * LANES] = scalar_sum[i : i + 1]
    few[8:9, :] = gain[0:1, :half]
    few[9:10, :] = gain[0:1, half:]
    few[10:15, 0 : 2 * states] = conv_sum[0:5, inner:]


def grad_tail(normed, g_in, conv, scalars, gate, gain, dims, head_size):
    heads, inner, states = dims
    width = normed.shape[1]
    vm = pl.BlockSpec(memory_space=pltpu.VMEM)
    return pl.pallas_call(
        functools.partial(grad_tail_kernel, dims),
        out_shape=(shape((OWN + head_size * SHARED, width // 2), BF), shape((FEW, width // 2), F32)),
        in_specs=[vm] * 6,
        out_specs=(vm, vm),
        compiler_params=pltpu.CompilerParams(vmem_limit_bytes=VMEM_LIMIT),
        name="grad_tail",
    )(normed, g_in, conv, scalars, gate, gain)


def grad_sum_kernel(size, heads, skew, g_in, w_in, above, u, block, normed, yn, go, body1, tail0, tail1, few0, few1, done, done_out,
                    first_o, second_o, tail_o, shared_o, few_o, du_o,
                    own, core, got, out, shared, shared_core, shared_got, few_core, few_seq, few_head,
                    body_send, body_own, du_out, du_got, du_rows, few_mine,
                    cs, cr, rs, rr, bs, br, ts, tr, ls, hs, hr, xs, fs, fr, gs, gr, ds, dr, c_local, c_send, c_recv):
    me, layer, head = lax.axis_index("seq"), lax.axis_index("section"), lax.axis_index("head")
    half = out.shape[0] // 2
    parts = half // PIECE
    total0 = body_own.shape[0]
    early = done.shape[0]
    cut = (parts - LATE) * PIECE
    far = size - 1
    up, down, other = {"seq": me + 1}, {"seq": me - 1}, {"section": 1 - layer}
    peers = [{"head": lax.rem(head + d, heads)} for d in range(1, heads)]
    blocks = [{"seq": lax.rem(me + d, size)} for d in range(1, size)]
    low_end, high_end = me == 0, me == size - 1
    barrier = pltpu.get_barrier_semaphore()
    inputs = Collect(0, heads, du_rows, go, du_o, c_local, c_send, c_recv)
    plane = inputs.greeted()
    for peer in plane + blocks:
        pl.semaphore_signal(barrier, inc=1, device_id=peer, device_id_type=MESH)
    pl.semaphore_wait(barrier, len(plane) + len(blocks))

    late = [
        pltpu.make_async_copy(
            body1.at[pl.ds(early + side * LATE * PIECE, LATE * PIECE)],
            own.at[pl.ds(side * half, LATE * PIECE)],
            xs.at[7 + side],
        )
        for side in range(2)
    ]
    for copy in late:
        copy.start()

    ready = [(done, pl.ds(0, early)), (done_out, pl.ds(normed.shape[1], done_out.shape[0]))]
    given = [
        pltpu.make_async_remote_copy(
            src_ref=src, dst_ref=first_o.at[at], send_sem=xs.at[9 + i], recv_sem=xs.at[5 + i],
            device_id=other, device_id_type=MESH,
        )
        for i, (src, at) in enumerate(ready)
    ]
    kept = [pltpu.make_async_copy(src, second_o.at[at], xs.at[9 + i]) for i, (src, at) in enumerate(ready)]

    def all_of(copies, act):
        for copy in copies:
            act(copy)

    pl.when(layer == 0)(lambda: all_of(given, lambda copy: copy.start()))
    pl.when(layer == 1)(lambda: all_of(kept, lambda copy: copy.start()))

    def fetch_tail(ours, others):
        return (
            pltpu.make_async_copy(ours, shared, xs.at[0]),
            pltpu.make_async_remote_copy(
                src_ref=others, dst_ref=shared_core, send_sem=xs.at[1], recv_sem=xs.at[2],
                device_id=other, device_id_type=MESH,
            ),
        )

    def start_all(copies):
        for copy in copies:
            copy.start()

    pl.when(layer == 0)(lambda: start_all(fetch_tail(tail0, tail1)))
    pl.when(layer == 1)(lambda: start_all(fetch_tail(tail1, tail0)))

    rows_here = u.shape[0] // heads
    du_copy = lambda d: pltpu.make_async_remote_copy(
        src_ref=du_out.at[d], dst_ref=du_got.at[d], send_sem=ds.at[d], recv_sem=dr.at[d],
        device_id=peers[d], device_id_type=MESH,
    )

    def few_to_core(src):
        return pltpu.make_async_remote_copy(
            src_ref=src, dst_ref=few_core, send_sem=xs.at[3], recv_sem=xs.at[4],
            device_id=other, device_id_type=MESH,
        )

    few_to_seq = lambda d: pltpu.make_async_remote_copy(
        src_ref=few_seq.at[me], dst_ref=few_seq.at[me], send_sem=fs.at[d], recv_sem=fr.at[d],
        device_id=blocks[d], device_id_type=MESH,
    )
    few_to_head = lambda d: pltpu.make_async_remote_copy(
        src_ref=few_head.at[head], dst_ref=few_head.at[head], send_sem=gs.at[d], recv_sem=gr.at[d],
        device_id=peers[d], device_id_type=MESH,
    )
    shared_block = lambda i: pl.ds(pl.multiple_of(OWN + i * SHARED, 32), SHARED)
    scatter = lambda d: pltpu.make_async_remote_copy(
        src_ref=shared.at[shared_block(lax.rem(head + d + 1, heads))], dst_ref=shared_got.at[d],
        send_sem=hs.at[0, d], recv_sem=hr.at[0, d], device_id=peers[d], device_id_type=MESH,
    )
    gather = lambda d: pltpu.make_async_remote_copy(
        src_ref=shared_o.at[head], dst_ref=shared_o.at[head],
        send_sem=hs.at[1, d], recv_sem=hr.at[1, d], device_id=peers[d], device_id_type=MESH,
    )

    for copy in fetch_tail(tail0, tail1):
        copy.wait()
    shared[...] = (shared[...].astype(F32) + shared_core[...].astype(F32)).astype(BF)
    for d in range(heads - 1):
        scatter(d).start()
    for d in range(heads - 1):
        to = block_of(lax.rem(head + d + 1, heads), rows_here)
        du_out[d] = dot(g_in[to, :], w_in[...], NT).astype(BF)
        du_copy(d).start()

    tile = 256
    in_tiles = normed.shape[1] // tile
    tiles = total0 // tile

    def body_copy(i):
        at = block_of(i, tile)
        return pltpu.make_async_remote_copy(
            src_ref=body_send.at[at], dst_ref=core.at[at], send_sem=cs.at[i], recv_sem=cr.at[i],
            device_id=other, device_id_type=MESH,
        )

    def make_tile(i, left, right):
        at = block_of(i, tile)
        wide = yn.shape[1]
        for which, target in ((1 - layer, body_send), (layer, body_own)):
            columns = pl.ds(pl.multiple_of(which * wide, wide), wide)
            target[at, :] = dot(left, right[:, columns], TN).astype(BF)
        body_copy(i).start()

    place = lambda side, p: pl.ds(pl.multiple_of(side * half + p * PIECE, PIECE), PIECE)
    is_late = lambda p: p < LATE
    is_tail = lambda side, p: jnp.logical_and(side == 1, jnp.logical_and(p >= LATE, p < LATE + TAIL))
    start0 = lambda side, p: (p - LATE) * PIECE + (cut - TAIL * PIECE) * side
    start1 = lambda side, p: early + side * LATE * PIECE + p * PIECE

    def sending(side, p, back, source):
        at = place(side, p)
        towards = down if (side == 0) != back else up
        target, send, recv = (out, bs, br) if back else (got, rs, rr)
        return pltpu.make_async_remote_copy(
            src_ref=source.at[at], dst_ref=target.at[at], send_sem=send.at[side, p],
            recv_sem=recv.at[side, p], device_id=towards, device_id_type=MESH,
        )

    def give(side, p, target, at):
        return pltpu.make_async_remote_copy(
            src_ref=out.at[place(side, p)], dst_ref=target.at[at], send_sem=ts.at[side, p],
            recv_sem=tr.at[side, p], device_id=other, device_id_type=MESH,
        )

    def keep(side, p, target, at):
        return pltpu.make_async_copy(out.at[place(side, p)], target.at[at], ls.at[side, p])

    def final(side, p, act_keep, act_give):
        at0 = lambda: pl.ds(pl.multiple_of(start0(side, p), PIECE), PIECE)
        at1 = lambda: pl.ds(pl.multiple_of(start1(side, p), PIECE), PIECE)
        late_piece = is_late(p)
        body0 = jnp.logical_not(jnp.logical_or(late_piece, is_tail(side, p)))
        pl.when(jnp.logical_and(body0, layer == 0))(lambda: act_keep(keep(side, p, first_o, at0())))
        pl.when(jnp.logical_and(body0, layer == 1))(lambda: act_give(give(side, p, second_o, at0())))
        pl.when(jnp.logical_and(late_piece, layer == 0))(lambda: act_give(give(side, p, first_o, at1())))
        pl.when(jnp.logical_and(late_piece, layer == 1))(lambda: act_keep(keep(side, p, second_o, at1())))

    begin = lambda copy: copy.start()

    def reduce(side, p):
        start, end = (high_end, low_end) if side == 0 else (low_end, high_end)
        at = place(side, p)

        @pl.when(jnp.logical_not(jnp.logical_or(is_late(p), is_tail(side, p))))
        def _():
            mine = pl.ds(pl.multiple_of(start0(side, p), PIECE), PIECE)
            own[at, :] = (body_own[mine, :].astype(F32) + core[mine, :].astype(F32)).astype(BF)

        @pl.when(start)
        def _():
            sending(side, p, False, own).start()

        @pl.when(jnp.logical_not(start))
        def _():
            sending(side, p, False, got).wait_recv()
            summed = (own[at, :].astype(F32) + got[at, :].astype(F32)).astype(BF)

            @pl.when(end)
            def _():
                out[at, :] = summed
                sending(side, p, True, out).start()
                final(side, p, begin, begin)

            @pl.when(jnp.logical_not(end))
            def _():
                got[at, :] = summed
                sending(side, p, False, got).start()

    def back(side, p):
        start, end = (high_end, low_end) if side == 0 else (low_end, high_end)

        @pl.when(jnp.logical_not(end))
        def _():
            sending(side, p, True, out).wait_recv()

            @pl.when(jnp.logical_not(start))
            def _():
                sending(side, p, True, out).start()

            final(side, p, begin, begin)

    def guarded(act, side, p):
        @pl.when(jnp.logical_and(p >= 0, p < parts))
        def _():
            act(side, p)

    tail_at = half + LATE * PIECE
    finished = LATE + TAIL + skew * (2 * far - me)
    for copy in late:
        copy.wait()

    def step(t, _):
        def one_tile(k, _):
            i = 2 * t + k

            @pl.when(i < in_tiles)
            def _():
                make_tile(i, normed[:, block_of(i, tile)], g_in)

            @pl.when(jnp.logical_and(i >= in_tiles, i < tiles))
            def _():
                make_tile(i, yn[:, block_of(i - in_tiles, tile)], go)

            pl.when(jnp.logical_and(i >= 2, i < tiles + 2))(lambda: body_copy(i - 2).wait())
            return 0

        lax.fori_loop(0, 2, one_tile, 0)

        @pl.when(t == 5)
        def _():
            here = block_of(head, rows_here)
            dn = dot(g_in[here, :], w_in[...], NT)
            for d in range(heads - 1):
                du_copy(d).wait()
                dn = dn + du_got[d].astype(F32)
            du, grad = input_gradient(dn, u[here, :], norm_gain_of(block, u.shape[1])[...], above[...])
            du_rows[...] = du.astype(BF)
            inputs.start()
            few_mine[...] = few0[...]
            wide = few0.shape[1]
            for i in range(2):
                few_mine[8 + i : 9 + i, :] = grad[:, i * wide : (i + 1) * wide]
            pl.when(layer == 0)(lambda: few_to_core(few1).start())
            pl.when(layer == 1)(lambda: few_to_core(few_mine).start())

        @pl.when(t == 7)
        def _():
            few_to_core(few_mine).wait()
            pl.when(layer == 0)(lambda: few_seq.__setitem__(me, few_mine[...] + few_core[...]))
            pl.when(layer == 1)(lambda: few_seq.__setitem__(me, few1[...] + few_core[...]))
            for d in range(size - 1):
                few_to_seq(d).start()

        @pl.when(t == 11)
        def _():
            for d in range(size - 1):
                few_to_seq(d).wait()
            total = few_seq[0]
            for i in range(1, size):
                total = total + few_seq[i]
            few_o[0 : FEW // 2, :] = total[0 : FEW // 2]
            few_head[head] = total[FEW // 2 :]
            for d in range(heads - 1):
                few_to_head(d).start()

        @pl.when(t == 16)
        def _():
            for d in range(heads - 1):
                few_to_head(d).wait()
            total = few_head[0]
            for i in range(1, heads):
                total = total + few_head[i]
            few_o[FEW // 2 :, :] = total

        @pl.when(t == 4)
        def _():
            total = shared[shared_block(head), :].astype(F32)
            for d in range(heads - 1):
                scatter(d).wait()
                total = total + shared_got[d].astype(F32)
            own[tail_at + OWN : tail_at + OWN + SHARED, :] = total.astype(BF)
            own[tail_at : tail_at + OWN, :] = shared[0:OWN, :]

        guarded(reduce, 0, t - skew * (far - me))
        guarded(reduce, 1, t - skew * me)
        guarded(back, 0, t - skew * (far + me))
        guarded(back, 1, t - skew * (2 * far - me))

        @pl.when(t == finished)
        def _():
            tail_o[...] = out[tail_at : tail_at + OWN, :]
            shared_o[head] = out[tail_at + OWN : tail_at + OWN + SHARED, :]
            for d in range(heads - 1):
                gather(d).start()

        return 0

    lax.fori_loop(0, parts + 2 * skew * far, step, 0)

    def drain(p, _):
        for side in range(2):
            start, end = (high_end, low_end) if side == 0 else (low_end, high_end)

            @pl.when(jnp.logical_not(end))
            def _():
                sending(side, p, False, got).wait_send()

            @pl.when(jnp.logical_not(start))
            def _():
                sending(side, p, True, out).wait_send()

            final(side, p, lambda copy: copy.wait(), lambda copy: copy.wait_send())
            final(side, p, lambda copy: give(side, p, first_o, pl.ds(0, PIECE)).wait_recv(), lambda copy: None)
        return 0

    lax.fori_loop(0, parts, drain, 0)
    for d in range(heads - 1):
        gather(d).wait()
    pl.when(layer == 0)(lambda: all_of(given, lambda copy: copy.wait_send()))
    pl.when(layer == 1)(lambda: all_of(kept, lambda copy: copy.wait()))
    pl.when(layer == 1)(lambda: all_of(given, lambda copy: copy.wait_recv()))

    inputs.finish()


def grad_sum(layer0, body1, tails, fews, done, size, heads, skew=1):
    width = body1.shape[1]
    total = body1.shape[0] + done[1].shape[0]
    n, d_model = layer0[3].shape
    half = LATE * PIECE + (total + OWN + SHARED) // 2
    parts = half // PIECE
    vm = pl.BlockSpec(memory_space=pltpu.VMEM)
    anywhere = pl.BlockSpec(memory_space=pl.ANY)
    pair = pltpu.SemaphoreType.DMA((2, parts))
    sems = lambda *k: pltpu.SemaphoreType.DMA(k)
    tiles = total // 256
    big = pltpu.VMEM((2 * half, width), BF)
    body = pltpu.VMEM((total, width), BF)
    return pl.pallas_call(
        functools.partial(grad_sum_kernel, size, heads, skew),
        out_shape=(
            shape((total, width), BF),
            shape((total, width), BF),
            shape((OWN, width), BF),
            shape((heads, SHARED, width), BF),
            shape((FEW, width), F32),
            shape((2 * n, d_model), BF),
        ),
        in_specs=[vm] * 8 + [anywhere] * 3 + [vm] * 2 + [anywhere] * 2,
        out_specs=(anywhere, anywhere, vm, vm, vm, anywhere),
        scratch_shapes=[big, body, big, big]
        + [pltpu.VMEM((OWN + heads * SHARED, width), BF) for _ in range(2)]
        + [pltpu.VMEM((heads - 1, SHARED, width), BF)]
        + [pltpu.VMEM((FEW, width), F32), pltpu.VMEM((size, FEW, width), F32)]
        + [pltpu.VMEM((heads, FEW // 2, width), F32)]
        + [body] * 2
        + [pltpu.VMEM((heads - 1, n // heads, d_model), BF) for _ in range(2)]
        + [pltpu.VMEM((n // heads, d_model), BF), pltpu.VMEM((FEW, width), F32)]
        + [sems(tiles)] * 2
        + [pair] * 7
        + [sems(2, heads - 1)] * 2
        + [sems(11)]
        + [sems(size - 1)] * 2
        + [sems(heads - 1)] * 4
        + collect_sems(heads),
        compiler_params=pltpu.CompilerParams(
            collective_id=8, has_side_effects=True, vmem_limit_bytes=VMEM_LIMIT
        ),
        name="grad_sum",
    )(*layer0, body1, *tails, *fews, *done)


def unpack_kernel(dims, first, second, first_low, second_low, own, shared, few,
                  z_o, x_o, out_o, bc_o, dt_o, conv_o, conv_bias_o, bc_conv_o, bc_bias_o,
                  dt_bias_o, a_log_o, skip_o, gate_o, gain_o):
    heads, inner, states = dims
    half = own.shape[1]
    z_o[...] = first[...].astype(F32)
    x_o[...] = second[...].astype(F32)
    out_o[:, :half] = first_low[...].astype(F32)
    out_o[:, half:] = second_low[...].astype(F32)

    @pl.when(pl.program_id(0) == 0)
    def _():
        blocks = jnp.concatenate([shared[i] for i in range(shared.shape[0])], axis=0)
        step = blocks.shape[0] // 2
        for i in range(2):
            rows = slice(i * half, (i + 1) * half)
            bc_o[rows, :] = jnp.transpose(blocks[i * step : i * step + 2 * states].astype(F32))
            dts = own[i * OWN // 2 : (i + 1) * OWN // 2, :].astype(F32)
            dts = jnp.concatenate([dts, jnp.zeros((LANES - OWN // 2, half), F32)], axis=0)
            dt_o[rows, :] = jnp.transpose(dts)[:, :heads]
            gain_o[:, rows] = few[8 + i : 9 + i, :]
        conv_o[...] = few[0:4, :]
        conv_bias_o[...] = few[4:5, :]
        gate_o[...] = few[5:6, :]
        bc_conv_o[...] = few[10:14, 0 : 2 * states]
        bc_bias_o[...] = few[14:15, 0 : 2 * states]
        dt_bias_o[...] = few[6:7, 0:heads]
        a_log_o[...] = few[6:7, LANES : LANES + heads]
        skip_o[...] = few[6:7, 2 * LANES : 2 * LANES + heads]


def unpack(first, second, own, shared, few, dims, steps=6):
    heads, inner, states = dims
    half = first.shape[1]
    width = 2 * half
    tall, low = width // steps, inner // steps
    upper = pl.BlockSpec((tall, half), lambda i: (i, 0))
    lower = pl.BlockSpec((low, half), lambda i: (width // low + i, 0))
    whole = lambda a: pl.BlockSpec(a.shape, lambda i: (0,) * len(a.shape))
    outs = [
        ((width, inner), (tall, inner)),
        ((width, inner), (tall, inner)),
        ((inner, width), (low, width)),
    ]
    fixed = [
        (width, 2 * states), (width, heads), (4, inner), (1, inner), (4, 2 * states), (1, 2 * states),
        (1, heads), (1, heads), (1, heads), (1, inner), (1, width),
    ]
    return pl.pallas_call(
        functools.partial(unpack_kernel, dims),
        grid=(steps,),
        out_shape=[shape(a, F32) for a, _ in outs] + [shape(a, F32) for a in fixed],
        in_specs=[upper] * 2 + [lower] * 2 + [whole(own), whole(shared), whole(few)],
        out_specs=[pl.BlockSpec(b, lambda i: (i, 0)) for _, b in outs]
        + [pl.BlockSpec(a, lambda i: (0, 0)) for a in fixed],
        compiler_params=pltpu.CompilerParams(vmem_limit_bytes=VMEM_LIMIT),
        name="unpack",
    )(first, second, first, second, own, shared, few)


def normalise(u, gain):
    uv = u.astype(F32)
    s = lax.rsqrt(jnp.mean(uv * uv, axis=-1, keepdims=True) + EPSILON)
    return (uv * s * gain).astype(BF)


def on_device(
    inputs, cotangent, norm_gain, w_z, w_x, w_bc, w_dt, conv_x, conv_x_bias, conv_bc, conv_bc_bias,
    dt_bias, a_log, d_skip, gate_gain, w_out,
):
    me = lax.axis_index("section")
    seq_size, head_size = lax.axis_size("seq"), lax.axis_size("head")
    micro, n, d_model = inputs.shape
    batch = micro // 2
    tokens = batch * n
    inner, heads, states = w_z.shape[2], w_dt.shape[2], w_bc.shape[2] // 2
    wide = inner + 2 * states
    full = inner * head_size
    dims = (heads, inner, states)
    pad_heads = lambda a: jnp.pad(a, ((0, 0),) * (a.ndim - 1) + ((0, LANES - heads),))

    taps_x = jnp.concatenate([conv_x[0], conv_x_bias, jnp.zeros((3, inner), F32)], axis=0)
    taps_bc = jnp.concatenate([conv_bc[0], conv_bc_bias, jnp.zeros((3, 2 * states), F32)], axis=0)
    taps = jnp.concatenate([taps_x, taps_bc], axis=1)
    scalars = pad_heads(jnp.concatenate([dt_bias, -jnp.exp(a_log)], axis=0)).reshape(1, -1)
    vectors = jnp.concatenate(
        [
            jnp.repeat(d_skip[0], inner // heads)[None],
            gate_gain,
            jnp.pad(scalars, ((0, 0), (0, inner - 2 * LANES))),
            jnp.zeros((5, inner), F32),
        ],
        axis=0,
    )
    gains = jnp.broadcast_to(norm_gain, (8, d_model))
    w_in0, w_out0, block0, w_in1, w_out1, block1 = both_layers(
        [[w_z[0], w_x[0], w_bc[0], pad_heads(w_dt[0])], [w_out[0]], [taps, vectors, gains]]
    )

    u = lax.dynamic_slice_in_dim(inputs, me * batch, batch, 0).reshape(tokens, d_model)
    cot = lax.dynamic_slice_in_dim(cotangent, me * batch, batch, 0).reshape(tokens, d_model)

    flat = lambda a: a.reshape(tokens, -1)
    stacked = lambda a: a.reshape(batch, n, -1)

    normed0 = normalise(u, block0[0:1, block0.shape[1] - d_model :])
    proj0 = stacked(dot(normed0, w_in0))
    cx0, dt0, cum0, state0, halo0, y0, yn0, stats0 = ssd_fwd(
        proj0, block0, None, dims, seq_size, head_size, full
    )
    h0, normed1, proj1 = head_fwd(flat(yn0), w_out0, u, head_size, [w_in1, block1])
    proj1 = stacked(proj1)
    dyn1 = stacked(dot(cot, w_out1, NT))
    cx1, dt1, cum1, state1, halo1, y1, yn1, stats1 = ssd_fwd(
        proj1, block1, dyn1, dims, seq_size, head_size, full
    )
    h1_rows, body1_out = head_fwd(flat(yn1), w_out1, h0, head_size, [], cot)

    g_in1, gate1, conv1, small1, layer_outputs = ssd_bwd(
        dyn1, y1, proj1, halo1, cx1, dt1, cum1, state1, stats1, block1, [h1_rows, h0],
        dims, seq_size, head_size, full,
    )
    g_in1, body1_out = lax.optimization_barrier((flat(g_in1), body1_out))
    done_out = lax.psum(body1_out, "seq")
    du1, du1_rows, gain1, dyn0, body1 = head_bwd(
        g_in1, w_in1, cot, h0, block1, w_out0, normed1, flat(yn1), head_size
    )
    body1_early, done_out = lax.optimization_barrier((body1[: d_model - 2 * LATE * PIECE], done_out))
    done = lax.psum(body1_early, "seq")
    tail1, few1 = grad_tail(normed1, g_in1, conv1, small1, gate1, gain1, dims, head_size)
    g_in0, gate0, conv0, small0 = ssd_bwd(
        stacked(dyn0), y0, proj0, halo0, cx0, dt0, cum0, state0, stats0, block0, [],
        dims, seq_size, head_size, full,
    )
    g_in0 = flat(g_in0)
    tail0, few0 = grad_tail(normed0, g_in0, conv0, small0, gate0, jnp.zeros_like(gain1), dims, head_size)
    first, second, own, shared, few, input_grads = grad_sum(
        (g_in0, w_in0, du1_rows, u, block0, normed0, flat(yn0), du1),
        body1, (tail0, tail1), (few0, few1), (done, done_out), seq_size, head_size,
    )
    g_z, g_x, g_out, g_bc, g_dt, g_conv, g_conv_bias, g_bc_conv, g_bc_bias, *scalars, g_gate, g_gain = unpack(
        first, second, own, shared, few, dims
    )

    return (
        layer_outputs.reshape(1, micro, n, d_model),
        input_grads.reshape(1, micro, n, d_model),
        g_gain,
        g_z[None],
        g_x[None],
        g_bc[None],
        g_dt[None],
        g_conv[None],
        g_conv_bias,
        g_bc_conv[None],
        g_bc_bias,
        *scalars,
        g_gate,
        g_out[None],
    )


def solution(mesh):
    in_specs = (
        P(None, "seq", None),
        P(None, "seq", None),
        P("section", None),
        P("section", None, "head"),
        P("section", None, "head"),
        P("section", None, None),
        P("section", None, "head"),
        P("section", None, "head"),
        P("section", "head"),
        P("section", None, None),
        P("section", None),
        P("section", "head"),
        P("section", "head"),
        P("section", "head"),
        P("section", "head"),
        P("section", "head", None),
    )
    out_specs = (
        P("section", None, "seq", None),
        P("section", None, "seq", None),
        P("section", None),
        P("section", None, "head"),
        P("section", None, "head"),
        P("section", None, None),
        P("section", None, "head"),
        P("section", None, "head"),
        P("section", "head"),
        P("section", None, None),
        P("section", None),
        P("section", "head"),
        P("section", "head"),
        P("section", "head"),
        P("section", "head"),
        P("section", "head", None),
    )
    return jax.shard_map(
        on_device, mesh=mesh, in_specs=in_specs, out_specs=out_specs, check_vma=False
    )
```

```python
import functools

import jax
import jax.numpy as jnp
from jax import lax
from jax.experimental import pallas as pl
from jax.experimental.pallas import tpu as pltpu
from jax.sharding import PartitionSpec as P

EPSILON = 1e-05
MESH = pl.DeviceIdType.MESH
HIGH = lax.Precision.HIGHEST
BF = jnp.bfloat16
F32 = jnp.float32
LANES = 128
VMEM_LIMIT = 56 * 2**20


def shape(dims, kind):
    return jax.ShapeDtypeStruct(dims, kind)


def dot(a, b, dims=((1,), (0,)), precision=None):
    return lax.dot_general(a, b, (dims, ((), ())), precision=precision, preferred_element_type=F32)


NT = ((1,), (1,))
TN = ((0,), (0,))


def halves(v):
    high = v.astype(BF)
    return high, (v - high.astype(F32)).astype(BF)


def dot_mask(v, mask, dims=((1,), (0,))):
    high, rest = halves(v)
    return dot(high, mask, dims) + dot(rest, mask, dims)


def dot3(a, b, dims=((1,), (0,))):
    a_high, a_rest = halves(a)
    b_high, b_rest = halves(b)
    return dot(a_high, b_high, dims) + dot(a_rest, b_high, dims) + dot(a_high, b_rest, dims)


def mask_dot(mask, v):
    high, rest = halves(v)
    return dot(mask, high) + dot(mask, rest)


def head_mask(width, heads):
    size = width // heads
    return (
        lax.broadcasted_iota(jnp.int32, (LANES, width), 0)
        == lax.broadcasted_iota(jnp.int32, (LANES, width), 1) // size
    ).astype(F32).astype(BF)


def order_mask(n, lower):
    rows = lax.broadcasted_iota(jnp.int32, (n, n), 0)
    columns = lax.broadcasted_iota(jnp.int32, (n, n), 1)
    return (rows >= columns) if lower else (rows <= columns)


def sigmoid(v):
    return 1.0 / (1.0 + jnp.exp(-v))


def softplus(v):
    return jnp.maximum(v, 0.0) + jnp.log1p(jnp.exp(-jnp.abs(v)))


def column(row_block):
    n = row_block.shape[1]
    return [
        jnp.transpose(jnp.broadcast_to(row_block[i : i + 1, :], (LANES, n))) for i in range(2)
    ]


def rows_of(columns):
    n = columns[0].shape[0]
    rows = [jnp.transpose(jnp.broadcast_to(c, (n, LANES)))[0:1] for c in columns]
    return jnp.concatenate(rows + [jnp.zeros((8 - len(rows), n), F32)], axis=0)


def conv_pre(ext, proj_xbc, halo, taps, bias):
    n = proj_xbc.shape[0]
    ext[0:8, :] = halo
    ext[8 : 8 + n, :] = proj_xbc
    pre = bias + taps[3:4, :] * proj_xbc
    for k in range(3):
        pre = pre + taps[k : k + 1, :] * ext[5 + k : 5 + k + n, :]
    return pre


def push(src, dst, send, recv, device):
    copy = pltpu.make_async_remote_copy(
        src_ref=src, dst_ref=dst, send_sem=send, recv_sem=recv, device_id=device, device_id_type=MESH
    )
    copy.start()
    return copy


def both_layers_kernel(places, *refs):
    count = len(places)
    groups = places[-1][0] + 1
    ins, outs = refs[:count], refs[count:-3]
    send, recv, local = refs[-3:]
    me = lax.axis_index("section")
    other = {"section": 1 - me}
    barrier = pltpu.get_barrier_semaphore()
    pl.semaphore_signal(barrier, inc=1, device_id=other, device_id_type=MESH)
    pl.semaphore_wait(barrier, 1)

    def copies(i, which, start, layer):
        target = outs[layer * groups + which].at[:, pl.ds(start, ins[i].shape[1])]
        return (
            pltpu.make_async_remote_copy(
                src_ref=ins[i], dst_ref=target, send_sem=send.at[i], recv_sem=recv.at[i],
                device_id=other, device_id_type=MESH,
            ),
            pltpu.make_async_copy(ins[i], target, local.at[i]),
        )

    for layer in range(2):

        @pl.when(me == layer)
        def _():
            for i, (which, start) in enumerate(places):
                for copy in copies(i, which, start, layer):
                    copy.start()

    for i, (which, start) in enumerate(places):
        for copy in copies(i, which, start, 0):
            copy.wait()


def both_layers(groups):
    places, flat, outs = [], [], []
    for i, group in enumerate(groups):
        start = 0
        for a in group:
            places.append((i, start))
            flat.append(a)
            start += a.shape[1]
        outs.append(shape((group[0].shape[0], start), group[0].dtype))
    count = len(flat)
    vm = pl.BlockSpec(memory_space=pltpu.VMEM)
    anywhere = pl.BlockSpec(memory_space=pl.ANY)
    return pl.pallas_call(
        functools.partial(both_layers_kernel, places),
        out_shape=tuple(outs) * 2,
        in_specs=[vm] * count,
        out_specs=(anywhere,) * (2 * len(outs)),
        scratch_shapes=[pltpu.SemaphoreType.DMA((count,)) for _ in range(3)],
        compiler_params=pltpu.CompilerParams(
            collective_id=0, has_side_effects=True, vmem_limit_bytes=VMEM_LIMIT
        ),
        name="both_layers",
    )(*flat)


def constants(block, dims):
    heads, inner, states = dims
    wide = inner + 2 * states
    return (
        block.at[0:4, 0:wide],
        block.at[4:5, 0:wide],
        block.at[2:3, wide : wide + LANES],
        block.at[2:3, wide + LANES : wide + 2 * LANES],
        block.at[0:1, wide : wide + inner],
        block.at[1:2, wide : wide + inner],
    )


def norm_gain_of(block, d_model):
    return block.at[0:1, block.shape[1] - d_model :]


class Line:
    def __init__(self, forward, size, parts, outgoing, incoming, send, recv):
        self.me = lax.axis_index("seq")
        self.size, self.parts = size, parts
        self.outgoing, self.incoming, self.send, self.recv = outgoing, incoming, send, recv
        first, last = self.me == 0, self.me == size - 1
        self.starts, self.ends = (first, last) if forward else (last, first)
        self.place = self.me if forward else size - 1 - self.me
        step = 1 if forward else -1
        self.target, self.source = {"seq": self.me + step}, {"seq": self.me - step}

    def greet(self, barrier):
        @pl.when(jnp.logical_not(self.starts))
        def _():
            pl.semaphore_signal(barrier, inc=1, device_id=self.source, device_id_type=MESH)

    def met(self, barrier, others=0):
        @pl.when(jnp.logical_not(self.ends))
        def _():
            pl.semaphore_wait(barrier, others + 1)

        if others:

            @pl.when(self.ends)
            def _():
                pl.semaphore_wait(barrier, others)

    def copy(self, m, p):
        width = self.outgoing.shape[2] // self.parts
        at = pl.ds(p * width, width)
        return pltpu.make_async_remote_copy(
            src_ref=self.outgoing.at[m, :, at],
            dst_ref=self.incoming.at[m, :, at],
            send_sem=self.send.at[m * self.parts + p],
            recv_sem=self.recv.at[m * self.parts + p],
            device_id=self.target,
            device_id_type=MESH,
        )

    def begin(self, m, own):
        @pl.when(self.starts)
        def _():
            self.incoming[m] = jnp.zeros_like(self.incoming[m])
            self.outgoing[m] = own.astype(self.outgoing.dtype)
            for p in range(self.parts):
                self.copy(m, p).start()

    def relay(self, own, decay, at_step, steps, lag, apart):
        width = self.outgoing.shape[2] // self.parts
        for i in range(self.outgoing.shape[0] * self.parts):
            m, p = i // self.parts, i % self.parts
            at = slice(p * width, (p + 1) * width)
            offset = apart * i // 2
            if at_step < steps - 1 and (at_step - offset < lag or (at_step - offset) % lag):
                continue
            due = jnp.minimum(self.place * lag + offset, steps - 1)

            @pl.when(jnp.logical_and(self.place > 0, due == at_step))
            def _():
                self.copy(m, p).wait_recv()

                @pl.when(jnp.logical_not(self.ends))
                def _():
                    passed = decay[m, 0:1, at] * self.incoming[m, :, at].astype(F32) + own[m, :, at]
                    self.outgoing[m, :, at] = passed.astype(self.outgoing.dtype)
                    self.copy(m, p).start()

    def finish(self):
        @pl.when(jnp.logical_not(self.ends))
        def _():
            for m in range(self.outgoing.shape[0]):
                for p in range(self.parts):
                    self.copy(m, p).wait_send()

    def halo(self, src, dst, m, send, recv):
        return pltpu.make_async_remote_copy(
            src_ref=src, dst_ref=dst, send_sem=send.at[m], recv_sem=recv.at[m],
            device_id=self.target, device_id_type=MESH,
        )


PARTS = 6


def ssd_fwd_kernel(dims, size, heads_axis, full, has_dyn, *refs):
    proj, block = refs[:2]
    taps, bias, dt_bias, a_neg, skip, gain = constants(block, dims)
    dyn = refs[2] if has_dyn else None
    (cx, dt_o, cum_o, state, halo, y_o, yn_o, stats_o,
     ext, own, decay, rim, outgoing, incoming, gates, square, square_got,
     send, recv, halo_send, halo_recv, stat_send, stat_recv) = refs[2 + has_dyn :]
    heads, inner, states = dims
    batch, n = proj.shape[0], proj.shape[1]
    wide = inner + 2 * states
    head_lanes = inner // heads
    columns = slice(inner, inner + wide)
    line = Line(True, size, PARTS, outgoing, incoming, send, recv)
    head = lax.axis_index("head")
    peers = [{"head": lax.rem(head + d, heads_axis)} for d in range(1, heads_axis)]
    barrier = pltpu.get_barrier_semaphore()
    line.greet(barrier)
    for peer in peers:
        pl.semaphore_signal(barrier, inc=1, device_id=peer, device_id_type=MESH)
    for m in range(batch):
        rim[m] = proj[m, n - 16 :, columns].astype(BF)
    line.met(barrier, len(peers))

    @pl.when(jnp.logical_not(line.ends))
    def _():
        for m in range(batch):
            line.halo(rim.at[m], halo.at[m], m, halo_send, halo_recv).start()

    @pl.when(line.starts)
    def _():
        halo[...] = jnp.zeros_like(halo)

    expand = head_mask(inner, heads)
    for m in range(batch):

        @pl.when(jnp.logical_not(line.starts))
        def _():
            line.halo(rim.at[m], halo.at[m], m, halo_send, halo_recv).wait_recv()

        xbc = proj[m, :, columns].astype(BF).astype(F32)
        pre = conv_pre(ext, xbc, halo[m, 8:].astype(F32), taps[...], bias[...])
        act = pre * sigmoid(pre)
        cx[m] = act
        dt = softplus(proj[m, :, inner + wide :] + dt_bias[...])
        cum = mask_dot(order_mask(n, True).astype(F32).astype(BF), dt * a_neg[...])
        dt_o[m] = dt
        cum_o[m] = cum
        last = cum[n - 1 : n, :]
        weight = dot_mask(jnp.exp(last - cum) * dt, expand)
        mine = dot3(act[:, inner : inner + states], act[:, :inner] * weight, TN)
        own[m] = mine
        decay[m] = dot_mask(jnp.broadcast_to(jnp.exp(last), (8, LANES)), expand)
        line.begin(m, mine)
    keep = order_mask(n, True)
    first = lax.broadcasted_iota(jnp.int32, (n, LANES), 1) < head_lanes
    pairs = heads // 2
    for m in range(batch):
        scores = dot3(cx[m, :, inner + states :], cx[m, :, inner : inner + states], NT)
        cums = cum_o[m]
        cums_t = jnp.transpose(cums)
        dt_wide = dot_mask(dt_o[m], expand)
        for p in range(pairs):

            line.relay(own, decay, m * pairs + p, batch * pairs, 4, 2)
            lanes = slice(p * LANES, (p + 1) * LANES)
            x = cx[m, :, lanes]
            dtx, dtx_rest = halves(x * dt_wide[:, lanes])
            both = []
            for h in (2 * p, 2 * p + 1):
                sums = []
                for low, high in ((0, n // 2), (n // 2, n)):
                    lag = cums[low:high, h : h + 1] - cums_t[h : h + 1, 0:high]
                    lag = jnp.where(keep[low:high, 0:high], lag, -1e30)
                    top, rest = halves(scores[low:high, 0:high] * jnp.exp(lag))
                    sums.append(dot(top, dtx[0:high]) + dot(rest, dtx[0:high]) + dot(top, dtx_rest[0:high]))
                both.append(jnp.concatenate(sums, axis=0))
            y_o[m, :, lanes] = skip[:, lanes] * x + jnp.where(first, both[0], both[1])
    for m in range(batch):
        entered = incoming[m]
        state[m] = entered
        y = y_o[m] + dot_mask(jnp.exp(cum_o[m]), expand) * dot3(cx[m, :, inner + states :], entered)
        y_o[m] = y
        z = proj[m, :, :inner]
        gated = y * z * sigmoid(z)
        gates[m] = gated
        stats = [jnp.sum(gated * gated, axis=1, keepdims=True)]
        if has_dyn:
            stats.append(jnp.sum(gated * gain[...] * dyn[m], axis=1, keepdims=True))
        square[m] = rows_of(stats)
    copies = [
        push(square, square_got.at[d], stat_send.at[d], stat_recv.at[d], peer) for d, peer in enumerate(peers)
    ]
    for copy in copies:
        copy.wait()
    for m in range(batch):
        total = square[m]
        for d in range(heads_axis - 1):
            total = total + square_got[d, m]
        gs = lax.rsqrt(total[0:1] / full + EPSILON)
        stats_o[m] = jnp.concatenate([gs, total[1:]], axis=0)
        yn_o[m] = (gates[m] * column(stats_o[m])[0][:, 0:1] * gain[...]).astype(BF)
    line.finish()

    @pl.when(jnp.logical_not(line.ends))
    def _():
        for m in range(batch):
            line.halo(rim.at[m], halo.at[m], m, halo_send, halo_recv).wait_send()


def ssd_fwd(proj, block, dyn, dims, size, heads_axis, full):
    heads, inner, states = dims
    batch, n, _ = proj.shape
    wide = inner + 2 * states
    vm = pl.BlockSpec(memory_space=pltpu.VMEM)
    has_dyn = dyn is not None
    moved = (batch, states, inner)
    outs = (
        shape((batch, n, wide), F32),
        shape((batch, n, LANES), F32),
        shape((batch, n, LANES), F32),
        shape(moved, F32),
        shape((batch, 16, wide), BF),
        shape((batch, n, inner), F32),
        shape((batch, n, inner), BF),
        shape((batch, 8, n), F32),
    )
    return pl.pallas_call(
        functools.partial(ssd_fwd_kernel, dims, size, heads_axis, full, has_dyn),
        out_shape=outs,
        in_specs=[vm] * (2 + has_dyn),
        out_specs=(vm,) * len(outs),
        scratch_shapes=[
            pltpu.VMEM((n + 8, wide), F32),
            pltpu.VMEM(moved, F32),
            pltpu.VMEM((batch, 8, inner), F32),
            pltpu.VMEM((batch, 16, wide), BF),
            pltpu.VMEM(moved, F32),
            pltpu.VMEM(moved, F32),
            pltpu.VMEM((batch, n, inner), F32),
            pltpu.VMEM((batch, 8, n), F32),
            pltpu.VMEM((heads_axis - 1, batch, 8, n), F32),
            pltpu.SemaphoreType.DMA((batch * PARTS,)),
            pltpu.SemaphoreType.DMA((batch * PARTS,)),
            pltpu.SemaphoreType.DMA((batch,)),
            pltpu.SemaphoreType.DMA((batch,)),
            pltpu.SemaphoreType.DMA((heads_axis - 1,)),
            pltpu.SemaphoreType.DMA((heads_axis - 1,)),
        ],
        compiler_params=pltpu.CompilerParams(
            collective_id=1 + has_dyn, has_side_effects=True, vmem_limit_bytes=VMEM_LIMIT
        ),
        name="ssd_fwd",
    )(proj, block, *([dyn] if has_dyn else []))


def ssd_bwd_kernel(
    dims, size, heads_axis, full, has_across,
    dyn, y, proj, halo, cx, dt, cum, state, stats, block, *refs
):
    taps, bias, dt_bias, a_neg, skip, gain = constants(block, dims)
    if has_across:
        h_rows, h_whole, h_o, *refs = refs[:2] + refs[6:7] + refs[2:6] + refs[7:]
        *refs, c_local, c_send, c_recv = refs
    (
    g_in, gate_o, conv_o, small_o,
    dy, dxw, dpre, own, decay, ext, rowq, colq, d_scores, outgoing, incoming, rim, square, square_got,
    send, recv, rim_send, rim_recv, stat_send, stat_recv,
    ) = refs
    heads, inner, states = dims
    batch, n = dyn.shape[0], dyn.shape[1]
    wide = inner + 2 * states
    columns = slice(inner, inner + wide)
    size_p = inner // heads
    pairs = heads // 2
    line = Line(False, size, PARTS, outgoing, incoming, send, recv)
    head = lax.axis_index("head")
    peers = [{"head": lax.rem(head + d, heads_axis)} for d in range(1, heads_axis)]
    barrier = pltpu.get_barrier_semaphore()
    line.greet(barrier)
    if has_across:
        outputs = Collect(1, heads_axis, h_rows, h_whole, h_o, c_local, c_send, c_recv)
        peers = outputs.greeted()
    for peer in peers:
        pl.semaphore_signal(barrier, inc=1, device_id=peer, device_id_type=MESH)
    if not has_across:
        for m in range(batch):
            z = proj[m, :, :inner]
            square[m] = rows_of([jnp.sum(dyn[m] * gain[...] * y[m] * z * sigmoid(z), axis=1, keepdims=True)])
    line.met(barrier, len(peers))
    if has_across:
        outputs.start()
    else:
        copies = [
            push(square, square_got.at[d], stat_send.at[d], stat_recv.at[d], peers[d])
            for d in range(heads_axis - 1)
        ]
    expand = head_mask(inner, heads)
    if not has_across:
        for copy in copies:
            copy.wait()
    for m in range(batch):
        gs, across = [v[:, 0:1] for v in column(stats[m])]
        if has_across:
            pass
        else:
            total = square[m]
            for d in range(heads_axis - 1):
                total = total + square_got[d, m]
            across = column(total)[0][:, 0:1]
        z = proj[m, :, :inner]
        sig = sigmoid(z)
        yv = y[m]
        gated = yv * z * sig
        dynv = dyn[m]
        scaled = gated * gs
        gate_o[m] = jnp.broadcast_to(jnp.sum(dynv * scaled, axis=0, keepdims=True), (8, inner))
        dgated = gs * gain[...] * dynv - gated * (gs * gs * gs * across / full)
        dyv = dgated * z * sig
        dy[m] = dyv
        g_in[m, :, :inner] = (dgated * yv * sig * (1.0 + z * (1.0 - sig))).astype(BF)
        cums = cum[m]
        moved = dot_mask(jnp.exp(cums), expand) * dyv
        mine = dot3(cx[m, :, inner + states :], moved, TN)
        own[m] = mine
        decay[m] = dot_mask(jnp.broadcast_to(jnp.exp(cums[n - 1 : n, :]), (8, LANES)), expand)
        line.begin(m, mine)
    keep = order_mask(n, False)
    lane = lax.broadcasted_iota(jnp.int32, (n, LANES), 1)
    first = lane < size_p
    rowq[...] = jnp.zeros_like(rowq)
    for m in range(batch):
        scores_t = dot3(cx[m, :, inner : inner + states], cx[m, :, inner + states :], NT)
        cums = cum[m]
        cums_t = jnp.transpose(cums)
        dt_wide = dot_mask(dt[m], expand)
        colq[m] = jnp.zeros_like(colq[m])
        d_scores[m] = jnp.zeros_like(d_scores[m])
        for p in range(pairs):

            line.relay(own, decay, m * pairs + p, batch * pairs, 2, 1)
            lanes = slice(p * LANES, (p + 1) * LANES)
            dtx, dtx_rest = halves(cx[m, :, lanes] * dt_wide[:, lanes])
            dyb, dy_rest = halves(dy[m, :, lanes])
            both, gathered = [], [0.0, 0.0]
            for j, h in enumerate((2 * p, 2 * p + 1)):
                side = first if j == 0 else jnp.logical_not(first)
                mine, mine_rest = [jnp.where(side, v, jnp.zeros((), BF)) for v in (dtx, dtx_rest)]
                sums, row_sums, column_sums = [], [], []
                for i, (low, high) in enumerate(((0, n // 2), (n // 2, n))):
                    lag = jnp.where(
                        keep[low:high, low:n], cums_t[h : h + 1, low:n] - cums[low:high, h : h + 1], -1e30
                    )
                    decays = jnp.exp(lag)
                    weights = scores_t[low:high, low:n] * decays
                    d_weights = (
                        dot(mine[low:high], dyb[low:n], NT)
                        + dot(mine[low:high], dy_rest[low:n], NT)
                        + dot(mine_rest[low:high], dyb[low:n], NT)
                    )
                    q = d_weights * weights
                    gathered[i] = gathered[i] + d_weights * decays
                    row_sums.append(jnp.sum(q, axis=0, keepdims=True))
                    column_sums.append(jnp.sum(q, axis=1, keepdims=True))
                    sums.append(dot(weights.astype(BF), dyb[low:n]))
                rowq[m, h : h + 1, :] = row_sums[0]
                rowq[m, h : h + 1, n // 2 :] += row_sums[1]
                colq[m] += jnp.where(lane == h, jnp.concatenate(column_sums, axis=0), 0.0)
                both.append(jnp.concatenate(sums, axis=0))
            d_scores[m, 0 : n // 2, :] += gathered[0]
            d_scores[m, n // 2 :, n // 2 :] += gathered[1]
            dxw[m, :, lanes] = jnp.where(first, both[0], both[1])
    fold = lambda v: dot_mask(v, expand, NT)
    for m in range(batch):
        x = cx[m, :, :inner]
        b = cx[m, :, inner : inner + states]
        c = cx[m, :, inner + states :]
        b_high, b_rest = halves(b)
        dyv, dxv, dtv, cums = dy[m], dxw[m], dt[m], cum[m]
        last = cums[n - 1 : n, :]
        entered, later_b = state[m], incoming[m]
        moved = dot_mask(jnp.exp(cums), expand) * dyv
        carried = dot3(c, entered)
        tail = jnp.exp(last - cums)
        weight = tail * dtv
        weight_wide = dot_mask(weight, expand)
        pulled = dot(b_high, later_b) + dot(b_rest, later_b)
        dx = dot_mask(dtv, expand) * dxv + weight_wide * pulled + skip[...] * dyv
        dw = fold(x * pulled)
        wdw = weight * dw
        change = jnp.transpose(rowq[m]) + fold(carried * moved) - colq[m] - wdw
        ends = jnp.sum(entered * later_b.astype(F32), axis=0, keepdims=True)
        ends = jnp.sum(wdw, axis=0, keepdims=True) + jnp.exp(last) * fold(jnp.broadcast_to(ends, (8, inner)))[0:1]
        log_grad = mask_dot(order_mask(n, False).astype(F32).astype(BF), change) + ends
        ddt = fold(x * dxv) + tail * dw + a_neg[...] * log_grad
        ddt_raw = ddt * sigmoid(proj[m, :, inner + wide :] + dt_bias[...])
        g_in[m, :, inner + wide :] = ddt_raw.astype(BF)
        small_o[m] = jnp.concatenate(
            [
                jnp.sum(ddt_raw, axis=0, keepdims=True),
                jnp.sum(dtv * log_grad, axis=0, keepdims=True) * a_neg[...],
                fold(jnp.broadcast_to(jnp.sum(x * dyv, axis=0, keepdims=True), (8, inner)))[0:1],
                jnp.zeros((5, LANES), F32),
            ],
            axis=0,
        )
        xw_high, xw_rest = halves(x * weight_wide)
        dc = dot3(d_scores[m], b, TN) + dot3(moved, entered, NT)
        db = dot3(d_scores[m], c) + dot(xw_high, later_b, NT) + dot(xw_rest, later_b, NT)
        xbc = proj[m, :, columns].astype(BF).astype(F32)
        pre = conv_pre(ext, xbc, halo[m, 8:].astype(F32), taps[...], bias[...])
        sig = sigmoid(pre)
        d_act = jnp.concatenate([dx, db, dc], axis=1) * sig * (1.0 + pre * (1.0 - sig))
        dpre[m, 0:n, :] = d_act
        rim_copy = line.halo(dpre.at[m, pl.ds(0, 8)], rim.at[m], m, rim_send, rim_recv)
        pl.when(jnp.logical_not(line.ends))(rim_copy.start)
        rows = [jnp.sum(d_act * ext[5 + k : 5 + k + n, :], axis=0, keepdims=True) for k in range(4)]
        rows.append(jnp.sum(d_act, axis=0, keepdims=True))
        conv_o[m] = jnp.concatenate(rows + [jnp.zeros((3, wide), F32)], axis=0)

    @pl.when(line.starts)
    def _():
        rim[...] = jnp.zeros_like(rim)

    for m in range(batch):
        rim_copy = line.halo(dpre.at[m, pl.ds(0, 8)], rim.at[m], m, rim_send, rim_recv)
        pl.when(jnp.logical_not(line.starts))(rim_copy.wait_recv)
        dpre[m, n : n + 8, :] = rim[m]
        total = taps[3:4, :] * dpre[m, 0:n, :]
        for k in range(3):
            total = total + taps[k : k + 1, :] * dpre[m, 3 - k : 3 - k + n, :]
        g_in[m, :, columns] = total.astype(BF)
        pl.when(jnp.logical_not(line.ends))(rim_copy.wait_send)
    line.finish()
    if has_across:
        outputs.finish()


def ssd_bwd(dyn, y, proj, halo, cx, dt, cum, state, stats, block, outputs,
            dims, size, heads_axis, full):
    has_across = bool(outputs)
    heads, inner, states = dims
    batch, n, wide = cx.shape
    vm = pl.BlockSpec(memory_space=pltpu.VMEM)
    moved = (batch, states, inner)
    outs = (
        shape((batch, n, inner + wide + LANES), BF),
        shape((batch, 8, inner), F32),
        shape((batch, 8, wide), F32),
        shape((batch, 8, LANES), F32),
    ) + tuple(shape((2 * a.shape[0], a.shape[1]), BF) for a in outputs[1:])
    sems = lambda k: pltpu.SemaphoreType.DMA((k,))
    return pl.pallas_call(
        functools.partial(ssd_bwd_kernel, dims, size, heads_axis, full, has_across),
        out_shape=outs,
        in_specs=[vm] * (10 + len(outputs)),
        out_specs=(vm,) * 4 + (pl.BlockSpec(memory_space=pl.ANY),) * has_across,
        scratch_shapes=[
            pltpu.VMEM((batch, n, inner), F32),
            pltpu.VMEM((batch, n, inner), F32),
            pltpu.VMEM((batch, n + 8, wide), F32),
            pltpu.VMEM(moved, F32),
            pltpu.VMEM((batch, 8, inner), F32),
            pltpu.VMEM((n + 8, wide), F32),
            pltpu.VMEM((batch, LANES, n), F32),
            pltpu.VMEM((batch, n, LANES), F32),
            pltpu.VMEM((batch, n, n), F32),
            pltpu.VMEM(moved, BF),
            pltpu.VMEM(moved, BF),
            pltpu.VMEM((batch, 8, wide), F32),
            pltpu.VMEM((batch, 8, n), F32),
            pltpu.VMEM((heads_axis - 1, batch, 8, n), F32),
            sems(batch * PARTS),
            sems(batch * PARTS),
            sems(batch),
            sems(batch),
            sems(heads_axis - 1),
            sems(heads_axis - 1),
        ]
        + (collect_sems(heads_axis) if has_across else []),
        compiler_params=pltpu.CompilerParams(
            collective_id=10 + has_across, has_side_effects=True, vmem_limit_bytes=VMEM_LIMIT
        ),
        name="ssd_bwd",
    )(dyn, y, proj, halo, cx, dt, cum, state, stats, block, *outputs)


def greet(size, core=False):
    me = lax.axis_index("head")
    barrier = pltpu.get_barrier_semaphore()
    peers = [{"head": lax.rem(me + d, size)} for d in range(1, size)]
    others = [{"section": 1 - lax.axis_index("section")}] if core else []
    for peer in peers + others:
        pl.semaphore_signal(barrier, inc=1, device_id=peer, device_id_type=MESH)
    pl.semaphore_wait(barrier, len(peers) + len(others))
    return me, peers


def block_of(index, rows):
    return pl.ds(pl.multiple_of(index * rows, rows), rows)


def normal(u, gain):
    uv = u.astype(F32)
    s = lax.rsqrt(jnp.sum(uv * uv, axis=1, keepdims=True) / uv.shape[1] + EPSILON)
    return (uv * s * gain).astype(BF)


def head_fwd_kernel(size, onward, yn, w_out, u, *refs):
    if onward:
        w_in, block, h_o, normed_o, proj_o, out, got, send, recv = refs
        gain = norm_gain_of(block, u.shape[1])
    else:
        go, h_o, body_o, out, got, body_send, body_got, send, recv, body_ss, body_rs = refs
    rows = yn.shape[0] // size
    me, peers = greet(size, core=not onward)
    copies = []
    for d, peer in enumerate(peers):
        to = lax.rem(me + d + 1, size)
        out[d] = dot(yn[block_of(to, rows), :], w_out[...]).astype(out.dtype)
        copies.append(push(out.at[d], got.at[d], send.at[0, d], recv.at[0, d], peer))
    mine = block_of(me, rows)
    total = dot(yn[mine, :], w_out[...])
    if not onward:
        body = body_halves(lambda which, i: body_tile(None, None, yn, go, which, i), body_o, body_send, body_got, body_ss, body_rs)
    for copy in copies:
        copy.wait()
    for d in range(size - 1):
        total = total + got[d].astype(F32)
    h = (u[mine, :].astype(F32) + total).astype(BF)
    if not onward:
        h_o[...] = h
        add_halves(body, body_o, body_got)
        return
    h_o[mine, :] = h
    copies = [
        push(h_o.at[mine], h_o.at[mine], send.at[1, d], recv.at[1, d], peer) for d, peer in enumerate(peers)
    ]

    def project(at):
        normed = normal(h_o[at, :], gain[...])
        normed_o[at, :] = normed
        proj_o[at, :] = dot(normed, w_in[...])

    project(mine)
    for d, copy in enumerate(copies):
        copy.wait_recv()
        project(block_of(lax.rem(me + size - d - 1, size), rows))
    for copy in copies:
        copy.wait_send()


def head_fwd(yn, w_out, u, size, onward, go=None):
    n, d_model = u.shape
    body = (yn.shape[1], d_model // 2)
    tiles = body[0] // 256
    rows = n // size
    vm = pl.BlockSpec(memory_space=pltpu.VMEM)
    kind = F32 if onward else BF
    outs = [shape((n if onward else rows, d_model), BF)]
    if onward:
        outs += [shape((n, d_model), BF), shape((n, onward[0].shape[1]), F32)]
    else:
        outs += [shape(body, BF)]
        onward = [go]
    more = go is not None
    return pl.pallas_call(
        functools.partial(head_fwd_kernel, size, not more),
        out_shape=tuple(outs),
        in_specs=[vm] * (3 + len(onward)),
        out_specs=(vm,) * len(outs),
        scratch_shapes=[
            pltpu.VMEM((size - 1, rows, d_model), kind),
            pltpu.VMEM((size - 1, rows, d_model), kind),
        ]
        + [pltpu.VMEM(body, BF)] * (2 * more)
        + [pltpu.SemaphoreType.DMA((2, size - 1))] * 2
        + [pltpu.SemaphoreType.DMA((tiles,))] * (2 * more),
        compiler_params=pltpu.CompilerParams(
            collective_id=6 if more else 3, has_side_effects=True, vmem_limit_bytes=VMEM_LIMIT
        ),
        name="head_fwd",
    )(yn, w_out, u, *onward)


def input_gradient(dn, u, gain, above):
    uv = u.astype(F32)
    width = uv.shape[1]
    s = lax.rsqrt(jnp.sum(uv * uv, axis=1, keepdims=True) / width + EPSILON)
    scaled = dn * gain
    inner = jnp.sum(scaled * uv, axis=1, keepdims=True)
    return (
        above.astype(F32) + s * scaled - uv * (s * s * s * inner / width),
        jnp.sum(dn * uv * s, axis=0, keepdims=True),
    )


def body_tile(normed, g_in, yn, go, half, i):
    left, right = (yn, go) if normed is None else (normed, g_in)
    wide = yn.shape[1]
    at = pl.ds(pl.multiple_of(half * wide, wide), wide)
    return dot(left[:, i * 256 : (i + 1) * 256], right[:, at], TN)


def body_halves(make, out, sent, got, send, recv):
    layer = lax.axis_index("section")
    copies = []
    for i in range(out.shape[0] // 256):
        at = pl.ds(i * 256, 256)
        sent[at, :] = make(1 - layer, i).astype(BF)
        copies.append(push(sent.at[at], got.at[at], send.at[i], recv.at[i], {"section": 1 - layer}))
    for i in range(out.shape[0] // 256):
        out[i * 256 : (i + 1) * 256, :] = make(layer, i).astype(BF)
    return copies


def add_halves(copies, out, got):
    for i, copy in enumerate(copies):
        at = slice(i * 256, (i + 1) * 256)
        copy.wait()
        out[at, :] = (out[at, :].astype(F32) + got[at, :].astype(F32)).astype(BF)


def head_bwd_kernel(size, g_in, w_in, upper, u, block, w_out, normed, yn, du_o, mine_o, grad_o, dyn_o, body_o,
                    out, got, body_send, body_got, send, recv, body_ss, body_rs):
    rows = u.shape[0] // size
    gain = norm_gain_of(block, u.shape[1])
    me, peers = greet(size, core=True)
    copies = []
    for d, peer in enumerate(peers):
        to = lax.rem(me + d + 1, size)
        out[d] = dot(g_in[block_of(to, rows), :], w_in[...], NT).astype(BF)
        copies.append(push(out.at[d], got.at[d], send.at[0, d], recv.at[0, d], peer))
    mine = block_of(me, rows)
    dn = dot(g_in[mine, :], w_in[...], NT)
    make = lambda which, i: body_tile(normed, g_in, yn, upper, which, i)
    body = body_halves(make, body_o, body_send, body_got, body_ss, body_rs)
    for copy in copies:
        copy.wait()
    for d in range(size - 1):
        dn = dn + got[d].astype(F32)
    du, grad = input_gradient(dn, u[mine, :], gain[...], upper[mine, :])
    grad_o[...] = jnp.broadcast_to(grad, grad_o.shape)
    mine_o[...] = du
    du_o[mine, :] = du.astype(BF)
    copies = [
        push(du_o.at[mine], du_o.at[mine], send.at[1, d], recv.at[1, d], peer) for d, peer in enumerate(peers)
    ]
    add_halves(body, body_o, body_got)
    dyn_o[mine, :] = dot(du_o[mine, :], w_out[...], NT)
    for d, copy in enumerate(copies):
        copy.wait_recv()
        at = block_of(lax.rem(me + size - d - 1, size), rows)
        dyn_o[at, :] = dot(du_o[at, :], w_out[...], NT)
    for copy in copies:
        copy.wait_send()


def head_bwd(g_in, w_in, upper, u, gain, w_out, normed, yn, size):
    n, d_model = u.shape
    inner = yn.shape[1]
    rows = n // size
    tiles = d_model // 256
    body = (d_model, d_model // 2)
    vm = pl.BlockSpec(memory_space=pltpu.VMEM)
    return pl.pallas_call(
        functools.partial(head_bwd_kernel, size),
        out_shape=(
            shape((n, d_model), BF),
            shape((rows, d_model), F32),
            shape((8, d_model), F32),
            shape((n, inner), F32),
            shape(body, BF),
        ),
        in_specs=[vm] * 8,
        out_specs=(vm,) * 5,
        scratch_shapes=[
            pltpu.VMEM((size - 1, rows, d_model), BF),
            pltpu.VMEM((size - 1, rows, d_model), BF),
            pltpu.VMEM(body, BF),
            pltpu.VMEM(body, BF),
            pltpu.SemaphoreType.DMA((2, size - 1)),
            pltpu.SemaphoreType.DMA((2, size - 1)),
            pltpu.SemaphoreType.DMA((tiles,)),
            pltpu.SemaphoreType.DMA((tiles,)),
        ],
        compiler_params=pltpu.CompilerParams(
            collective_id=5, has_side_effects=True, vmem_limit_bytes=VMEM_LIMIT
        ),
        name="head_bwd",
    )(g_in, w_in, upper, u, gain, w_out, normed, yn)


class Collect:
    def __init__(self, by_rows, size, rows, whole, out, local, send, recv):
        self.by_rows, self.size = by_rows, size
        self.rows, self.whole, self.out = rows, whole, out
        self.local, self.send, self.recv = local, send, recv
        self.core, self.head = lax.axis_index("section"), lax.axis_index("head")
        count = rows.shape[0]
        self.row_part = pl.ds(pl.multiple_of(self.core * whole.shape[0] + self.head * count, count), count)
        self.whole_part = block_of(self.core, whole.shape[0])

    def greeted(self):
        return [
            {"section": lax.rem(self.core + c, 2), "head": lax.rem(self.head + d, self.size)}
            for c in range(2)
            for d in range(self.size)
            if c or d
        ]

    def row_copy(self, sender, d):
        return pltpu.make_async_remote_copy(
            src_ref=self.rows, dst_ref=self.out.at[self.row_part],
            send_sem=self.send.at[d], recv_sem=self.recv.at[sender * self.size + d],
            device_id={"section": self.by_rows, "head": lax.rem(self.head + d, self.size)}, device_id_type=MESH,
        )

    def whole_copy(self):
        return pltpu.make_async_remote_copy(
            src_ref=self.whole, dst_ref=self.out.at[self.whole_part],
            send_sem=self.send.at[self.size], recv_sem=self.recv.at[2 * self.size],
            device_id={"section": 1 - self.by_rows}, device_id_type=MESH,
        )

    def start(self):
        @pl.when(self.core == self.by_rows)
        def _():
            pltpu.make_async_copy(self.rows, self.out.at[self.row_part], self.local).start()
            for d in range(1, self.size):
                self.row_copy(self.by_rows, d).start()
            self.whole_copy().start()

        @pl.when(self.core != self.by_rows)
        def _():
            pltpu.make_async_copy(self.whole, self.out.at[self.whole_part], self.local).start()
            for d in range(self.size):
                self.row_copy(1 - self.by_rows, d).start()

    def finish(self):
        @pl.when(self.core == self.by_rows)
        def _():
            pltpu.make_async_copy(self.rows, self.out.at[self.row_part], self.local).wait()
            for d in range(1, self.size):
                self.row_copy(self.by_rows, d).wait()
            for d in range(self.size):
                self.row_copy(1 - self.by_rows, d).wait_recv()
            self.whole_copy().wait_send()

        @pl.when(self.core != self.by_rows)
        def _():
            pltpu.make_async_copy(self.whole, self.out.at[self.whole_part], self.local).wait()
            for d in range(self.size):
                self.row_copy(1 - self.by_rows, d).wait_send()
            self.whole_copy().wait_recv()


def collect_sems(size):
    return [
        pltpu.SemaphoreType.DMA,
        pltpu.SemaphoreType.DMA((size + 1,)),
        pltpu.SemaphoreType.DMA((2 * size + 1,)),
    ]


OWN = 32
SHARED = 160
PIECE = 96
TAIL = (OWN + SHARED) // PIECE
LATE = 4
FEW = 16


def grad_tail_kernel(dims, normed, g_in, conv, scalars, gate, gain, tail, few):
    heads, inner, states = dims
    half = normed.shape[1] // 2
    split = 2 * inner + 2 * states
    rest = dot(g_in[:, 2 * inner :], normed[...], TN).astype(BF)
    step = (tail.shape[0] - OWN) // 2
    tail[...] = jnp.zeros_like(tail)
    for i in range(2):
        lanes = slice(i * half, (i + 1) * half)
        tail[i * OWN // 2 : (i + 1) * OWN // 2, :] = rest[2 * states : 2 * states + OWN // 2, lanes]
        tail[OWN + i * step : OWN + i * step + 2 * states, :] = rest[: 2 * states, lanes]
    conv_sum, scalar_sum, gate_sum = conv[0], scalars[0], gate[0]
    for i in range(1, conv.shape[0]):
        conv_sum, scalar_sum, gate_sum = conv_sum + conv[i], scalar_sum + scalars[i], gate_sum + gate[i]
    few[...] = jnp.zeros_like(few)
    few[0:5, :] = conv_sum[0:5, :inner]
    few[5:6, :] = gate_sum[0:1]
    for i in range(3):
        few[6:7, i * LANES : (i + 1) * LANES] = scalar_sum[i : i + 1]
    few[8:9, :] = gain[0:1, :half]
    few[9:10, :] = gain[0:1, half:]
    few[10:15, 0 : 2 * states] = conv_sum[0:5, inner:]


def grad_tail(normed, g_in, conv, scalars, gate, gain, dims, head_size):
    heads, inner, states = dims
    width = normed.shape[1]
    vm = pl.BlockSpec(memory_space=pltpu.VMEM)
    return pl.pallas_call(
        functools.partial(grad_tail_kernel, dims),
        out_shape=(shape((OWN + head_size * SHARED, width // 2), BF), shape((FEW, width // 2), F32)),
        in_specs=[vm] * 6,
        out_specs=(vm, vm),
        compiler_params=pltpu.CompilerParams(vmem_limit_bytes=VMEM_LIMIT),
        name="grad_tail",
    )(normed, g_in, conv, scalars, gate, gain)


def grad_sum_kernel(size, heads, skew, g_in, w_in, above, u, block, normed, yn, go, body1, tail0, tail1, few0, few1, done, done_out,
                    first_o, second_o, tail_o, shared_o, few_o, du_o,
                    own, core, got, out, shared, shared_core, shared_got, few_core, few_seq, few_head,
                    body_send, body_own, du_out, du_got, du_rows, few_mine,
                    cs, cr, rs, rr, bs, br, ts, tr, ls, hs, hr, xs, fs, fr, gs, gr, ds, dr, c_local, c_send, c_recv):
    me, layer, head = lax.axis_index("seq"), lax.axis_index("section"), lax.axis_index("head")
    half = out.shape[0] // 2
    parts = half // PIECE
    total0 = body_own.shape[0]
    early = done.shape[0]
    cut = (parts - LATE) * PIECE
    far = size - 1
    up, down, other = {"seq": me + 1}, {"seq": me - 1}, {"section": 1 - layer}
    peers = [{"head": lax.rem(head + d, heads)} for d in range(1, heads)]
    blocks = [{"seq": lax.rem(me + d, size)} for d in range(1, size)]
    low_end, high_end = me == 0, me == size - 1
    barrier = pltpu.get_barrier_semaphore()
    inputs = Collect(0, heads, du_rows, go, du_o, c_local, c_send, c_recv)
    plane = inputs.greeted()
    for peer in plane + blocks:
        pl.semaphore_signal(barrier, inc=1, device_id=peer, device_id_type=MESH)
    pl.semaphore_wait(barrier, len(plane) + len(blocks))

    late = [
        pltpu.make_async_copy(
            body1.at[pl.ds(early + side * LATE * PIECE, LATE * PIECE)],
            own.at[pl.ds(side * half, LATE * PIECE)],
            xs.at[7 + side],
        )
        for side in range(2)
    ]
    for copy in late:
        copy.start()

    ready = [(done, pl.ds(0, early)), (done_out, pl.ds(normed.shape[1], done_out.shape[0]))]
    given = [
        pltpu.make_async_remote_copy(
            src_ref=src, dst_ref=first_o.at[at], send_sem=xs.at[9 + i], recv_sem=xs.at[5 + i],
            device_id=other, device_id_type=MESH,
        )
        for i, (src, at) in enumerate(ready)
    ]
    kept = [pltpu.make_async_copy(src, second_o.at[at], xs.at[9 + i]) for i, (src, at) in enumerate(ready)]

    def all_of(copies, act):
        for copy in copies:
            act(copy)

    pl.when(layer == 0)(lambda: all_of(given, lambda copy: copy.start()))
    pl.when(layer == 1)(lambda: all_of(kept, lambda copy: copy.start()))

    def fetch_tail(ours, others):
        return (
            pltpu.make_async_copy(ours, shared, xs.at[0]),
            pltpu.make_async_remote_copy(
                src_ref=others, dst_ref=shared_core, send_sem=xs.at[1], recv_sem=xs.at[2],
                device_id=other, device_id_type=MESH,
            ),
        )

    def start_all(copies):
        for copy in copies:
            copy.start()

    pl.when(layer == 0)(lambda: start_all(fetch_tail(tail0, tail1)))
    pl.when(layer == 1)(lambda: start_all(fetch_tail(tail1, tail0)))

    rows_here = u.shape[0] // heads
    du_copy = lambda d: pltpu.make_async_remote_copy(
        src_ref=du_out.at[d], dst_ref=du_got.at[d], send_sem=ds.at[d], recv_sem=dr.at[d],
        device_id=peers[d], device_id_type=MESH,
    )

    def few_to_core(src):
        return pltpu.make_async_remote_copy(
            src_ref=src, dst_ref=few_core, send_sem=xs.at[3], recv_sem=xs.at[4],
            device_id=other, device_id_type=MESH,
        )

    few_to_seq = lambda d: pltpu.make_async_remote_copy(
        src_ref=few_seq.at[me], dst_ref=few_seq.at[me], send_sem=fs.at[d], recv_sem=fr.at[d],
        device_id=blocks[d], device_id_type=MESH,
    )
    few_to_head = lambda d: pltpu.make_async_remote_copy(
        src_ref=few_head.at[head], dst_ref=few_head.at[head], send_sem=gs.at[d], recv_sem=gr.at[d],
        device_id=peers[d], device_id_type=MESH,
    )
    shared_block = lambda i: pl.ds(pl.multiple_of(OWN + i * SHARED, 32), SHARED)
    scatter = lambda d: pltpu.make_async_remote_copy(
        src_ref=shared.at[shared_block(lax.rem(head + d + 1, heads))], dst_ref=shared_got.at[d],
        send_sem=hs.at[0, d], recv_sem=hr.at[0, d], device_id=peers[d], device_id_type=MESH,
    )
    gather = lambda d: pltpu.make_async_remote_copy(
        src_ref=shared_o.at[head], dst_ref=shared_o.at[head],
        send_sem=hs.at[1, d], recv_sem=hr.at[1, d], device_id=peers[d], device_id_type=MESH,
    )

    for copy in fetch_tail(tail0, tail1):
        copy.wait()
    shared[...] = (shared[...].astype(F32) + shared_core[...].astype(F32)).astype(BF)
    for d in range(heads - 1):
        scatter(d).start()
    for d in range(heads - 1):
        to = block_of(lax.rem(head + d + 1, heads), rows_here)
        du_out[d] = dot(g_in[to, :], w_in[...], NT).astype(BF)
        du_copy(d).start()

    tile = 256
    in_tiles = normed.shape[1] // tile
    tiles = total0 // tile

    def body_copy(i):
        at = block_of(i, tile)
        return pltpu.make_async_remote_copy(
            src_ref=body_send.at[at], dst_ref=core.at[at], send_sem=cs.at[i], recv_sem=cr.at[i],
            device_id=other, device_id_type=MESH,
        )

    def make_tile(i, left, right):
        at = block_of(i, tile)
        wide = yn.shape[1]
        for which, target in ((1 - layer, body_send), (layer, body_own)):
            columns = pl.ds(pl.multiple_of(which * wide, wide), wide)
            target[at, :] = dot(left, right[:, columns], TN).astype(BF)
        body_copy(i).start()

    place = lambda side, p: pl.ds(pl.multiple_of(side * half + p * PIECE, PIECE), PIECE)
    is_late = lambda p: p < LATE
    is_tail = lambda side, p: jnp.logical_and(side == 1, jnp.logical_and(p >= LATE, p < LATE + TAIL))
    start0 = lambda side, p: (p - LATE) * PIECE + (cut - TAIL * PIECE) * side
    start1 = lambda side, p: early + side * LATE * PIECE + p * PIECE

    def sending(side, p, back, source):
        at = place(side, p)
        towards = down if (side == 0) != back else up
        target, send, recv = (out, bs, br) if back else (got, rs, rr)
        return pltpu.make_async_remote_copy(
            src_ref=source.at[at], dst_ref=target.at[at], send_sem=send.at[side, p],
            recv_sem=recv.at[side, p], device_id=towards, device_id_type=MESH,
        )

    def give(side, p, target, at):
        return pltpu.make_async_remote_copy(
            src_ref=out.at[place(side, p)], dst_ref=target.at[at], send_sem=ts.at[side, p],
            recv_sem=tr.at[side, p], device_id=other, device_id_type=MESH,
        )

    def keep(side, p, target, at):
        return pltpu.make_async_copy(out.at[place(side, p)], target.at[at], ls.at[side, p])

    def final(side, p, act_keep, act_give):
        at0 = lambda: pl.ds(pl.multiple_of(start0(side, p), PIECE), PIECE)
        at1 = lambda: pl.ds(pl.multiple_of(start1(side, p), PIECE), PIECE)
        late_piece = is_late(p)
        body0 = jnp.logical_not(jnp.logical_or(late_piece, is_tail(side, p)))
        pl.when(jnp.logical_and(body0, layer == 0))(lambda: act_keep(keep(side, p, first_o, at0())))
        pl.when(jnp.logical_and(body0, layer == 1))(lambda: act_give(give(side, p, second_o, at0())))
        pl.when(jnp.logical_and(late_piece, layer == 0))(lambda: act_give(give(side, p, first_o, at1())))
        pl.when(jnp.logical_and(late_piece, layer == 1))(lambda: act_keep(keep(side, p, second_o, at1())))

    begin = lambda copy: copy.start()

    def reduce(side, p):
        start, end = (high_end, low_end) if side == 0 else (low_end, high_end)
        at = place(side, p)

        @pl.when(jnp.logical_not(jnp.logical_or(is_late(p), is_tail(side, p))))
        def _():
            mine = pl.ds(pl.multiple_of(start0(side, p), PIECE), PIECE)
            own[at, :] = (body_own[mine, :].astype(F32) + core[mine, :].astype(F32)).astype(BF)

        @pl.when(start)
        def _():
            sending(side, p, False, own).start()

        @pl.when(jnp.logical_not(start))
        def _():
            sending(side, p, False, got).wait_recv()
            summed = (own[at, :].astype(F32) + got[at, :].astype(F32)).astype(BF)

            @pl.when(end)
            def _():
                out[at, :] = summed
                sending(side, p, True, out).start()
                final(side, p, begin, begin)

            @pl.when(jnp.logical_not(end))
            def _():
                got[at, :] = summed
                sending(side, p, False, got).start()

    def back(side, p):
        start, end = (high_end, low_end) if side == 0 else (low_end, high_end)

        @pl.when(jnp.logical_not(end))
        def _():
            sending(side, p, True, out).wait_recv()

            @pl.when(jnp.logical_not(start))
            def _():
                sending(side, p, True, out).start()

            final(side, p, begin, begin)

    def guarded(act, side, p):
        @pl.when(jnp.logical_and(p >= 0, p < parts))
        def _():
            act(side, p)

    tail_at = half + LATE * PIECE
    finished = LATE + TAIL + skew * (2 * far - me)
    for copy in late:
        copy.wait()

    def step(t, _):
        def one_tile(k, _):
            i = 2 * t + k

            @pl.when(i < in_tiles)
            def _():
                make_tile(i, normed[:, block_of(i, tile)], g_in)

            @pl.when(jnp.logical_and(i >= in_tiles, i < tiles))
            def _():
                make_tile(i, yn[:, block_of(i - in_tiles, tile)], go)

            pl.when(jnp.logical_and(i >= 2, i < tiles + 2))(lambda: body_copy(i - 2).wait())
            return 0

        lax.fori_loop(0, 2, one_tile, 0)

        @pl.when(t == 5)
        def _():
            here = block_of(head, rows_here)
            dn = dot(g_in[here, :], w_in[...], NT)
            for d in range(heads - 1):
                du_copy(d).wait()
                dn = dn + du_got[d].astype(F32)
            du, grad = input_gradient(dn, u[here, :], norm_gain_of(block, u.shape[1])[...], above[...])
            du_rows[...] = du.astype(BF)
            inputs.start()
            few_mine[...] = few0[...]
            wide = few0.shape[1]
            for i in range(2):
                few_mine[8 + i : 9 + i, :] = grad[:, i * wide : (i + 1) * wide]
            pl.when(layer == 0)(lambda: few_to_core(few1).start())
            pl.when(layer == 1)(lambda: few_to_core(few_mine).start())

        @pl.when(t == 7)
        def _():
            few_to_core(few_mine).wait()
            pl.when(layer == 0)(lambda: few_seq.__setitem__(me, few_mine[...] + few_core[...]))
            pl.when(layer == 1)(lambda: few_seq.__setitem__(me, few1[...] + few_core[...]))
            for d in range(size - 1):
                few_to_seq(d).start()

        @pl.when(t == 11)
        def _():
            for d in range(size - 1):
                few_to_seq(d).wait()
            total = few_seq[0]
            for i in range(1, size):
                total = total + few_seq[i]
            few_o[0 : FEW // 2, :] = total[0 : FEW // 2]
            few_head[head] = total[FEW // 2 :]
            for d in range(heads - 1):
                few_to_head(d).start()

        @pl.when(t == 16)
        def _():
            for d in range(heads - 1):
                few_to_head(d).wait()
            total = few_head[0]
            for i in range(1, heads):
                total = total + few_head[i]
            few_o[FEW // 2 :, :] = total

        @pl.when(t == 4)
        def _():
            total = shared[shared_block(head), :].astype(F32)
            for d in range(heads - 1):
                scatter(d).wait()
                total = total + shared_got[d].astype(F32)
            own[tail_at + OWN : tail_at + OWN + SHARED, :] = total.astype(BF)
            own[tail_at : tail_at + OWN, :] = shared[0:OWN, :]

        guarded(reduce, 0, t - skew * (far - me))
        guarded(reduce, 1, t - skew * me)
        guarded(back, 0, t - skew * (far + me))
        guarded(back, 1, t - skew * (2 * far - me))

        @pl.when(t == finished)
        def _():
            tail_o[...] = out[tail_at : tail_at + OWN, :]
            shared_o[head] = out[tail_at + OWN : tail_at + OWN + SHARED, :]
            for d in range(heads - 1):
                gather(d).start()

        return 0

    lax.fori_loop(0, parts + 2 * skew * far, step, 0)

    def drain(p, _):
        for side in range(2):
            start, end = (high_end, low_end) if side == 0 else (low_end, high_end)

            @pl.when(jnp.logical_not(end))
            def _():
                sending(side, p, False, got).wait_send()

            @pl.when(jnp.logical_not(start))
            def _():
                sending(side, p, True, out).wait_send()

            final(side, p, lambda copy: copy.wait(), lambda copy: copy.wait_send())
            final(side, p, lambda copy: give(side, p, first_o, pl.ds(0, PIECE)).wait_recv(), lambda copy: None)
        return 0

    lax.fori_loop(0, parts, drain, 0)
    for d in range(heads - 1):
        gather(d).wait()
    pl.when(layer == 0)(lambda: all_of(given, lambda copy: copy.wait_send()))
    pl.when(layer == 1)(lambda: all_of(kept, lambda copy: copy.wait()))
    pl.when(layer == 1)(lambda: all_of(given, lambda copy: copy.wait_recv()))

    inputs.finish()


def grad_sum(layer0, body1, tails, fews, done, size, heads, skew=1):
    width = body1.shape[1]
    total = body1.shape[0] + done[1].shape[0]
    n, d_model = layer0[3].shape
    half = LATE * PIECE + (total + OWN + SHARED) // 2
    parts = half // PIECE
    vm = pl.BlockSpec(memory_space=pltpu.VMEM)
    anywhere = pl.BlockSpec(memory_space=pl.ANY)
    pair = pltpu.SemaphoreType.DMA((2, parts))
    sems = lambda *k: pltpu.SemaphoreType.DMA(k)
    tiles = total // 256
    big = pltpu.VMEM((2 * half, width), BF)
    body = pltpu.VMEM((total, width), BF)
    return pl.pallas_call(
        functools.partial(grad_sum_kernel, size, heads, skew),
        out_shape=(
            shape((total, width), BF),
            shape((total, width), BF),
            shape((OWN, width), BF),
            shape((heads, SHARED, width), BF),
            shape((FEW, width), F32),
            shape((2 * n, d_model), BF),
        ),
        in_specs=[vm] * 8 + [anywhere] * 3 + [vm] * 2 + [anywhere] * 2,
        out_specs=(anywhere, anywhere, vm, vm, vm, anywhere),
        scratch_shapes=[big, body, big, big]
        + [pltpu.VMEM((OWN + heads * SHARED, width), BF) for _ in range(2)]
        + [pltpu.VMEM((heads - 1, SHARED, width), BF)]
        + [pltpu.VMEM((FEW, width), F32), pltpu.VMEM((size, FEW, width), F32)]
        + [pltpu.VMEM((heads, FEW // 2, width), F32)]
        + [body] * 2
        + [pltpu.VMEM((heads - 1, n // heads, d_model), BF) for _ in range(2)]
        + [pltpu.VMEM((n // heads, d_model), BF), pltpu.VMEM((FEW, width), F32)]
        + [sems(tiles)] * 2
        + [pair] * 7
        + [sems(2, heads - 1)] * 2
        + [sems(11)]
        + [sems(size - 1)] * 2
        + [sems(heads - 1)] * 4
        + collect_sems(heads),
        compiler_params=pltpu.CompilerParams(
            collective_id=8, has_side_effects=True, vmem_limit_bytes=VMEM_LIMIT
        ),
        name="grad_sum",
    )(*layer0, body1, *tails, *fews, *done)


def unpack_kernel(dims, first, second, first_low, second_low, own, shared, few,
                  z_o, x_o, out_o, bc_o, dt_o, conv_o, conv_bias_o, bc_conv_o, bc_bias_o,
                  dt_bias_o, a_log_o, skip_o, gate_o, gain_o):
    heads, inner, states = dims
    half = own.shape[1]
    z_o[...] = first[...].astype(F32)
    x_o[...] = second[...].astype(F32)
    out_o[:, :half] = first_low[...].astype(F32)
    out_o[:, half:] = second_low[...].astype(F32)

    @pl.when(pl.program_id(0) == 0)
    def _():
        blocks = jnp.concatenate([shared[i] for i in range(shared.shape[0])], axis=0)
        step = blocks.shape[0] // 2
        for i in range(2):
            rows = slice(i * half, (i + 1) * half)
            bc_o[rows, :] = jnp.transpose(blocks[i * step : i * step + 2 * states].astype(F32))
            dts = own[i * OWN // 2 : (i + 1) * OWN // 2, :].astype(F32)
            dts = jnp.concatenate([dts, jnp.zeros((LANES - OWN // 2, half), F32)], axis=0)
            dt_o[rows, :] = jnp.transpose(dts)[:, :heads]
            gain_o[:, rows] = few[8 + i : 9 + i, :]
        conv_o[...] = few[0:4, :]
        conv_bias_o[...] = few[4:5, :]
        gate_o[...] = few[5:6, :]
        bc_conv_o[...] = few[10:14, 0 : 2 * states]
        bc_bias_o[...] = few[14:15, 0 : 2 * states]
        dt_bias_o[...] = few[6:7, 0:heads]
        a_log_o[...] = few[6:7, LANES : LANES + heads]
        skip_o[...] = few[6:7, 2 * LANES : 2 * LANES + heads]


def unpack(first, second, own, shared, few, dims, steps=6):
    heads, inner, states = dims
    half = first.shape[1]
    width = 2 * half
    tall, low = width // steps, inner // steps
    upper = pl.BlockSpec((tall, half), lambda i: (i, 0))
    lower = pl.BlockSpec((low, half), lambda i: (width // low + i, 0))
    whole = lambda a: pl.BlockSpec(a.shape, lambda i: (0,) * len(a.shape))
    outs = [
        ((width, inner), (tall, inner)),
        ((width, inner), (tall, inner)),
        ((inner, width), (low, width)),
    ]
    fixed = [
        (width, 2 * states), (width, heads), (4, inner), (1, inner), (4, 2 * states), (1, 2 * states),
        (1, heads), (1, heads), (1, heads), (1, inner), (1, width),
    ]
    return pl.pallas_call(
        functools.partial(unpack_kernel, dims),
        grid=(steps,),
        out_shape=[shape(a, F32) for a, _ in outs] + [shape(a, F32) for a in fixed],
        in_specs=[upper] * 2 + [lower] * 2 + [whole(own), whole(shared), whole(few)],
        out_specs=[pl.BlockSpec(b, lambda i: (i, 0)) for _, b in outs]
        + [pl.BlockSpec(a, lambda i: (0, 0)) for a in fixed],
        compiler_params=pltpu.CompilerParams(vmem_limit_bytes=VMEM_LIMIT),
        name="unpack",
    )(first, second, first, second, own, shared, few)


def normalise(u, gain):
    uv = u.astype(F32)
    s = lax.rsqrt(jnp.mean(uv * uv, axis=-1, keepdims=True) + EPSILON)
    return (uv * s * gain).astype(BF)


def on_device(
    inputs, cotangent, norm_gain, w_z, w_x, w_bc, w_dt, conv_x, conv_x_bias, conv_bc, conv_bc_bias,
    dt_bias, a_log, d_skip, gate_gain, w_out,
):
    me = lax.axis_index("section")
    seq_size, head_size = lax.axis_size("seq"), lax.axis_size("head")
    micro, n, d_model = inputs.shape
    batch = micro // 2
    tokens = batch * n
    inner, heads, states = w_z.shape[2], w_dt.shape[2], w_bc.shape[2] // 2
    wide = inner + 2 * states
    full = inner * head_size
    dims = (heads, inner, states)
    pad_heads = lambda a: jnp.pad(a, ((0, 0),) * (a.ndim - 1) + ((0, LANES - heads),))

    taps_x = jnp.concatenate([conv_x[0], conv_x_bias, jnp.zeros((3, inner), F32)], axis=0)
    taps_bc = jnp.concatenate([conv_bc[0], conv_bc_bias, jnp.zeros((3, 2 * states), F32)], axis=0)
    taps = jnp.concatenate([taps_x, taps_bc], axis=1)
    scalars = pad_heads(jnp.concatenate([dt_bias, -jnp.exp(a_log)], axis=0)).reshape(1, -1)
    vectors = jnp.concatenate(
        [
            jnp.repeat(d_skip[0], inner // heads)[None],
            gate_gain,
            jnp.pad(scalars, ((0, 0), (0, inner - 2 * LANES))),
            jnp.zeros((5, inner), F32),
        ],
        axis=0,
    )
    gains = jnp.broadcast_to(norm_gain, (8, d_model))
    w_in0, w_out0, block0, w_in1, w_out1, block1 = both_layers(
        [[w_z[0], w_x[0], w_bc[0], pad_heads(w_dt[0])], [w_out[0]], [taps, vectors, gains]]
    )

    u = lax.dynamic_slice_in_dim(inputs, me * batch, batch, 0).reshape(tokens, d_model)
    cot = lax.dynamic_slice_in_dim(cotangent, me * batch, batch, 0).reshape(tokens, d_model)

    flat = lambda a: a.reshape(tokens, -1)
    stacked = lambda a: a.reshape(batch, n, -1)

    normed0 = normalise(u, block0[0:1, block0.shape[1] - d_model :])
    proj0 = stacked(dot(normed0, w_in0))
    cx0, dt0, cum0, state0, halo0, y0, yn0, stats0 = ssd_fwd(
        proj0, block0, None, dims, seq_size, head_size, full
    )
    h0, normed1, proj1 = head_fwd(flat(yn0), w_out0, u, head_size, [w_in1, block1])
    proj1 = stacked(proj1)
    dyn1 = stacked(dot(cot, w_out1, NT))
    cx1, dt1, cum1, state1, halo1, y1, yn1, stats1 = ssd_fwd(
        proj1, block1, dyn1, dims, seq_size, head_size, full
    )
    h1_rows, body1_out = head_fwd(flat(yn1), w_out1, h0, head_size, [], cot)

    g_in1, gate1, conv1, small1, layer_outputs = ssd_bwd(
        dyn1, y1, proj1, halo1, cx1, dt1, cum1, state1, stats1, block1, [h1_rows, h0],
        dims, seq_size, head_size, full,
    )
    g_in1, body1_out = lax.optimization_barrier((flat(g_in1), body1_out))
    done_out = lax.psum(body1_out, "seq")
    du1, du1_rows, gain1, dyn0, body1 = head_bwd(
        g_in1, w_in1, cot, h0, block1, w_out0, normed1, flat(yn1), head_size
    )
    body1_early, done_out = lax.optimization_barrier((body1[: d_model - 2 * LATE * PIECE], done_out))
    done = lax.psum(body1_early, "seq")
    tail1, few1 = grad_tail(normed1, g_in1, conv1, small1, gate1, gain1, dims, head_size)
    g_in0, gate0, conv0, small0 = ssd_bwd(
        stacked(dyn0), y0, proj0, halo0, cx0, dt0, cum0, state0, stats0, block0, [],
        dims, seq_size, head_size, full,
    )
    g_in0 = flat(g_in0)
    tail0, few0 = grad_tail(normed0, g_in0, conv0, small0, gate0, jnp.zeros_like(gain1), dims, head_size)
    first, second, own, shared, few, input_grads = grad_sum(
        (g_in0, w_in0, du1_rows, u, block0, normed0, flat(yn0), du1),
        body1, (tail0, tail1), (few0, few1), (done, done_out), seq_size, head_size,
    )
    g_z, g_x, g_out, g_bc, g_dt, g_conv, g_conv_bias, g_bc_conv, g_bc_bias, *scalars, g_gate, g_gain = unpack(
        first, second, own, shared, few, dims
    )

    return (
        layer_outputs.reshape(1, micro, n, d_model),
        input_grads.reshape(1, micro, n, d_model),
        g_gain,
        g_z[None],
        g_x[None],
        g_bc[None],
        g_dt[None],
        g_conv[None],
        g_conv_bias,
        g_bc_conv[None],
        g_bc_bias,
        *scalars,
        g_gate,
        g_out[None],
    )


def solution(mesh):
    in_specs = (
        P(None, "seq", None),
        P(None, "seq", None),
        P("section", None),
        P("section", None, "head"),
        P("section", None, "head"),
        P("section", None, None),
        P("section", None, "head"),
        P("section", None, "head"),
        P("section", "head"),
        P("section", None, None),
        P("section", None),
        P("section", "head"),
        P("section", "head"),
        P("section", "head"),
        P("section", "head"),
        P("section", "head", None),
    )
    out_specs = (
        P("section", None, "seq", None),
        P("section", None, "seq", None),
        P("section", None),
        P("section", None, "head"),
        P("section", None, "head"),
        P("section", None, None),
        P("section", None, "head"),
        P("section", None, "head"),
        P("section", "head"),
        P("section", None, None),
        P("section", None),
        P("section", "head"),
        P("section", "head"),
        P("section", "head"),
        P("section", "head"),
        P("section", "head", None),
    )
    return jax.shard_map(
        on_device, mesh=mesh, in_specs=in_specs, out_specs=out_specs, check_vma=False
    )
```
